512 devices in a mesh: gx: 64 (over z, y), gy: 8 (over x, core).
Axes of the slice: x: 4, y: 8, z: 8, core: 2. Of those that a mesh axis runs over, the one named last changes fastest.
Arguments:
- forward_coeff: float32 [192, 65536], P(None, ('gx', 'gy')), may hold values from -6 to 6
- incident: float32 [192, 65536], P(None, ('gx', 'gy')), may hold values from -6 to 6
- cost_grad: float32 [192, 65536], P(None, ('gx', 'gy')), may hold values from -6 to 6
- tmat_real: float32 [4, 96, 96], replicated, may hold values from -0.21875 to 0.21875
- tmat_imag: float32 [4, 96, 96], replicated, may hold values from -0.21875 to 0.21875
- translation_real: float32 [10, 96, 96], replicated, may hold values from -0.125 to 0.125
- translation_imaginary: float32 [10, 96, 96], replicated, may hold values from -0.125 to 0.125
- neighbours: int32 [10, 65536], P(None, ('gx', 'gy')), may hold values from -1 to 65535, as said below
- particle_type: int32 [65536], P(('gx', 'gy')), may hold values from 0 to 3
Outputs:
- adjoint: float32 [192, 65536], P(None, ('gx', 'gy'))
- sensitivity: float32 [4, 192, 192], replicated
The draws below stay inside these ranges and needn't reach their ends.
Inputs may be any that keep to these rules, and one draw needn't show every extreme that they name: `neighbours`: particles sit on a lattice cut into spatial tiles of 4 rows (wide direction) by 32 columns (short direction); tile t holds slots t * 128 to t * 128 + 127, tiles numbered along the short direction fastest, and slot p of a tile sits at row p // 32 and column p % 32 of its tile. An entry of -1 marks an empty slot. Any other entry names a particle whose lattice row and column differ from the particle's own by dr and dc with 0 < dr^2 + dc^2 <= 5; the entries of one particle's list name distinct particles.
All inputs are finite; a program needn't handle non-finite values.
Results may differ from the reference program's by a relative error of at most 0.0001.
Values sent between devices are 32-bit elements; how exact they have to be, the bound alone decides.
No kernel may reach another device: no remote copies, remote signals or barrier semaphores. Data moves between devices by JAX's collectives and lax.ppermute only.
A program may use at most 64 MiB of HBM per device.

```python
import jax
import jax.numpy as jnp
from jax import lax

COEFFICIENT_SIZE = 96
COEFFICIENT_REAL = 192
NEIGHBOUR_SLOTS = 10
TYPES = 4
KRYLOV = 2
TROWS = 4
TCOLS = 32
PDEV = 128
NPART = 65536
N_GX = 64
N_GY = 8


def draw_neighbours(key, part):
    total_count = PDEV * N_GX * N_GY
    particle_ids = jnp.arange(total_count, dtype=jnp.int32)
    tile_index = particle_ids // PDEV
    tile_row = tile_index // N_GY
    tile_col = tile_index % N_GY
    own_slot = particle_ids % PDEV
    site_row = tile_row * TROWS + own_slot // TCOLS
    site_col = tile_col * TCOLS + own_slot % TCOLS
    reach_row = jnp.array([1, -1, 0, 0, 1, 1, -1, -1, 2, -2, 0, 0, 2, 2, -2, -2, 1, 1, -1, -1], dtype=jnp.int32)
    reach_col = jnp.array([0, 0, 1, -1, 1, -1, 1, -1, 0, 0, 2, -2, 1, -1, 1, -1, 2, -2, 2, -2], dtype=jnp.int32)
    random_subkeys = jax.random.split(jax.random.fold_in(key, 17), 2)
    ranking_values = jax.random.randint(random_subkeys[0], (20, total_count), 0, 2 ** 20) * 32 + jnp.arange(20, dtype=jnp.int32)[:, None]
    selected_entries = jnp.argsort(ranking_values, axis=0)[:NEIGHBOUR_SLOTS].astype(jnp.int32)
    new_row = site_row[None, :] + jnp.take(reach_row, selected_entries)
    new_col = site_col[None, :] + jnp.take(reach_col, selected_entries)
    inside = (new_row >= 0) & (new_row < N_GX * TROWS) & (new_col >= 0) & (new_col < N_GY * TCOLS)
    safe_row = jnp.where(inside, new_row, 0)
    safe_col = jnp.where(inside, new_col, 0)
    final_output = (safe_row // TROWS * N_GY + safe_col // TCOLS) * PDEV + safe_row % TROWS * TCOLS + safe_col % TCOLS
    empty_slots = jax.random.randint(random_subkeys[1], (NEIGHBOUR_SLOTS, total_count), 0, 5) == 0
    final_output = jnp.where(inside & jnp.logical_not(empty_slots), final_output, -1).astype(jnp.int32)
    last_list = final_output[:, total_count - 2]
    last_list = jnp.where(last_list == total_count - 1, -1, last_list).at[0].set(total_count - 1)
    final_output = final_output.at[:, total_count - 2].set(last_list)
    final_output = final_output.at[NEIGHBOUR_SLOTS - 1, 0].set(-1)
    return final_output.astype(jnp.int32)


def with_ends(result, own_key, low, top_value):
    shape = result.shape
    place = [jax.random.randint(jax.random.fold_in(own_key, axis), (), 0, shape[axis]) for axis in range(len(shape))]
    result = result.at[tuple(place)].set(low)
    longest = shape.index(max(shape))
    place[longest] = (place[longest] + 1) % shape[longest]
    return result.at[tuple(place)].set(top_value)


def shard_levels(own_key, extent, cuts, smallest, largest):
    gain = 1.0
    for axis_at, shards_of in cuts:
        heights = jax.random.uniform(jax.random.fold_in(jax.random.fold_in(own_key, 6), axis_at), (shards_of,), jnp.float32, smallest / len(cuts), largest / len(cuts))
        gain = gain * jnp.repeat(jnp.exp(heights), extent[axis_at] // shards_of).reshape((-1,) + (1,) * (len(extent) - 1 - axis_at))
    return gain


def noise(rng, dims, scale, bound, pieces=(), held_as=jnp.bfloat16):
    values = scale * jax.random.normal(rng, dims, jnp.float32)
    if pieces:
        values = values * shard_levels(rng, dims, pieces, -0.22, 0.18)
    return jnp.clip(values, -bound, bound).astype(held_as)


def setup_inputs(seed: int = 0) -> dict:
    arg_keys = jax.random.split(jax.random.key(seed), 10)
    forward_coeff = noise(arg_keys[0], (COEFFICIENT_REAL, NPART), 1.0, 6.0, ((1, 512),), jnp.float32)
    incident = noise(arg_keys[1], (COEFFICIENT_REAL, NPART), 1.0, 6.0, ((1, 512),), jnp.float32)
    cost_grad = noise(arg_keys[2], (COEFFICIENT_REAL, NPART), 1.0, 6.0, ((1, 512),), jnp.float32)
    tmat_real = noise(arg_keys[3], (TYPES, COEFFICIENT_SIZE, COEFFICIENT_SIZE), (4 * COEFFICIENT_REAL) ** -0.5, 0.21875, (), jnp.float32)
    tmat_imag = noise(arg_keys[4], (TYPES, COEFFICIENT_SIZE, COEFFICIENT_SIZE), (4 * COEFFICIENT_REAL) ** -0.5, 0.21875, (), jnp.float32)
    translation_real = noise(arg_keys[5], (NEIGHBOUR_SLOTS, COEFFICIENT_SIZE, COEFFICIENT_SIZE), (12 * COEFFICIENT_REAL) ** -0.5, 0.125, (), jnp.float32)
    translation_imaginary = noise(arg_keys[6], (NEIGHBOUR_SLOTS, COEFFICIENT_SIZE, COEFFICIENT_SIZE), (12 * COEFFICIENT_REAL) ** -0.5, 0.125, (), jnp.float32)
    neighbours = draw_neighbours(jax.random.fold_in(arg_keys[9], 71), 0)
    particle_type = with_ends(jax.random.randint(arg_keys[8], (NPART,), 0, TYPES), jax.random.fold_in(arg_keys[8], 1), 0, TYPES - 1).astype(jnp.int32)
    return {"forward_coeff": forward_coeff, "incident": incident, "cost_grad": cost_grad, "tmat_real": tmat_real, "tmat_imag": tmat_imag, "translation_real": translation_real, "translation_imaginary": translation_imaginary, "neighbours": neighbours, "particle_type": particle_type}


HIGH = lax.Precision.HIGHEST

def complex_blocks(real_part, imag_part):
    upper_rows = jnp.concatenate([real_part, -imag_part], axis=2)
    lower_rows = jnp.concatenate([imag_part, real_part], axis=2)
    return jnp.concatenate([upper_rows, lower_rows], axis=1)

def small_solve(normal, right):
    factor = jnp.linalg.cholesky(normal)
    forward_vals = []
    for row_index in range(KRYLOV):
        partial_sum = right[row_index]
        for col_index in range(row_index):
            partial_sum = partial_sum - factor[row_index, col_index] * forward_vals[col_index]
        forward_vals.append(partial_sum / factor[row_index, row_index])
    backward_vals = [None] * KRYLOV
    for row_index in reversed(range(KRYLOV)):
        partial_sum = forward_vals[row_index]
        for col_index in range(row_index + 1, KRYLOV):
            partial_sum = partial_sum - factor[col_index, row_index] * backward_vals[col_index]
        backward_vals[row_index] = partial_sum / factor[row_index, row_index]
    return backward_vals

def reference(forward_coeff, incident, cost_grad, tmat_real, tmat_imag, translation_real, translation_imaginary, neighbours, particle_type):
    tmats = complex_blocks(tmat_real, tmat_imag)
    trans = complex_blocks(translation_real, translation_imaginary)
    tmat_adj = jnp.swapaxes(tmats, 1, 2)
    trans_adj = jnp.swapaxes(trans, 1, 2)
    kinds = jnp.arange(TYPES, dtype=jnp.int32)
    type_mask = (particle_type[None, :] == kinds[:, None]).astype(jnp.float32)
    target = jnp.where(neighbours >= 0, neighbours, NPART).astype(jnp.int32)

    def apply_adjoint(vector):
        scaled = jnp.zeros_like(vector)
        for kind_index in range(TYPES):
            scaled = scaled + type_mask[kind_index] * jnp.dot(tmat_adj[kind_index], vector, precision=HIGH)
        collected = jnp.zeros((COEFFICIENT_REAL, NPART + 1), jnp.float32)
        for neighbour_slot_index in range(NEIGHBOUR_SLOTS):
            collected = collected.at[:, target[neighbour_slot_index]].add(jnp.dot(trans_adj[neighbour_slot_index], scaled, precision=HIGH))
        return vector - collected[:, :NPART]
    padded_coeff = jnp.concatenate([forward_coeff, jnp.zeros((COEFFICIENT_REAL, 1), jnp.float32)], axis=1)
    exciting = incident
    for neighbour_slot_index in range(NEIGHBOUR_SLOTS):
        exciting = exciting + jnp.dot(trans[neighbour_slot_index], padded_coeff[:, target[neighbour_slot_index]], precision=HIGH)
    beta = jnp.sqrt(jnp.sum(cost_grad * cost_grad))
    basis = [cost_grad / beta]
    columns = []
    for column in range(KRYLOV):
        image = apply_adjoint(basis[column])
        projections = jnp.stack([jnp.sum(vec_item * image) for vec_item in basis])
        for row_index in range(column + 1):
            image = image - projections[row_index] * basis[row_index]
        height = jnp.sqrt(jnp.sum(image * image))
        columns.append(jnp.concatenate([projections, height[None], jnp.zeros((KRYLOV - column - 1,), jnp.float32)]))
        basis.append(image / height)
    hessen = jnp.stack(columns, axis=1)
    normal = jnp.dot(hessen.T, hessen, precision=HIGH)
    weights = small_solve(normal, beta * hessen[0])
    adjoint = weights[0] * basis[0]
    for column in range(1, KRYLOV):
        adjoint = adjoint + weights[column] * basis[column]
    sensitivity = jnp.stack([jnp.dot(adjoint * type_mask[kind_index], exciting.T, precision=HIGH) for kind_index in range(TYPES)])
    return (adjoint, sensitivity)
```

```python
import jax
import jax.numpy as jnp
from jax import lax
from jax.experimental import pallas as pl
from jax.experimental.pallas import tpu as pltpu
from jax.sharding import PartitionSpec as P

F32 = jnp.float32
BF16 = jnp.bfloat16
W = 192
HALF = 96
PT = 128
SLOTS = 10
KINDS = 4
META = 16
ROWS = W + META
CHUNK = 296
VMEM = 56 * 1024 * 1024


def params():
    return pltpu.CompilerParams(vmem_limit_bytes=VMEM)


def split(x):
    hi = x.astype(BF16)
    return hi, (x - hi.astype(F32)).astype(BF16)


def dot(a, b):
    return lax.dot_general(a, b, (((1,), (0,)), ((), ())), preferred_element_type=F32)


def dot_nt(a, b):
    return lax.dot_general(a, b, (((1,), (1,)), ((), ())), preferred_element_type=F32)


def lanes(rows):
    return lax.broadcasted_iota(jnp.int32, (rows, PT), 1)


def pack_wide_kernel(fc_ref, b_ref, nb_ref, pt_ref, up_ref, dn_ref):
    meta = jnp.concatenate(
        [
            (nb_ref[...] + 1).astype(F32),
            pt_ref[...].astype(F32),
            jnp.zeros((META - SLOTS - 1, PT), F32),
        ],
        axis=0,
    )
    top, low = fc_ref[0:HALF, :], fc_ref[HALF:W, :]
    first = lanes(HALF) < 64
    for ref in (up_ref, dn_ref):
        ref[0:W, :] = b_ref[...]
        ref[W:ROWS, :] = meta
    up_ref[ROWS : ROWS + HALF, :] = jnp.where(first, pltpu.roll(top, 64, 1), low)
    dn_ref[ROWS : ROWS + HALF, :] = jnp.where(first, top, pltpu.roll(low, 64, 1))


def unpack_fc(up, dn):
    first = lanes(HALF) < 64
    return jnp.concatenate(
        [
            jnp.where(first, dn, pltpu.roll(up, 64, 1)),
            jnp.where(first, pltpu.roll(dn, 64, 1), up),
        ],
        axis=0,
    )


def pack_short_kernel(fc_ref, own_ref, up_ref, dn_ref, lo_ref, hi_ref):
    first = lanes(META) < 64
    fc_ud = unpack_fc(up_ref[ROWS : ROWS + HALF, :], dn_ref[ROWS : ROWS + HALF, :])

    def part(rows, tiles):
        col = lanes(rows.stop - rows.start) % 32
        up, own, dn, edge, edge_ud = tiles

        def moved(x, shift):
            return pltpu.roll(x, shift, 1) if shift else x

        low = moved(up, 0)
        low = jnp.where(col < 4, low, moved(own, 4))
        low = jnp.where(col < 8, low, moved(dn, 8))
        low = jnp.where(col < 12, low, moved(edge, 12))
        lo_ref[rows, :] = jnp.where(col < 14, low, moved(edge_ud, 14))
        high = moved(edge, 114)
        high = jnp.where(col < 18, high, moved(edge_ud, 116))
        high = jnp.where(col < 20, high, moved(up, 120))
        high = jnp.where(col < 24, high, moved(own, 124))
        hi_ref[rows, :] = jnp.where(col < 28, high, dn)

    part(slice(0, W), (up_ref[0:W, :], own_ref[0:W, :], dn_ref[0:W, :], fc_ref[...], fc_ud))
    m = slice(W, ROWS)
    meta_ud = jnp.where(first, dn_ref[m, :], up_ref[m, :])
    part(m, (up_ref[m, :], own_ref[m, :], dn_ref[m, :], own_ref[m, :], meta_ud))


def target_ids(base, row_stride):
    spot = lax.broadcasted_iota(jnp.int32, (3 * PT, PT), 0)
    lane = spot % PT
    row, col = lane // 32, lane % 32
    shift = jnp.where(row < 2, row_stride, -row_stride)
    own = base + lane
    beside = base + row * 32
    lr = jnp.where(
        col < 14,
        beside + PT + col - 12,
        jnp.where(
            col < 16,
            beside + PT + shift + col - 14,
            jnp.where(col < 18, beside - PT + col + 14, beside - PT + shift + col + 12),
        ),
    )
    lr = jnp.where((col >= 12) & (col < 20), lr, -10)
    ids = jnp.where(spot < PT, own, jnp.where(spot < 2 * PT, own + shift, lr))
    return jnp.where(ids >= 0, ids + 1, -10).astype(F32)


def main_kernel(
    base_ref,
    own_ref,
    up_ref,
    dn_ref,
    lf_ref,
    rt_ref,
    fc_ref,
    inc_ref,
    tw_ref,
    lw_ref,
    fw_ref,
    chunk_ref,
    u1_ref,
    ghi_ref,
    glo_ref,
):
    m = slice(W, ROWS)
    ids = target_ids(base_ref[0], base_ref[1])
    own_ids = ids[0:PT, :]
    first = lanes(META) < 64
    col = lanes(META) % 32
    b = own_ref[0:W, :]
    m_own, m_up, m_dn = own_ref[m, :], up_ref[m, :], dn_ref[m, :]
    m_ud = jnp.where(first, m_dn, m_up)
    wide = lanes(W) % 32 >= 16
    m_lr = jnp.where(col >= 16, lf_ref[m, :], rt_ref[m, :])
    x_lr = jnp.where(wide, lf_ref[0:W, :], rt_ref[0:W, :])
    b_zone = (col < 12) | (col >= 20)
    row_id = lax.broadcasted_iota(jnp.int32, (META, PT), 0)
    m_b = jnp.where(b_zone | (row_id >= SLOTS), m_lr, 0.0)
    m_f = jnp.where(b_zone & (row_id < SLOTS), 0.0, m_lr)

    def product(w_ref, hi, lo):
        rows = dot(w_ref[...], hi)
        return rows[0:W] + rows[W : 2 * W] + dot(w_ref[0:W, :], lo)

    def scaled_by_type(blocks, metas):
        his, los = [], []
        for v, meta in zip(blocks, metas):
            hi, lo = split(v)
            kind = meta[SLOTS : SLOTS + 1, :]
            his.append([jnp.where(kind == float(k), hi, jnp.zeros_like(hi)) for k in range(KINDS)])
            los.append([jnp.where(kind == float(k), lo, jnp.zeros_like(lo)) for k in range(KINDS)])
        hi = jnp.concatenate(
            [jnp.concatenate([h[k] for h in his], axis=1) for k in range(KINDS)], axis=0
        )
        lo = jnp.concatenate(
            [jnp.concatenate([x[k] for x in los], axis=1) for k in range(KINDS)], axis=0
        )
        s_hi, s_lo = split(product(tw_ref, hi, lo))
        return jnp.concatenate([s_hi, s_lo], axis=0)

    def one_hot(at, meta, s):
        return jnp.where(at == meta[s : s + 1, :], 1.0, 0.0).astype(BF16)

    metas = (m_own, m_up, m_dn, m_b)
    stack = scaled_by_type((b, up_ref[0:W, :], dn_ref[0:W, :], x_lr), metas)
    for s in range(SLOTS):
        pick = jnp.concatenate([one_hot(ids, meta, s) for meta in metas], axis=1)
        g = dot_nt(stack, pick)
        hi, lo = split(g[0:W] + g[W : 2 * W])
        ghi_ref[s * W : (s + 1) * W, :] = hi
        glo_ref[s * W : (s + 1) * W, :] = lo
    u1_all = product(lw_ref, ghi_ref[...], glo_ref[...])
    u1 = u1_all[:, 0:PT]
    u1_ref[...] = u1

    metas = (m_own, m_ud, m_f)
    stack = scaled_by_type([u1_all[:, i * PT : (i + 1) * PT] for i in range(3)], metas)
    for s in range(0, SLOTS, 2):
        pick = jnp.concatenate(
            [
                jnp.concatenate([one_hot(own_ids, meta, t) for meta in metas], axis=1)
                for t in (s, s + 1)
            ],
            axis=0,
        )
        g = dot_nt(stack, pick)
        hi, lo = split(g[0:W] + g[W : 2 * W])
        for t in (0, 1):
            rows = slice((s + t) * W, (s + t + 1) * W)
            ghi_ref[rows, 0:PT] = hi[:, t * PT : (t + 1) * PT]
            glo_ref[rows, 0:PT] = lo[:, t * PT : (t + 1) * PT]
    u2 = product(lw_ref, ghi_ref[:, 0:PT], glo_ref[:, 0:PT])

    fc_ud = unpack_fc(up_ref[ROWS : ROWS + HALF, :], dn_ref[ROWS : ROWS + HALF, :])
    f_hi, f_lo = split(jnp.concatenate([fc_ref[...], fc_ud, x_lr], axis=1))
    stack = jnp.concatenate([f_hi, f_lo], axis=0)
    for s in range(0, SLOTS, 2):
        pick = jnp.concatenate([one_hot(ids, m_own, s), one_hot(ids, m_own, s + 1)], axis=1)
        g = dot(stack, pick).astype(BF16)
        for t in (0, 1):
            rows = slice((s + t) * W, (s + t + 1) * W)
            ghi_ref[rows, PT : 2 * PT] = g[0:W, t * PT : (t + 1) * PT]
            glo_ref[rows, PT : 2 * PT] = g[W : 2 * W, t * PT : (t + 1) * PT]
    exc = inc_ref[...] + product(fw_ref, ghi_ref[:, PT : 2 * PT], glo_ref[:, PT : 2 * PT])

    e_hi, e_lo = split(jnp.concatenate([exc, jnp.zeros((64, PT), F32)], axis=0))
    v_hi, v_lo = split(jnp.concatenate([b, u1], axis=0))
    kind = m_own[SLOTS : SLOTS + 1, :]
    for k in range(KINDS):
        here = kind == float(k)
        k_hi = jnp.where(here, v_hi, jnp.zeros_like(v_hi))
        k_lo = jnp.where(here, v_lo, jnp.zeros_like(v_lo))
        out = dot_nt(k_hi, e_hi) + dot_nt(k_lo, e_hi) + dot_nt(k_hi, e_lo)
        for which in range(2):
            for h in range(2):
                block = out[which * W + h * HALF : which * W + (h + 1) * HALF, :]
                at = which * 144
                chunk_ref[2 * k + h, at : at + 96, :] = block[:, 0:PT]
                chunk_ref[2 * k + h, at + 96 : at + 144, :] = block[0:48, PT:] + pltpu.roll(
                    block[48:96, PT:], 64, 1
                )

    lane = lanes(8)
    gram = jnp.zeros((8, PT), F32)
    for i, (p, q) in enumerate(((b, b), (b, u1), (u1, u1), (b, u2), (u1, u2), (u2, u2))):
        gram = jnp.where(lane == i, jnp.sum(p * q), gram)
    for g in range(8):
        chunk_ref[g, 288:296, :] = gram


def spread_kernel(in_ref, out_ref):
    total = in_ref[0]
    for i in range(1, 8):
        total = total + in_ref[i]
    out_ref[...] = jnp.zeros_like(out_ref)
    for which in range(2):
        for j in range(3):
            at = which * 144 + j * 48
            out_ref[pl.ds(3 * which + j, 48, 8), :] = total[at : at + 48, :]
    out_ref[pl.ds(6, 64, 8), :] = jnp.broadcast_to(total[288:289, :], (64, PT))


def combine_kernel(in_ref, b_ref, u1_ref, out_ref, adj_ref):
    total = jnp.sum(in_ref[...].reshape(64, 8, PT), axis=0)
    lane = lanes(1)

    def entry(i):
        return jnp.sum(jnp.where(lane == i, total[6:7, :], 0.0), axis=1, keepdims=True)

    g00, g01, g11, g02, g12, g22 = [entry(i) for i in range(6)]
    alpha = g01 / g00
    beta = jnp.sqrt(g00)
    p2 = g11 - alpha * g01
    pn = jnp.sqrt(p2)
    h00 = 1.0 - alpha
    h10 = pn / beta
    h01 = (g02 - alpha * g01) / (beta * pn)
    qv1 = (g12 - alpha * g11 - alpha * g02 + alpha * alpha * g01) / p2
    h11 = 1.0 - qv1
    n00 = h00 * h00 + h10 * h10
    n01 = h00 * h01 + h10 * h11
    n11 = 1.0 - 2.0 * qv1 + (g22 - 2.0 * alpha * g12 + alpha * alpha * g11) / p2
    r0 = beta * h00
    r1 = beta * h01
    f00 = jnp.sqrt(n00)
    f10 = n01 / f00
    f11 = jnp.sqrt(n11 - f10 * f10)
    y0 = r0 / f00
    y1 = (r1 - f10 * y0) / f11
    w1 = y1 / f11
    w0 = (y0 - f10 * w1) / f00
    c1 = -w1 / pn
    c0 = w0 / beta - c1 * alpha
    mixed = jnp.concatenate(
        [c0 * total[0:3, :] + c1 * total[3:6, :], jnp.zeros((5, PT), F32)], axis=0
    )
    for i in range(64):
        out_ref[8 * i : 8 * i + 8, :] = mixed
    adj_ref[...] = c0 * b_ref[...] + c1 * u1_ref[...]


def expand_kernel(in_ref, out_ref):
    a0 = in_ref[pl.ds(0, 48, 8), :]
    a1 = in_ref[pl.ds(1, 48, 8), :]
    edge = in_ref[pl.ds(2, 48, 8), :]
    turned = pltpu.roll(edge, 64, 1)
    for i in range(8):
        out_ref[i, 0:48, 0:PT] = a0
        out_ref[i, 48:96, 0:PT] = a1
        out_ref[i, 0:48, PT:W] = edge[:, 0:64]
        out_ref[i, 48:96, PT:W] = turned[:, 0:64]


def call(kernel, shapes, *args, smem=0, **kw):
    return pl.pallas_call(
        kernel,
        out_shape=[jax.ShapeDtypeStruct(s, F32) for s in shapes],
        in_specs=[pl.BlockSpec(memory_space=pltpu.SMEM)] * smem
        + [pl.BlockSpec(memory_space=pltpu.VMEM)] * (len(args) - smem),
        compiler_params=params(),
        **kw,
    )(*args)


def complex_blocks(real_part, imag_part):
    upper_rows = jnp.concatenate([real_part, -imag_part], axis=2)
    lower_rows = jnp.concatenate([imag_part, real_part], axis=2)
    return jnp.concatenate([upper_rows, lower_rows], axis=1)


def weight_pair(w):
    n = w.shape[0]
    side = jnp.swapaxes(w, 0, 1).reshape(W, n * W)
    hi = lax.reduce_precision(side, 8, 7)
    return jnp.concatenate([hi, side - hi], axis=0).astype(BF16)


def shifted(block, axis, step):
    n = lax.axis_size(axis)
    return lax.ppermute(block, axis, [(i, i + step) for i in range(n) if 0 <= i + step < n])


def body(
    forward_coeff,
    incident,
    cost_grad,
    tmat_real,
    tmat_imag,
    translation_real,
    translation_imaginary,
    neighbours,
    particle_type,
):
    n_short = lax.axis_size("gy")
    tile = lax.axis_index("gx") * n_short + lax.axis_index("gy")
    base = jnp.stack([tile * PT, jnp.int32(n_short * PT)]).astype(jnp.int32)

    to_up, to_dn = call(
        pack_wide_kernel,
        [(ROWS + HALF, PT)] * 2,
        forward_coeff,
        cost_grad,
        neighbours,
        particle_type.reshape(1, PT),
    )
    up = shifted(to_up, "gx", 1)
    dn = shifted(to_dn, "gx", -1)
    to_lo, to_hi = call(
        pack_short_kernel, [(ROWS, PT)] * 2, forward_coeff, to_up, up, dn
    )
    lf = shifted(to_hi, "gy", 1)
    rt = shifted(to_lo, "gy", -1)

    tmats = complex_blocks(tmat_real, tmat_imag)
    trans = complex_blocks(translation_real, translation_imaginary)
    tw = weight_pair(jnp.swapaxes(tmats, 1, 2))
    lw = weight_pair(jnp.swapaxes(trans, 1, 2))
    fw = weight_pair(trans)

    chunks, u1 = call(
        main_kernel,
        [(8, CHUNK, PT), (W, PT)],
        base,
        to_up,
        up,
        dn,
        lf,
        rt,
        forward_coeff,
        incident,
        tw,
        lw,
        fw,
        smem=1,
        scratch_shapes=[pltpu.VMEM((SLOTS * W, 3 * PT), BF16)] * 2,
    )
    got = lax.all_to_all(chunks, "gy", 0, 0)
    (pieces,) = call(spread_kernel, [(512, PT)], got)
    got = lax.all_to_all(pieces.reshape(64, 8, PT), "gx", 0, 0)
    mixed, adjoint = call(
        combine_kernel, [(512, PT), (W, PT)], got.reshape(512, PT), cost_grad, u1
    )
    got = lax.all_to_all(mixed.reshape(64, 8, PT), "gx", 0, 0)
    (copies,) = call(expand_kernel, [(8, HALF, W)], got.reshape(512, PT))
    sensitivity = lax.all_to_all(copies, "gy", 0, 0).reshape(KINDS, W, W)
    return (adjoint, sensitivity)


def solution(mesh):
    placed = (
        P(None, ("gx", "gy")),
        P(None, ("gx", "gy")),
        P(None, ("gx", "gy")),
        P(),
        P(),
        P(),
        P(),
        P(None, ("gx", "gy")),
        P(("gx", "gy")),
    )
    return jax.shard_map(
        body, mesh=mesh, in_specs=placed, out_specs=(P(None, ("gx", "gy")), P()), check_vma=False
    )
```

```python
import jax
import jax.numpy as jnp
from jax import lax
from jax.experimental import pallas as pl
from jax.experimental.pallas import tpu as pltpu
from jax.sharding import PartitionSpec as P

F32 = jnp.float32
BF16 = jnp.bfloat16
W = 192
HALF = 96
PT = 128
SLOTS = 10
KINDS = 4
META = 16
ROWS = W + META
CHUNK = 296
PART = 1024
MIB = 1024 * 1024


def split(x):
    hi = x.astype(BF16)
    return hi, (x - hi.astype(F32)).astype(BF16)


def dot(a, b):
    return lax.dot_general(a, b, (((1,), (0,)), ((), ())), preferred_element_type=F32)


def dot_nt(a, b):
    return lax.dot_general(a, b, (((1,), (1,)), ((), ())), preferred_element_type=F32)


def lanes(rows):
    return lax.broadcasted_iota(jnp.int32, (rows, PT), 1)


def pack_wide_kernel(fc_ref, b_ref, nb_ref, pt_ref, up_ref, dn_ref):
    meta = jnp.concatenate(
        [
            (nb_ref[...] + 1).astype(F32),
            pt_ref[...].astype(F32),
            jnp.zeros((META - SLOTS - 1, PT), F32),
        ],
        axis=0,
    )
    top, low = fc_ref[0:HALF, :], fc_ref[HALF:W, :]
    first = lanes(HALF) < 64
    for ref in (up_ref, dn_ref):
        ref[0:W, :] = b_ref[...]
        ref[W:ROWS, :] = meta
    up_ref[ROWS : ROWS + HALF, :] = jnp.where(first, pltpu.roll(top, 64, 1), low)
    dn_ref[ROWS : ROWS + HALF, :] = jnp.where(first, top, pltpu.roll(low, 64, 1))


def unpack_fc(up, dn):
    first = lanes(HALF) < 64
    return jnp.concatenate(
        [
            jnp.where(first, dn, pltpu.roll(up, 64, 1)),
            jnp.where(first, pltpu.roll(dn, 64, 1), up),
        ],
        axis=0,
    )


def pack_short_kernel(fc_ref, own_ref, up_ref, dn_ref, lo_ref, hi_ref):
    first = lanes(META) < 64
    fc_ud = unpack_fc(up_ref[ROWS : ROWS + HALF, :], dn_ref[ROWS : ROWS + HALF, :])

    def part(rows, tiles):
        col = lanes(rows.stop - rows.start) % 32
        up, own, dn, edge, edge_ud = tiles

        def moved(x, shift):
            return pltpu.roll(x, shift, 1) if shift else x

        low = moved(up, 0)
        low = jnp.where(col < 4, low, moved(own, 4))
        low = jnp.where(col < 8, low, moved(dn, 8))
        low = jnp.where(col < 12, low, moved(edge, 12))
        lo_ref[rows, :] = jnp.where(col < 14, low, moved(edge_ud, 14))
        high = moved(edge, 114)
        high = jnp.where(col < 18, high, moved(edge_ud, 116))
        high = jnp.where(col < 20, high, moved(up, 120))
        high = jnp.where(col < 24, high, moved(own, 124))
        hi_ref[rows, :] = jnp.where(col < 28, high, dn)

    part(slice(0, W), (up_ref[0:W, :], own_ref[0:W, :], dn_ref[0:W, :], fc_ref[...], fc_ud))
    m = slice(W, ROWS)
    meta_ud = jnp.where(first, dn_ref[m, :], up_ref[m, :])
    part(m, (up_ref[m, :], own_ref[m, :], dn_ref[m, :], own_ref[m, :], meta_ud))


def weight_kernel(tr_ref, ti_ref, lr_ref, li_ref, tw_ref, lw_ref, fw_ref):
    def turned(ref):
        n = ref.shape[0]
        fill = -n * HALF % PT
        side = jnp.concatenate([ref[...].reshape(n * HALF, HALF), jnp.zeros((n * HALF, 32), F32)], axis=1)
        if fill:
            side = jnp.concatenate([side, jnp.zeros((fill, PT), F32)], axis=0)
        return split(jnp.transpose(side)[0:HALF, :])

    def beside(ref):
        n = ref.shape[0]
        return split(
            jnp.concatenate([ref[s] for s in range(n)] + [jnp.zeros((HALF, -n * HALF % PT), F32)], axis=1)
        )

    def store(ref, real, imag, sign):
        width = real[0].shape[1]
        for at, re, im in zip((0, W), real, imag):
            ref[at : at + HALF, 0:width] = re
            ref[at : at + HALF, width:] = im if sign > 0 else -im
            ref[at + HALF : at + W, 0:width] = -im if sign > 0 else im
            ref[at + HALF : at + W, width:] = re

    store(tw_ref, turned(tr_ref), turned(ti_ref), 1)
    store(lw_ref, turned(lr_ref), turned(li_ref), 1)
    store(fw_ref, beside(lr_ref), beside(li_ref), -1)


def target_ids(base, row_stride):
    spot = lax.broadcasted_iota(jnp.int32, (3 * PT, PT), 0)
    lane = spot % PT
    row, col = lane // 32, lane % 32
    shift = jnp.where(row < 2, row_stride, -row_stride)
    own = base + lane
    beside = base + row * 32
    lr = jnp.where(
        col < 14,
        beside + PT + col - 12,
        jnp.where(
            col < 16,
            beside + PT + shift + col - 14,
            jnp.where(col < 18, beside - PT + col + 14, beside - PT + shift + col + 12),
        ),
    )
    lr = jnp.where((col >= 12) & (col < 20), lr, -10)
    ids = jnp.where(spot < PT, own, jnp.where(spot < 2 * PT, own + shift, lr))
    return jnp.where(ids >= 0, ids + 1, -10).astype(F32)


def main_kernel(
    base_ref,
    own_ref,
    up_ref,
    dn_ref,
    lf_ref,
    rt_ref,
    fc_ref,
    inc_ref,
    tw_ref,
    lw_ref,
    fw_ref,
    chunk_ref,
    u1_ref,
    ghi_ref,
    glo_ref,
):
    m = slice(W, ROWS)
    ids = target_ids(base_ref[0], base_ref[1])
    own_ids = ids[0:PT, :]
    first = lanes(META) < 64
    col = lanes(META) % 32
    b = own_ref[0:W, :]
    m_own, m_up, m_dn = own_ref[m, :], up_ref[m, :], dn_ref[m, :]
    m_ud = jnp.where(first, m_dn, m_up)
    wide = lanes(W) % 32 >= 16
    m_lr = jnp.where(col >= 16, lf_ref[m, :], rt_ref[m, :])
    x_lr = jnp.where(wide, lf_ref[0:W, :], rt_ref[0:W, :])
    b_zone = (col < 12) | (col >= 20)
    row_id = lax.broadcasted_iota(jnp.int32, (META, PT), 0)
    m_b = jnp.where(b_zone | (row_id >= SLOTS), m_lr, 0.0)
    m_f = jnp.where(b_zone & (row_id < SLOTS), 0.0, m_lr)

    def product(w_ref, hi, lo):
        rows = dot(w_ref[...], hi)
        return rows[0:W] + rows[W : 2 * W] + dot(w_ref[0:W, :], lo)

    def scaled_by_type(blocks, metas):
        his, los = [], []
        for v, meta in zip(blocks, metas):
            hi, lo = split(v)
            kind = meta[SLOTS : SLOTS + 1, :]
            his.append([jnp.where(kind == float(k), hi, jnp.zeros_like(hi)) for k in range(KINDS)])
            los.append([jnp.where(kind == float(k), lo, jnp.zeros_like(lo)) for k in range(KINDS)])
        def by_part(pieces):
            whole = [jnp.concatenate([p[k] for p in pieces], axis=1) for k in range(KINDS)]
            return jnp.concatenate([w[0:HALF] for w in whole] + [w[HALF:W] for w in whole], axis=0)

        hi, lo = by_part(his), by_part(los)
        s_hi, s_lo = split(product(tw_ref, hi, lo))
        return jnp.concatenate([s_hi, s_lo], axis=0)

    def one_hot(at, meta, s):
        return jnp.where(at == meta[s : s + 1, :], 1.0, 0.0).astype(BF16)

    for ref in (ghi_ref, glo_ref):
        for at in (SLOTS * HALF, PART + SLOTS * HALF):
            ref[at : at + PART - SLOTS * HALF, :] = jnp.zeros((PART - SLOTS * HALF, 3 * PT), BF16)

    metas = (m_own, m_up, m_dn, m_b)
    stack = scaled_by_type((b, up_ref[0:W, :], dn_ref[0:W, :], x_lr), metas)
    for s in range(SLOTS):
        pick = jnp.concatenate([one_hot(ids, meta, s) for meta in metas], axis=1)
        g = dot_nt(stack, pick)
        hi, lo = split(g[0:W] + g[W : 2 * W])
        for ref, part in ((ghi_ref, hi), (glo_ref, lo)):
            ref[s * HALF : (s + 1) * HALF, :] = part[0:HALF]
            ref[PART + s * HALF : PART + (s + 1) * HALF, :] = part[HALF:W]
    u1_all = product(lw_ref, ghi_ref[...], glo_ref[...])
    u1 = u1_all[:, 0:PT]
    u1_ref[...] = u1

    metas = (m_own, m_ud, m_f)
    stack = scaled_by_type([u1_all[:, i * PT : (i + 1) * PT] for i in range(3)], metas)
    for s in range(0, SLOTS, 2):
        pick = jnp.concatenate(
            [
                jnp.concatenate([one_hot(own_ids, meta, t) for meta in metas], axis=1)
                for t in (s, s + 1)
            ],
            axis=0,
        )
        g = dot_nt(stack, pick)
        hi, lo = split(g[0:W] + g[W : 2 * W])
        for t in (0, 1):
            at = (s + t) * HALF
            for ref, part in ((ghi_ref, hi), (glo_ref, lo)):
                ref[at : at + HALF, 0:PT] = part[0:HALF, t * PT : (t + 1) * PT]
                ref[PART + at : PART + at + HALF, 0:PT] = part[HALF:W, t * PT : (t + 1) * PT]
    u2 = product(lw_ref, ghi_ref[:, 0:PT], glo_ref[:, 0:PT])

    fc_ud = unpack_fc(up_ref[ROWS : ROWS + HALF, :], dn_ref[ROWS : ROWS + HALF, :])
    f_hi, f_lo = split(jnp.concatenate([fc_ref[...], fc_ud, x_lr], axis=1))
    stack = jnp.concatenate([f_hi, f_lo], axis=0)
    for s in range(0, SLOTS, 2):
        pick = jnp.concatenate([one_hot(ids, m_own, s), one_hot(ids, m_own, s + 1)], axis=1)
        g = dot(stack, pick).astype(BF16)
        for t in (0, 1):
            at = (s + t) * HALF
            for ref, part in ((ghi_ref, g[0:W]), (glo_ref, g[W : 2 * W])):
                ref[at : at + HALF, PT : 2 * PT] = part[0:HALF, t * PT : (t + 1) * PT]
                ref[PART + at : PART + at + HALF, PT : 2 * PT] = part[
                    HALF:W, t * PT : (t + 1) * PT
                ]
    exc = inc_ref[...] + product(fw_ref, ghi_ref[:, PT : 2 * PT], glo_ref[:, PT : 2 * PT])

    e_hi, e_lo = split(jnp.concatenate([exc, jnp.zeros((64, PT), F32)], axis=0))
    v_hi, v_lo = split(jnp.concatenate([b, u1], axis=0))
    kind = m_own[SLOTS : SLOTS + 1, :]
    for k in range(KINDS):
        here = kind == float(k)
        k_hi = jnp.where(here, v_hi, jnp.zeros_like(v_hi))
        k_lo = jnp.where(here, v_lo, jnp.zeros_like(v_lo))
        out = dot_nt(k_hi, e_hi) + dot_nt(k_lo, e_hi) + dot_nt(k_hi, e_lo)
        for which in range(2):
            for h in range(2):
                block = out[which * W + h * HALF : which * W + (h + 1) * HALF, :]
                at = which * 144
                chunk_ref[2 * k + h, at : at + 96, :] = block[:, 0:PT]
                chunk_ref[2 * k + h, at + 96 : at + 144, :] = block[0:48, PT:] + pltpu.roll(
                    block[48:96, PT:], 64, 1
                )

    lane = lanes(8)
    gram = jnp.zeros((8, PT), F32)
    for i, (p, q) in enumerate(((b, b), (b, u1), (u1, u1), (b, u2), (u1, u2), (u2, u2))):
        gram = jnp.where(lane == i, jnp.sum(p * q), gram)
    for g in range(8):
        chunk_ref[g, 288:296, :] = gram


def spread_kernel(in_ref, out_ref):
    total = in_ref[0]
    for i in range(1, 8):
        total = total + in_ref[i]
    out_ref[...] = jnp.zeros_like(out_ref)
    for which in range(2):
        for j in range(3):
            at = which * 144 + j * 48
            out_ref[pl.ds(3 * which + j, 48, 8), :] = total[at : at + 48, :]
    out_ref[pl.ds(6, 64, 8), :] = jnp.broadcast_to(total[288:289, :], (64, PT))


def combine_kernel(in_ref, b_ref, u1_ref, out_ref, adj_ref):
    total = jnp.sum(in_ref[...].reshape(64, 8, PT), axis=0)
    lane = lanes(1)

    def entry(i):
        return jnp.sum(jnp.where(lane == i, total[6:7, :], 0.0), axis=1, keepdims=True)

    g00, g01, g11, g02, g12, g22 = [entry(i) for i in range(6)]
    alpha = g01 / g00
    beta = jnp.sqrt(g00)
    p2 = g11 - alpha * g01
    pn = jnp.sqrt(p2)
    h00 = 1.0 - alpha
    h10 = pn / beta
    h01 = (g02 - alpha * g01) / (beta * pn)
    qv1 = (g12 - alpha * g11 - alpha * g02 + alpha * alpha * g01) / p2
    h11 = 1.0 - qv1
    n00 = h00 * h00 + h10 * h10
    n01 = h00 * h01 + h10 * h11
    n11 = 1.0 - 2.0 * qv1 + (g22 - 2.0 * alpha * g12 + alpha * alpha * g11) / p2
    r0 = beta * h00
    r1 = beta * h01
    f00 = jnp.sqrt(n00)
    f10 = n01 / f00
    f11 = jnp.sqrt(n11 - f10 * f10)
    y0 = r0 / f00
    y1 = (r1 - f10 * y0) / f11
    w1 = y1 / f11
    w0 = (y0 - f10 * w1) / f00
    c1 = -w1 / pn
    c0 = w0 / beta - c1 * alpha
    mixed = c0 * total[0:3, :] + c1 * total[3:6, :]
    mixed = jnp.concatenate([mixed, jnp.zeros((1, PT), F32)] * 2, axis=0)
    for i in range(32):
        out_ref[8 * i : 8 * i + 8, :] = mixed
    adj_ref[...] = c0 * b_ref[...] + c1 * u1_ref[...]


def copies_kernel(in_ref, out_ref):
    for j in range(3):
        rows = in_ref[pl.ds(j, 48, 4), :]
        for i in range(8):
            out_ref[i, 48 * j : 48 * (j + 1), :] = rows


def expand_kernel(in_ref, out_ref):
    for k in range(KINDS):
        for h in range(2):
            block = in_ref[2 * k + h]
            at = h * HALF
            edge = block[96:144, :]
            out_ref[k, at : at + HALF, 0:PT] = block[0:HALF, :]
            out_ref[k, at : at + 48, PT:W] = edge[:, 0:64]
            out_ref[k, at + 48 : at + HALF, PT:W] = pltpu.roll(edge, 64, 1)[:, 0:64]


def call(kernel, shapes, *args, smem=0, mib=6, dtype=F32, **kw):
    return pl.pallas_call(
        kernel,
        out_shape=[jax.ShapeDtypeStruct(s, dtype) for s in shapes],
        in_specs=[pl.BlockSpec(memory_space=pltpu.SMEM)] * smem
        + [pl.BlockSpec(memory_space=pltpu.VMEM)] * (len(args) - smem),
        compiler_params=pltpu.CompilerParams(vmem_limit_bytes=mib * MIB),
        **kw,
    )(*args)


def shifted(block, axis, step):
    n = lax.axis_size(axis)
    return lax.ppermute(block, axis, [(i, i + step) for i in range(n) if 0 <= i + step < n])


def body(
    forward_coeff,
    incident,
    cost_grad,
    tmat_real,
    tmat_imag,
    translation_real,
    translation_imaginary,
    neighbours,
    particle_type,
):
    n_short = lax.axis_size("gy")
    tile = lax.axis_index("gx") * n_short + lax.axis_index("gy")
    base = jnp.stack([tile * PT, jnp.int32(n_short * PT)]).astype(jnp.int32)

    to_up, to_dn = call(
        pack_wide_kernel,
        [(ROWS + HALF, PT)] * 2,
        forward_coeff,
        cost_grad,
        neighbours,
        particle_type.reshape(1, PT),
    )
    up = shifted(to_up, "gx", 1)
    dn = shifted(to_dn, "gx", -1)
    to_lo, to_hi = call(
        pack_short_kernel, [(ROWS, PT)] * 2, forward_coeff, to_up, up, dn
    )
    lf = shifted(to_hi, "gy", 1)
    rt = shifted(to_lo, "gy", -1)

    tw, lw, fw = call(
        weight_kernel,
        [(2 * W, KINDS * W), (2 * W, 2 * PART), (2 * W, 2 * PART)],
        tmat_real,
        tmat_imag,
        translation_real,
        translation_imaginary,
        mib=16,
        dtype=BF16,
    )

    chunks, u1 = call(
        main_kernel,
        [(8, CHUNK, PT), (W, PT)],
        base,
        to_up,
        up,
        dn,
        lf,
        rt,
        forward_coeff,
        incident,
        tw,
        lw,
        fw,
        smem=1,
        mib=24,
        scratch_shapes=[pltpu.VMEM((2 * PART, 3 * PT), BF16)] * 2,
    )
    got = lax.all_to_all(chunks, "gy", 0, 0)
    (pieces,) = call(spread_kernel, [(512, PT)], got)
    got = lax.all_to_all(pieces.reshape(64, 8, PT), "gx", 0, 0)
    mixed, adjoint = call(
        combine_kernel, [(256, PT), (W, PT)], got.reshape(512, PT), cost_grad, u1
    )
    got = lax.all_to_all(mixed.reshape(64, 4, PT), "gx", 0, 0)
    (copies,) = call(copies_kernel, [(8, 144, PT)], got.reshape(256, PT))
    got = lax.all_to_all(copies, "gy", 0, 0)
    (sensitivity,) = call(expand_kernel, [(KINDS, W, W)], got)
    return (adjoint, sensitivity)


def solution(mesh):
    placed = (
        P(None, ("gx", "gy")),
        P(None, ("gx", "gy")),
        P(None, ("gx", "gy")),
        P(),
        P(),
        P(),
        P(),
        P(None, ("gx", "gy")),
        P(("gx", "gy")),
    )
    return jax.shard_map(
        body, mesh=mesh, in_specs=placed, out_specs=(P(None, ("gx", "gy")), P()), check_vma=False
    )
```

```python
import jax
import jax.numpy as jnp
from jax import lax
from jax.experimental import pallas as pl
from jax.experimental.pallas import tpu as pltpu
from jax.sharding import PartitionSpec as P

F32 = jnp.float32
BF16 = jnp.bfloat16
W = 192
HALF = 96
PT = 128
SLOTS = 10
KINDS = 4
META = 16
ROWS = W + META
CHUNK = 296
PART = 1024
MIB = 1024 * 1024


def split(x):
    hi = x.astype(BF16)
    return hi, (x - hi.astype(F32)).astype(BF16)


def dot(a, b):
    return lax.dot_general(a, b, (((1,), (0,)), ((), ())), preferred_element_type=F32)


def dot_nt(a, b):
    return lax.dot_general(a, b, (((1,), (1,)), ((), ())), preferred_element_type=F32)


def lanes(rows):
    return lax.broadcasted_iota(jnp.int32, (rows, PT), 1)


def fetch(sources, targets, sems):
    copies = [
        pltpu.make_async_copy(src, dst, sems.at[i])
        for i, (src, dst) in enumerate(zip(sources, targets))
    ]
    for copy in copies:
        copy.start()
    for copy in copies:
        copy.wait()


def pack_wide_kernel(*refs):
    up_ref, dn_ref = refs[4:6]
    fc_ref, b_ref, nb_ref, pt_ref = refs[6:10]
    fetch(refs[0:4], refs[6:10], refs[10])
    meta = jnp.concatenate(
        [
            (nb_ref[...] + 1).astype(F32),
            pt_ref[...].astype(F32),
            jnp.zeros((META - SLOTS - 1, PT), F32),
        ],
        axis=0,
    )
    top, low = fc_ref[0:HALF, :], fc_ref[HALF:W, :]
    first = lanes(HALF) < 64
    for ref in (up_ref, dn_ref):
        ref[0:W, :] = b_ref[...]
        ref[W:ROWS, :] = meta
    up_ref[ROWS : ROWS + HALF, :] = jnp.where(first, pltpu.roll(top, 64, 1), low)
    dn_ref[ROWS : ROWS + HALF, :] = jnp.where(first, top, pltpu.roll(low, 64, 1))


def unpack_fc(up, dn):
    first = lanes(HALF) < 64
    return jnp.concatenate(
        [
            jnp.where(first, dn, pltpu.roll(up, 64, 1)),
            jnp.where(first, pltpu.roll(dn, 64, 1), up),
        ],
        axis=0,
    )


def pack_short_kernel(fc_ref, own_ref, up_ref, dn_ref, lo_ref, hi_ref):
    first = lanes(META) < 64
    fc_ud = unpack_fc(up_ref[ROWS : ROWS + HALF, :], dn_ref[ROWS : ROWS + HALF, :])

    def part(rows, tiles):
        col = lanes(rows.stop - rows.start) % 32
        up, own, dn, edge, edge_ud = tiles

        def moved(x, shift):
            return pltpu.roll(x, shift, 1) if shift else x

        low = moved(up, 0)
        low = jnp.where(col < 4, low, moved(own, 4))
        low = jnp.where(col < 8, low, moved(dn, 8))
        low = jnp.where(col < 12, low, moved(edge, 12))
        lo_ref[rows, :] = jnp.where(col < 14, low, moved(edge_ud, 14))
        high = moved(edge, 114)
        high = jnp.where(col < 18, high, moved(edge_ud, 116))
        high = jnp.where(col < 20, high, moved(up, 120))
        high = jnp.where(col < 24, high, moved(own, 124))
        hi_ref[rows, :] = jnp.where(col < 28, high, dn)

    part(slice(0, W), (up_ref[0:W, :], own_ref[0:W, :], dn_ref[0:W, :], fc_ref[...], fc_ud))
    m = slice(W, ROWS)
    meta_ud = jnp.where(first, dn_ref[m, :], up_ref[m, :])
    part(m, (up_ref[m, :], own_ref[m, :], dn_ref[m, :], own_ref[m, :], meta_ud))


def weight_kernel(*refs):
    tw_ref, lw_ref, fw_ref = refs[4:7]
    tr_ref, ti_ref, lr_ref, li_ref = refs[7:11]
    fetch(refs[0:4], refs[7:11], refs[11])

    def turned(ref):
        n = ref.shape[0]
        fill = -n * HALF % PT
        side = jnp.concatenate([ref[...].reshape(n * HALF, HALF), jnp.zeros((n * HALF, 32), F32)], axis=1)
        if fill:
            side = jnp.concatenate([side, jnp.zeros((fill, PT), F32)], axis=0)
        return split(jnp.transpose(side)[0:HALF, :])

    def beside(ref):
        n = ref.shape[0]
        return split(
            jnp.concatenate([ref[s] for s in range(n)] + [jnp.zeros((HALF, -n * HALF % PT), F32)], axis=1)
        )

    def store(ref, real, imag, sign):
        width = real[0].shape[1]
        for at, re, im in zip((0, W), real, imag):
            ref[at : at + HALF, 0:width] = re
            ref[at : at + HALF, width:] = im if sign > 0 else -im
            ref[at + HALF : at + W, 0:width] = -im if sign > 0 else im
            ref[at + HALF : at + W, width:] = re

    store(tw_ref, turned(tr_ref), turned(ti_ref), 1)
    store(lw_ref, turned(lr_ref), turned(li_ref), 1)
    store(fw_ref, beside(lr_ref), beside(li_ref), -1)


def target_ids(base, row_stride):
    spot = lax.broadcasted_iota(jnp.int32, (3 * PT, PT), 0)
    lane = spot % PT
    row, col = lane // 32, lane % 32
    shift = jnp.where(row < 2, row_stride, -row_stride)
    own = base + lane
    beside = base + row * 32
    lr = jnp.where(
        col < 14,
        beside + PT + col - 12,
        jnp.where(
            col < 16,
            beside + PT + shift + col - 14,
            jnp.where(col < 18, beside - PT + col + 14, beside - PT + shift + col + 12),
        ),
    )
    lr = jnp.where((col >= 12) & (col < 20), lr, -10)
    ids = jnp.where(spot < PT, own, jnp.where(spot < 2 * PT, own + shift, lr))
    return jnp.where(ids >= 0, ids + 1, -10).astype(F32)


def main_kernel(
    base_ref,
    own_ref,
    up_ref,
    dn_ref,
    lf_ref,
    rt_ref,
    fc_ref,
    inc_ref,
    tw_ref,
    lw_ref,
    fw_ref,
    vec_ref,
    ghi_ref,
    glo_ref,
):
    m = slice(W, ROWS)
    ids = target_ids(base_ref[0], base_ref[1])
    own_ids = ids[0:PT, :]
    first = lanes(META) < 64
    col = lanes(META) % 32
    b = own_ref[0:W, :]
    m_own, m_up, m_dn = own_ref[m, :], up_ref[m, :], dn_ref[m, :]
    m_ud = jnp.where(first, m_dn, m_up)
    wide = lanes(W) % 32 >= 16
    m_lr = jnp.where(col >= 16, lf_ref[m, :], rt_ref[m, :])
    x_lr = jnp.where(wide, lf_ref[0:W, :], rt_ref[0:W, :])
    b_zone = (col < 12) | (col >= 20)
    row_id = lax.broadcasted_iota(jnp.int32, (META, PT), 0)
    m_b = jnp.where(b_zone | (row_id >= SLOTS), m_lr, 0.0)
    m_f = jnp.where(b_zone & (row_id < SLOTS), 0.0, m_lr)

    def product(w_ref, hi, lo):
        rows = dot(w_ref[...], hi)
        return rows[0:W] + rows[W : 2 * W] + dot(w_ref[0:W, :], lo)

    def scaled_by_type(blocks, metas):
        his, los = [], []
        for v, meta in zip(blocks, metas):
            hi, lo = split(v)
            kind = meta[SLOTS : SLOTS + 1, :]
            his.append([jnp.where(kind == float(k), hi, jnp.zeros_like(hi)) for k in range(KINDS)])
            los.append([jnp.where(kind == float(k), lo, jnp.zeros_like(lo)) for k in range(KINDS)])
        def by_part(pieces):
            whole = [jnp.concatenate([p[k] for p in pieces], axis=1) for k in range(KINDS)]
            return jnp.concatenate([w[0:HALF] for w in whole] + [w[HALF:W] for w in whole], axis=0)

        hi, lo = by_part(his), by_part(los)
        s_hi, s_lo = split(product(tw_ref, hi, lo))
        return jnp.concatenate([s_hi, s_lo], axis=0)

    def one_hot(at, meta, s):
        return jnp.where(at == meta[s : s + 1, :], 1.0, 0.0).astype(BF16)

    for ref in (ghi_ref, glo_ref):
        for at in (SLOTS * HALF, PART + SLOTS * HALF):
            ref[at : at + PART - SLOTS * HALF, :] = jnp.zeros((PART - SLOTS * HALF, 3 * PT), BF16)

    metas = (m_own, m_up, m_dn, m_b)
    stack = scaled_by_type((b, up_ref[0:W, :], dn_ref[0:W, :], x_lr), metas)
    for s in range(SLOTS):
        pick = jnp.concatenate([one_hot(ids, meta, s) for meta in metas], axis=1)
        g = dot_nt(stack, pick)
        hi, lo = split(g[0:W] + g[W : 2 * W])
        for ref, part in ((ghi_ref, hi), (glo_ref, lo)):
            ref[s * HALF : (s + 1) * HALF, :] = part[0:HALF]
            ref[PART + s * HALF : PART + (s + 1) * HALF, :] = part[HALF:W]
    u1_all = product(lw_ref, ghi_ref[...], glo_ref[...])
    u1 = u1_all[:, 0:PT]
    vec_ref[0:W, :] = b
    vec_ref[W : 2 * W, :] = u1

    metas = (m_own, m_ud, m_f)
    stack = scaled_by_type([u1_all[:, i * PT : (i + 1) * PT] for i in range(3)], metas)
    for s in range(0, SLOTS, 2):
        pick = jnp.concatenate(
            [
                jnp.concatenate([one_hot(own_ids, meta, t) for meta in metas], axis=1)
                for t in (s, s + 1)
            ],
            axis=0,
        )
        g = dot_nt(stack, pick)
        hi, lo = split(g[0:W] + g[W : 2 * W])
        for t in (0, 1):
            at = (s + t) * HALF
            for ref, part in ((ghi_ref, hi), (glo_ref, lo)):
                ref[at : at + HALF, 0:PT] = part[0:HALF, t * PT : (t + 1) * PT]
                ref[PART + at : PART + at + HALF, 0:PT] = part[HALF:W, t * PT : (t + 1) * PT]
    u2 = product(lw_ref, ghi_ref[:, 0:PT], glo_ref[:, 0:PT])

    fc_ud = unpack_fc(up_ref[ROWS : ROWS + HALF, :], dn_ref[ROWS : ROWS + HALF, :])
    f_hi, f_lo = split(jnp.concatenate([fc_ref[...], fc_ud, x_lr], axis=1))
    stack = jnp.concatenate([f_hi, f_lo], axis=0)
    for s in range(0, SLOTS, 2):
        pick = jnp.concatenate([one_hot(ids, m_own, s), one_hot(ids, m_own, s + 1)], axis=1)
        g = dot(stack, pick).astype(BF16)
        for t in (0, 1):
            at = (s + t) * HALF
            for ref, part in ((ghi_ref, g[0:W]), (glo_ref, g[W : 2 * W])):
                ref[at : at + HALF, PT : 2 * PT] = part[0:HALF, t * PT : (t + 1) * PT]
                ref[PART + at : PART + at + HALF, PT : 2 * PT] = part[
                    HALF:W, t * PT : (t + 1) * PT
                ]
    exc = inc_ref[...] + product(fw_ref, ghi_ref[:, PT : 2 * PT], glo_ref[:, PT : 2 * PT])

    vec_ref[2 * W : 3 * W, :] = exc

    lane, row = lanes(8), lax.broadcasted_iota(jnp.int32, (8, PT), 0)
    gram = jnp.zeros((8, PT), F32)
    for i, (p, q) in enumerate(((b, b), (b, u1), (u1, u1), (b, u2), (u1, u2), (u2, u2))):
        gram = jnp.where(lane == i, jnp.sum(p * q), gram)
    vec_ref[3 * W :, :] = jnp.where(row == 0, gram, m_own[SLOTS : SLOTS + 1, :])


def outer_kernel(base_ref, own_ref, other_ref, chunk_ref):
    def both(rows):
        return jnp.concatenate([own_ref[rows, :], other_ref[rows, :]], axis=1)

    exc = both(slice(2 * W, 3 * W))
    e_hi, e_lo = split(jnp.concatenate([exc, jnp.zeros((64, 2 * PT), F32)], axis=0))
    v_hi, v_lo = split(both(slice(0, 2 * W)))
    kind = both(slice(3 * W + 1, 3 * W + 2))
    for k in range(2):
        here = kind == (2 * base_ref[2] + k).astype(F32)
        k_hi = jnp.where(here, v_hi, jnp.zeros_like(v_hi))
        k_lo = jnp.where(here, v_lo, jnp.zeros_like(v_lo))
        out = dot_nt(k_hi, e_hi) + dot_nt(k_lo, e_hi) + dot_nt(k_hi, e_lo)
        for which in range(2):
            for h in range(2):
                block = out[which * W + h * HALF : which * W + (h + 1) * HALF, :]
                at = which * 144
                chunk_ref[2 * k + h, at : at + 96, :] = block[:, 0:PT]
                chunk_ref[2 * k + h, at + 96 : at + 144, :] = block[0:48, PT:] + pltpu.roll(
                    block[48:96, PT:], 64, 1
                )
    gram = own_ref[3 * W :, :] + other_ref[3 * W :, :]
    for g in range(4):
        chunk_ref[g, 288:296, :] = gram


def spread_kernel(in_ref, out_ref):
    total = in_ref[0]
    for i in range(1, 4):
        total = total + in_ref[i]
    out_ref[...] = jnp.zeros_like(out_ref)
    for which in range(2):
        for j in range(3):
            at = which * 144 + j * 48
            out_ref[pl.ds(3 * which + j, 48, 8), :] = total[at : at + 48, :]
    out_ref[pl.ds(6, 64, 8), :] = jnp.broadcast_to(total[288:289, :], (64, PT))


def combine_kernel(in_ref, vec_ref, out_ref, adj_ref):
    total = jnp.sum(in_ref[...].reshape(64, 8, PT), axis=0)
    lane = lanes(1)

    def entry(i):
        return jnp.sum(jnp.where(lane == i, total[6:7, :], 0.0), axis=1, keepdims=True)

    g00, g01, g11, g02, g12, g22 = [entry(i) for i in range(6)]
    alpha = g01 / g00
    beta = jnp.sqrt(g00)
    p2 = g11 - alpha * g01
    pn = jnp.sqrt(p2)
    h00 = 1.0 - alpha
    h10 = pn / beta
    h01 = (g02 - alpha * g01) / (beta * pn)
    qv1 = (g12 - alpha * g11 - alpha * g02 + alpha * alpha * g01) / p2
    h11 = 1.0 - qv1
    n00 = h00 * h00 + h10 * h10
    n01 = h00 * h01 + h10 * h11
    n11 = 1.0 - 2.0 * qv1 + (g22 - 2.0 * alpha * g12 + alpha * alpha * g11) / p2
    r0 = beta * h00
    r1 = beta * h01
    f00 = jnp.sqrt(n00)
    f10 = n01 / f00
    f11 = jnp.sqrt(n11 - f10 * f10)
    y0 = r0 / f00
    y1 = (r1 - f10 * y0) / f11
    w1 = y1 / f11
    w0 = (y0 - f10 * w1) / f00
    c1 = -w1 / pn
    c0 = w0 / beta - c1 * alpha
    mixed = c0 * total[0:3, :] + c1 * total[3:6, :]
    mixed = jnp.concatenate([mixed, jnp.zeros((1, PT), F32)] * 2, axis=0)
    for i in range(32):
        out_ref[8 * i : 8 * i + 8, :] = mixed
    adj_ref[...] = c0 * vec_ref[0:W, :] + c1 * vec_ref[W : 2 * W, :]


def copies_kernel(in_ref, out_ref):
    for j in range(3):
        rows = in_ref[pl.ds(j, 48, 4), :]
        for i in range(4):
            out_ref[i, 48 * j : 48 * (j + 1), :] = rows


def expand_kernel(base_ref, own_ref, other_ref, out_ref):
    core = base_ref[2]
    for ref, first in ((own_ref, 2 * core), (other_ref, 2 - 2 * core)):
        for k in range(2):
            for h in range(2):
                block = ref[2 * k + h]
                at = h * HALF
                edge = block[96:144, :]
                out_ref[first + k, at : at + HALF, 0:PT] = block[0:HALF, :]
                out_ref[first + k, at : at + 48, PT:W] = edge[:, 0:64]
                out_ref[first + k, at + 48 : at + HALF, PT:W] = pltpu.roll(edge, 64, 1)[:, 0:64]


def call(kernel, shapes, *args, smem=0, mib=6, dtype=F32, fetched=False, **kw):
    if fetched:
        kw["scratch_shapes"] = [pltpu.VMEM(a.shape, a.dtype) for a in args]
        kw["scratch_shapes"].append(pltpu.SemaphoreType.DMA((len(args),)))
    return pl.pallas_call(
        kernel,
        out_shape=[jax.ShapeDtypeStruct(s, dtype) for s in shapes],
        in_specs=[pl.BlockSpec(memory_space=pltpu.SMEM)] * smem
        + [pl.BlockSpec(memory_space=pltpu.HBM if fetched else pltpu.VMEM)] * (len(args) - smem),
        compiler_params=pltpu.CompilerParams(vmem_limit_bytes=mib * MIB),
        **kw,
    )(*args)


def shifted(block, axis, step):
    n = lax.axis_size(axis)
    return lax.ppermute(block, axis, [(i, i + step) for i in range(n) if 0 <= i + step < n])


def body(
    forward_coeff,
    incident,
    cost_grad,
    tmat_real,
    tmat_imag,
    translation_real,
    translation_imaginary,
    neighbours,
    particle_type,
):
    n_short = lax.axis_size("gy")
    tile = lax.axis_index("gx") * n_short + lax.axis_index("gy")
    core = lax.axis_index("gy") % 2
    base = jnp.stack([tile * PT, jnp.int32(n_short * PT), core]).astype(jnp.int32)

    to_up, to_dn = call(
        pack_wide_kernel,
        [(ROWS + HALF, PT)] * 2,
        forward_coeff,
        cost_grad,
        neighbours,
        particle_type.reshape(1, PT),
        mib=60,
        fetched=True,
    )
    up = shifted(to_up, "gx", 1)
    dn = shifted(to_dn, "gx", -1)
    to_lo, to_hi = call(
        pack_short_kernel, [(ROWS, PT)] * 2, forward_coeff, to_up, up, dn
    )
    lf = shifted(to_hi, "gy", 1)
    rt = shifted(to_lo, "gy", -1)

    tw, lw, fw = call(
        weight_kernel,
        [(2 * W, KINDS * W), (2 * W, 2 * PART), (2 * W, 2 * PART)],
        tmat_real,
        tmat_imag,
        translation_real,
        translation_imaginary,
        mib=16,
        dtype=BF16,
        fetched=True,
    )

    (vectors,) = call(
        main_kernel,
        [(3 * W + 8, PT)],
        base,
        to_up,
        up,
        dn,
        lf,
        rt,
        forward_coeff,
        incident,
        tw,
        lw,
        fw,
        smem=1,
        mib=24,
        scratch_shapes=[pltpu.VMEM((2 * PART, 3 * PT), BF16)] * 2,
    )
    pairs = [(i, i ^ 1) for i in range(n_short)]
    lines = [list(range(c, n_short, 2)) for c in range(2)]
    partner = lax.ppermute(vectors, "gy", pairs)
    (chunks,) = call(outer_kernel, [(4, CHUNK, PT)], base, vectors, partner, smem=1)
    got = lax.all_to_all(chunks, "gy", 0, 0, axis_index_groups=lines)
    (pieces,) = call(spread_kernel, [(512, PT)], got)
    got = lax.all_to_all(pieces.reshape(64, 8, PT), "gx", 0, 0)
    mixed, adjoint = call(combine_kernel, [(256, PT), (W, PT)], got.reshape(512, PT), vectors)
    got = lax.all_to_all(mixed.reshape(64, 4, PT), "gx", 0, 0)
    (copies,) = call(copies_kernel, [(4, 144, PT)], got.reshape(256, PT))
    half = lax.all_to_all(copies, "gy", 0, 0, axis_index_groups=lines)
    other = lax.ppermute(half, "gy", pairs)
    (sensitivity,) = call(expand_kernel, [(KINDS, W, W)], base, half, other, smem=1)
    return (adjoint, sensitivity)


def solution(mesh):
    placed = (
        P(None, ("gx", "gy")),
        P(None, ("gx", "gy")),
        P(None, ("gx", "gy")),
        P(),
        P(),
        P(),
        P(),
        P(None, ("gx", "gy")),
        P(("gx", "gy")),
    )
    return jax.shard_map(
        body, mesh=mesh, in_specs=placed, out_specs=(P(None, ("gx", "gy")), P()), check_vma=False
    )
```

```python
import jax
import jax.numpy as jnp
from jax import lax
from jax.experimental import pallas as pl
from jax.experimental.pallas import tpu as pltpu
from jax.sharding import PartitionSpec as P

F32 = jnp.float32
BF16 = jnp.bfloat16
W = 192
HALF = 96
PT = 128
SLOTS = 10
KINDS = 4
META = 16
ROWS = W + META
CHUNK = 296
PART = 1024
MIB = 1024 * 1024


def split(x):
    hi = x.astype(BF16)
    return hi, (x - hi.astype(F32)).astype(BF16)


def dot(a, b):
    return lax.dot_general(a, b, (((1,), (0,)), ((), ())), preferred_element_type=F32)


def dot_nt(a, b):
    return lax.dot_general(a, b, (((1,), (1,)), ((), ())), preferred_element_type=F32)


def lanes(rows):
    return lax.broadcasted_iota(jnp.int32, (rows, PT), 1)


def fetch(sources, targets, sems):
    copies = [
        pltpu.make_async_copy(src, dst, sems.at[i])
        for i, (src, dst) in enumerate(zip(sources, targets))
    ]
    for copy in copies:
        copy.start()
    for copy in copies:
        copy.wait()


def meta_rows(nb_ref, pt_ref):
    return jnp.concatenate(
        [
            (nb_ref[...] + 1).astype(F32),
            pt_ref[...].astype(F32),
            jnp.zeros((META - SLOTS - 1, PT), F32),
        ],
        axis=0,
    )


def pack_wide_kernel(*refs):
    up_ref, dn_ref = refs[4:6]
    fc_ref, b_ref, nb_ref, pt_ref = refs[6:10]
    fetch(refs[0:4], refs[6:10], refs[10])
    meta = meta_rows(nb_ref, pt_ref)
    top, low = fc_ref[0:HALF, :], fc_ref[HALF:W, :]
    first = lanes(HALF) < 64
    for ref in (up_ref, dn_ref):
        ref[0:W, :] = b_ref[...]
        ref[W:ROWS, :] = meta
    up_ref[ROWS : ROWS + HALF, :] = jnp.where(first, pltpu.roll(top, 64, 1), low)
    dn_ref[ROWS : ROWS + HALF, :] = jnp.where(first, top, pltpu.roll(low, 64, 1))


def unpack_fc(up, dn):
    first = lanes(HALF) < 64
    return jnp.concatenate(
        [
            jnp.where(first, dn, pltpu.roll(up, 64, 1)),
            jnp.where(first, pltpu.roll(dn, 64, 1), up),
        ],
        axis=0,
    )


def pack_short_kernel(fc_ref, b_ref, nb_ref, pt_ref, up_ref, dn_ref, lo_ref, hi_ref):
    first = lanes(META) < 64
    meta = meta_rows(nb_ref, pt_ref)
    fc_ud = unpack_fc(up_ref[ROWS : ROWS + HALF, :], dn_ref[ROWS : ROWS + HALF, :])

    def part(rows, tiles):
        col = lanes(rows.stop - rows.start) % 32
        up, own, dn, edge, edge_ud = tiles

        def moved(x, shift):
            return pltpu.roll(x, shift, 1) if shift else x

        low = moved(up, 0)
        low = jnp.where(col < 4, low, moved(own, 4))
        low = jnp.where(col < 8, low, moved(dn, 8))
        low = jnp.where(col < 12, low, moved(edge, 12))
        lo_ref[rows, :] = jnp.where(col < 14, low, moved(edge_ud, 14))
        high = moved(edge, 114)
        high = jnp.where(col < 18, high, moved(edge_ud, 116))
        high = jnp.where(col < 20, high, moved(up, 120))
        high = jnp.where(col < 24, high, moved(own, 124))
        hi_ref[rows, :] = jnp.where(col < 28, high, dn)

    part(slice(0, W), (up_ref[0:W, :], b_ref[...], dn_ref[0:W, :], fc_ref[...], fc_ud))
    m = slice(W, ROWS)
    meta_ud = jnp.where(first, dn_ref[m, :], up_ref[m, :])
    part(m, (up_ref[m, :], meta, dn_ref[m, :], meta, meta_ud))


def weight_kernel(tr_ref, ti_ref, lr_ref, li_ref, tw_ref, lw_ref, fw_ref):
    def turned(ref):
        n = ref.shape[0]
        fill = -n * HALF % PT
        side = jnp.concatenate([ref[...].reshape(n * HALF, HALF), jnp.zeros((n * HALF, 32), F32)], axis=1)
        if fill:
            side = jnp.concatenate([side, jnp.zeros((fill, PT), F32)], axis=0)
        return split(jnp.transpose(side)[0:HALF, :])

    def beside(ref):
        n = ref.shape[0]
        return split(
            jnp.concatenate([ref[s] for s in range(n)] + [jnp.zeros((HALF, -n * HALF % PT), F32)], axis=1)
        )

    def store(ref, real, imag, sign):
        width = real[0].shape[1]
        for at, re, im in zip((0, W), real, imag):
            ref[at : at + HALF, 0:width] = re
            ref[at : at + HALF, width:] = im if sign > 0 else -im
            ref[at + HALF : at + W, 0:width] = -im if sign > 0 else im
            ref[at + HALF : at + W, width:] = re

    store(tw_ref, turned(tr_ref), turned(ti_ref), 1)
    store(lw_ref, turned(lr_ref), turned(li_ref), 1)
    store(fw_ref, beside(lr_ref), beside(li_ref), -1)


def target_ids(base, row_stride):
    spot = lax.broadcasted_iota(jnp.int32, (3 * PT, PT), 0)
    lane = spot % PT
    row, col = lane // 32, lane % 32
    shift = jnp.where(row < 2, row_stride, -row_stride)
    own = base + lane
    beside = base + row * 32
    lr = jnp.where(
        col < 14,
        beside + PT + col - 12,
        jnp.where(
            col < 16,
            beside + PT + shift + col - 14,
            jnp.where(col < 18, beside - PT + col + 14, beside - PT + shift + col + 12),
        ),
    )
    lr = jnp.where((col >= 12) & (col < 20), lr, -10)
    ids = jnp.where(spot < PT, own, jnp.where(spot < 2 * PT, own + shift, lr))
    return jnp.where(ids >= 0, ids + 1, -10).astype(F32)


def main_kernel(
    base_ref,
    b_ref,
    nb_ref,
    pt_ref,
    up_ref,
    dn_ref,
    lf_ref,
    rt_ref,
    fc_ref,
    inc_ref,
    tw_ref,
    lw_ref,
    fw_ref,
    vec_ref,
    ghi_ref,
    glo_ref,
):
    m = slice(W, ROWS)
    ids = target_ids(base_ref[0], base_ref[1])
    own_ids = ids[0:PT, :]
    first = lanes(META) < 64
    col = lanes(META) % 32
    b = b_ref[...]
    m_own, m_up, m_dn = meta_rows(nb_ref, pt_ref), up_ref[m, :], dn_ref[m, :]
    m_ud = jnp.where(first, m_dn, m_up)
    wide = lanes(W) % 32 >= 16
    m_lr = jnp.where(col >= 16, lf_ref[m, :], rt_ref[m, :])
    x_lr = jnp.where(wide, lf_ref[0:W, :], rt_ref[0:W, :])
    b_zone = (col < 12) | (col >= 20)
    row_id = lax.broadcasted_iota(jnp.int32, (META, PT), 0)
    m_b = jnp.where(b_zone | (row_id >= SLOTS), m_lr, 0.0)
    m_f = jnp.where(b_zone & (row_id < SLOTS), 0.0, m_lr)

    def product(w_ref, hi, lo):
        rows = dot(w_ref[...], hi)
        return rows[0:W] + rows[W : 2 * W] + dot(w_ref[0:W, :], lo)

    def scaled_by_type(blocks, metas):
        his, los = [], []
        for v, meta in zip(blocks, metas):
            hi, lo = split(v)
            kind = meta[SLOTS : SLOTS + 1, :]
            his.append([jnp.where(kind == float(k), hi, jnp.zeros_like(hi)) for k in range(KINDS)])
            los.append([jnp.where(kind == float(k), lo, jnp.zeros_like(lo)) for k in range(KINDS)])
        def by_part(pieces):
            whole = [jnp.concatenate([p[k] for p in pieces], axis=1) for k in range(KINDS)]
            return jnp.concatenate([w[0:HALF] for w in whole] + [w[HALF:W] for w in whole], axis=0)

        hi, lo = by_part(his), by_part(los)
        s_hi, s_lo = split(product(tw_ref, hi, lo))
        return jnp.concatenate([s_hi, s_lo], axis=0)

    def one_hot(at, meta, s):
        return jnp.where(at == meta[s : s + 1, :], 1.0, 0.0).astype(BF16)

    for ref in (ghi_ref, glo_ref):
        for at in (SLOTS * HALF, PART + SLOTS * HALF):
            ref[at : at + PART - SLOTS * HALF, :] = jnp.zeros((PART - SLOTS * HALF, 3 * PT), BF16)

    metas = (m_own, m_up, m_dn, m_b)
    stack = scaled_by_type((b, up_ref[0:W, :], dn_ref[0:W, :], x_lr), metas)
    for s in range(SLOTS):
        pick = jnp.concatenate([one_hot(ids, meta, s) for meta in metas], axis=1)
        g = dot_nt(stack, pick)
        hi, lo = split(g[0:W] + g[W : 2 * W])
        for ref, part in ((ghi_ref, hi), (glo_ref, lo)):
            ref[s * HALF : (s + 1) * HALF, :] = part[0:HALF]
            ref[PART + s * HALF : PART + (s + 1) * HALF, :] = part[HALF:W]
    u1_all = product(lw_ref, ghi_ref[...], glo_ref[...])
    u1 = u1_all[:, 0:PT]
    vec_ref[0:W, :] = b
    vec_ref[W : 2 * W, :] = u1

    metas = (m_own, m_ud, m_f)
    stack = scaled_by_type([u1_all[:, i * PT : (i + 1) * PT] for i in range(3)], metas)
    for s in range(0, SLOTS, 2):
        pick = jnp.concatenate(
            [
                jnp.concatenate([one_hot(own_ids, meta, t) for meta in metas], axis=1)
                for t in (s, s + 1)
            ],
            axis=0,
        )
        g = dot_nt(stack, pick)
        hi, lo = split(g[0:W] + g[W : 2 * W])
        for t in (0, 1):
            at = (s + t) * HALF
            for ref, part in ((ghi_ref, hi), (glo_ref, lo)):
                ref[at : at + HALF, 0:PT] = part[0:HALF, t * PT : (t + 1) * PT]
                ref[PART + at : PART + at + HALF, 0:PT] = part[HALF:W, t * PT : (t + 1) * PT]
    u2 = product(lw_ref, ghi_ref[:, 0:PT], glo_ref[:, 0:PT])

    fc_ud = unpack_fc(up_ref[ROWS : ROWS + HALF, :], dn_ref[ROWS : ROWS + HALF, :])
    f_hi, f_lo = split(jnp.concatenate([fc_ref[...], fc_ud, x_lr], axis=1))
    stack = jnp.concatenate([f_hi, f_lo], axis=0)
    for s in range(0, SLOTS, 2):
        pick = jnp.concatenate([one_hot(ids, m_own, s), one_hot(ids, m_own, s + 1)], axis=1)
        g = dot(stack, pick).astype(BF16)
        for t in (0, 1):
            at = (s + t) * HALF
            for ref, part in ((ghi_ref, g[0:W]), (glo_ref, g[W : 2 * W])):
                ref[at : at + HALF, PT : 2 * PT] = part[0:HALF, t * PT : (t + 1) * PT]
                ref[PART + at : PART + at + HALF, PT : 2 * PT] = part[
                    HALF:W, t * PT : (t + 1) * PT
                ]
    exc = inc_ref[...] + product(fw_ref, ghi_ref[:, PT : 2 * PT], glo_ref[:, PT : 2 * PT])

    vec_ref[2 * W : 3 * W, :] = exc

    lane, row = lanes(8), lax.broadcasted_iota(jnp.int32, (8, PT), 0)
    gram = jnp.zeros((8, PT), F32)
    for i, (p, q) in enumerate(((b, b), (b, u1), (u1, u1), (b, u2), (u1, u2), (u2, u2))):
        gram = jnp.where(lane == i, jnp.sum(p * q), gram)
    vec_ref[3 * W :, :] = jnp.where(row == 0, gram, m_own[SLOTS : SLOTS + 1, :])


def outer_kernel(base_ref, own_ref, other_ref, chunk_ref):
    def both(rows):
        return jnp.concatenate([own_ref[rows, :], other_ref[rows, :]], axis=1)

    exc = both(slice(2 * W, 3 * W))
    e_hi, e_lo = split(jnp.concatenate([exc, jnp.zeros((64, 2 * PT), F32)], axis=0))
    v_hi, v_lo = split(both(slice(0, 2 * W)))
    kind = both(slice(3 * W + 1, 3 * W + 2))
    for k in range(2):
        here = kind == (2 * base_ref[2] + k).astype(F32)
        k_hi = jnp.where(here, v_hi, jnp.zeros_like(v_hi))
        k_lo = jnp.where(here, v_lo, jnp.zeros_like(v_lo))
        out = dot_nt(k_hi, e_hi) + dot_nt(k_lo, e_hi) + dot_nt(k_hi, e_lo)
        for which in range(2):
            for h in range(2):
                block = out[which * W + h * HALF : which * W + (h + 1) * HALF, :]
                at = which * 144
                chunk_ref[2 * k + h, at : at + 96, :] = block[:, 0:PT]
                chunk_ref[2 * k + h, at + 96 : at + 144, :] = block[0:48, PT:] + pltpu.roll(
                    block[48:96, PT:], 64, 1
                )
    gram = own_ref[3 * W :, :] + other_ref[3 * W :, :]
    for g in range(4):
        chunk_ref[g, 288:296, :] = gram


def spread_kernel(in_ref, out_ref):
    total = in_ref[0]
    for i in range(1, 4):
        total = total + in_ref[i]
    out_ref[...] = jnp.zeros_like(out_ref)
    for which in range(2):
        for j in range(3):
            at = which * 144 + j * 48
            out_ref[pl.ds(3 * which + j, 48, 8), :] = total[at : at + 48, :]
    out_ref[pl.ds(6, 64, 8), :] = jnp.broadcast_to(total[288:289, :], (64, PT))


def combine_kernel(in_ref, vec_ref, out_ref, adj_ref):
    total = jnp.sum(in_ref[...].reshape(64, 8, PT), axis=0)
    lane = lanes(1)

    def entry(i):
        return jnp.sum(jnp.where(lane == i, total[6:7, :], 0.0), axis=1, keepdims=True)

    g00, g01, g11, g02, g12, g22 = [entry(i) for i in range(6)]
    alpha = g01 / g00
    beta = jnp.sqrt(g00)
    p2 = g11 - alpha * g01
    pn = jnp.sqrt(p2)
    h00 = 1.0 - alpha
    h10 = pn / beta
    h01 = (g02 - alpha * g01) / (beta * pn)
    qv1 = (g12 - alpha * g11 - alpha * g02 + alpha * alpha * g01) / p2
    h11 = 1.0 - qv1
    n00 = h00 * h00 + h10 * h10
    n01 = h00 * h01 + h10 * h11
    n11 = 1.0 - 2.0 * qv1 + (g22 - 2.0 * alpha * g12 + alpha * alpha * g11) / p2
    r0 = beta * h00
    r1 = beta * h01
    f00 = jnp.sqrt(n00)
    f10 = n01 / f00
    f11 = jnp.sqrt(n11 - f10 * f10)
    y0 = r0 / f00
    y1 = (r1 - f10 * y0) / f11
    w1 = y1 / f11
    w0 = (y0 - f10 * w1) / f00
    c1 = -w1 / pn
    c0 = w0 / beta - c1 * alpha
    mixed = c0 * total[0:3, :] + c1 * total[3:6, :]
    mixed = jnp.concatenate([mixed, jnp.zeros((1, PT), F32)] * 2, axis=0)
    for i in range(32):
        out_ref[8 * i : 8 * i + 8, :] = mixed
    adj_ref[...] = c0 * vec_ref[0:W, :] + c1 * vec_ref[W : 2 * W, :]


def copies_kernel(in_ref, out_ref):
    for j in range(3):
        rows = in_ref[pl.ds(j, 48, 4), :]
        for i in range(4):
            out_ref[i, 48 * j : 48 * (j + 1), :] = rows


def expand_kernel(base_ref, own_ref, other_ref, out_ref):
    core = base_ref[2]
    for ref, first in ((own_ref, 2 * core), (other_ref, 2 - 2 * core)):
        for k in range(2):
            for h in range(2):
                block = ref[2 * k + h]
                at = h * HALF
                edge = block[96:144, :]
                out_ref[first + k, at : at + HALF, 0:PT] = block[0:HALF, :]
                out_ref[first + k, at : at + 48, PT:W] = edge[:, 0:64]
                out_ref[first + k, at + 48 : at + HALF, PT:W] = pltpu.roll(edge, 64, 1)[:, 0:64]


def call(kernel, shapes, *args, smem=0, mib=6, dtype=F32, fetched=False, **kw):
    if fetched:
        kw["scratch_shapes"] = [pltpu.VMEM(a.shape, a.dtype) for a in args]
        kw["scratch_shapes"].append(pltpu.SemaphoreType.DMA((len(args),)))
    return pl.pallas_call(
        kernel,
        out_shape=[jax.ShapeDtypeStruct(s, dtype) for s in shapes],
        in_specs=[pl.BlockSpec(memory_space=pltpu.SMEM)] * smem
        + [pl.BlockSpec(memory_space=pltpu.HBM if fetched else pltpu.VMEM)] * (len(args) - smem),
        compiler_params=pltpu.CompilerParams(vmem_limit_bytes=mib * MIB),
        **kw,
    )(*args)


def shifted(block, axis, step):
    n = lax.axis_size(axis)
    return lax.ppermute(block, axis, [(i, i + step) for i in range(n) if 0 <= i + step < n])


def body(
    forward_coeff,
    incident,
    cost_grad,
    tmat_real,
    tmat_imag,
    translation_real,
    translation_imaginary,
    neighbours,
    particle_type,
):
    n_short = lax.axis_size("gy")
    tile = lax.axis_index("gx") * n_short + lax.axis_index("gy")
    core = lax.axis_index("gy") % 2
    base = jnp.stack([tile * PT, jnp.int32(n_short * PT), core]).astype(jnp.int32)

    kinds = particle_type.reshape(1, PT)
    to_up, to_dn = call(
        pack_wide_kernel,
        [(ROWS + HALF, PT)] * 2,
        forward_coeff,
        cost_grad,
        neighbours,
        kinds,
        mib=60,
        fetched=True,
    )
    up = shifted(to_up, "gx", 1)
    dn = shifted(to_dn, "gx", -1)
    to_lo, to_hi = call(
        pack_short_kernel, [(ROWS, PT)] * 2, forward_coeff, cost_grad, neighbours, kinds, up, dn
    )
    lf = shifted(to_hi, "gy", 1)
    rt = shifted(to_lo, "gy", -1)

    tw, lw, fw = call(
        weight_kernel,
        [(2 * W, KINDS * W), (2 * W, 2 * PART), (2 * W, 2 * PART)],
        tmat_real,
        tmat_imag,
        translation_real,
        translation_imaginary,
        mib=16,
        dtype=BF16,
    )

    (vectors,) = call(
        main_kernel,
        [(3 * W + 8, PT)],
        base,
        cost_grad,
        neighbours,
        kinds,
        up,
        dn,
        lf,
        rt,
        forward_coeff,
        incident,
        tw,
        lw,
        fw,
        smem=1,
        mib=24,
        scratch_shapes=[pltpu.VMEM((2 * PART, 3 * PT), BF16)] * 2,
    )
    pairs = [(i, i ^ 1) for i in range(n_short)]
    lines = [list(range(c, n_short, 2)) for c in range(2)]
    partner = lax.ppermute(vectors, "gy", pairs)
    (chunks,) = call(outer_kernel, [(4, CHUNK, PT)], base, vectors, partner, smem=1)
    got = lax.all_to_all(chunks, "gy", 0, 0, axis_index_groups=lines)
    (pieces,) = call(spread_kernel, [(512, PT)], got)
    got = lax.all_to_all(pieces.reshape(64, 8, PT), "gx", 0, 0)
    mixed, adjoint = call(combine_kernel, [(256, PT), (W, PT)], got.reshape(512, PT), vectors)
    got = lax.all_to_all(mixed.reshape(64, 4, PT), "gx", 0, 0)
    (copies,) = call(copies_kernel, [(4, 144, PT)], got.reshape(256, PT))
    half = lax.all_to_all(copies, "gy", 0, 0, axis_index_groups=lines)
    other = lax.ppermute(half, "gy", pairs)
    (sensitivity,) = call(expand_kernel, [(KINDS, W, W)], base, half, other, smem=1)
    return (adjoint, sensitivity)


def solution(mesh):
    placed = (
        P(None, ("gx", "gy")),
        P(None, ("gx", "gy")),
        P(None, ("gx", "gy")),
        P(),
        P(),
        P(),
        P(),
        P(None, ("gx", "gy")),
        P(("gx", "gy")),
    )
    return jax.shard_map(
        body, mesh=mesh, in_specs=placed, out_specs=(P(None, ("gx", "gy")), P()), check_vma=False
    )
```

```python
import jax
import jax.numpy as jnp
from jax import lax
from jax.experimental import pallas as pl
from jax.experimental.pallas import tpu as pltpu
from jax.sharding import PartitionSpec as P

F32 = jnp.float32
BF16 = jnp.bfloat16
W = 192
HALF = 96
PT = 128
SLOTS = 10
KINDS = 4
META = 16
ROWS = W + META
CHUNK = 296
PART = 1024
MIB = 1024 * 1024


def split(x):
    hi = x.astype(BF16)
    return hi, (x - hi.astype(F32)).astype(BF16)


def dot(a, b):
    return lax.dot_general(a, b, (((1,), (0,)), ((), ())), preferred_element_type=F32)


def dot_nt(a, b):
    return lax.dot_general(a, b, (((1,), (1,)), ((), ())), preferred_element_type=F32)


def lanes(rows):
    return lax.broadcasted_iota(jnp.int32, (rows, PT), 1)


def fetch(sources, targets, sems):
    copies = [
        pltpu.make_async_copy(src, dst, sems.at[i])
        for i, (src, dst) in enumerate(zip(sources, targets))
    ]
    for copy in copies:
        copy.start()
    for copy in copies:
        copy.wait()


def meta_rows(nb_ref, pt_ref):
    return jnp.concatenate(
        [
            (nb_ref[...] + 1).astype(F32),
            pt_ref[...].astype(F32),
            jnp.zeros((META - SLOTS - 1, PT), F32),
        ],
        axis=0,
    )


def pack_wide_kernel(*refs):
    up_ref, dn_ref = refs[4:6]
    fc_ref, b_ref, nb_ref, pt_ref = refs[6:10]
    fetch(refs[0:4], refs[6:10], refs[10])
    meta = meta_rows(nb_ref, pt_ref)
    top, low = fc_ref[0:HALF, :], fc_ref[HALF:W, :]
    first = lanes(HALF) < 64
    for ref in (up_ref, dn_ref):
        ref[0:W, :] = b_ref[...]
        ref[W:ROWS, :] = meta
    up_ref[ROWS : ROWS + HALF, :] = jnp.where(first, pltpu.roll(top, 64, 1), low)
    dn_ref[ROWS : ROWS + HALF, :] = jnp.where(first, top, pltpu.roll(low, 64, 1))


def unpack_fc(up, dn):
    first = lanes(HALF) < 64
    return jnp.concatenate(
        [
            jnp.where(first, dn, pltpu.roll(up, 64, 1)),
            jnp.where(first, pltpu.roll(dn, 64, 1), up),
        ],
        axis=0,
    )


def pack_short_kernel(fc_ref, b_ref, nb_ref, pt_ref, up_ref, dn_ref, lo_ref, hi_ref):
    first = lanes(META) < 64
    meta = meta_rows(nb_ref, pt_ref)
    fc_ud = unpack_fc(up_ref[ROWS : ROWS + HALF, :], dn_ref[ROWS : ROWS + HALF, :])

    def part(rows, tiles):
        col = lanes(rows.stop - rows.start) % 32
        up, own, dn, edge, edge_ud = tiles

        def moved(x, shift):
            return pltpu.roll(x, shift, 1) if shift else x

        low = moved(up, 0)
        low = jnp.where(col < 4, low, moved(own, 4))
        low = jnp.where(col < 8, low, moved(dn, 8))
        low = jnp.where(col < 12, low, moved(edge, 12))
        lo_ref[rows, :] = jnp.where(col < 14, low, moved(edge_ud, 14))
        high = moved(edge, 114)
        high = jnp.where(col < 18, high, moved(edge_ud, 116))
        high = jnp.where(col < 20, high, moved(up, 120))
        high = jnp.where(col < 24, high, moved(own, 124))
        hi_ref[rows, :] = jnp.where(col < 28, high, dn)

    part(slice(0, W), (up_ref[0:W, :], b_ref[...], dn_ref[0:W, :], fc_ref[...], fc_ud))
    m = slice(W, ROWS)
    meta_ud = jnp.where(first, dn_ref[m, :], up_ref[m, :])
    part(m, (up_ref[m, :], meta, dn_ref[m, :], meta, meta_ud))


def weight_kernel(tr_ref, ti_ref, lr_ref, li_ref, tw_ref, lw_ref, fw_ref):
    def turned(ref):
        n = ref.shape[0]
        fill = -n * HALF % PT
        side = jnp.concatenate([ref[...].reshape(n * HALF, HALF), jnp.zeros((n * HALF, 32), F32)], axis=1)
        if fill:
            side = jnp.concatenate([side, jnp.zeros((fill, PT), F32)], axis=0)
        return split(jnp.transpose(side)[0:HALF, :])

    def beside(ref):
        n = ref.shape[0]
        return split(
            jnp.concatenate([ref[s] for s in range(n)] + [jnp.zeros((HALF, -n * HALF % PT), F32)], axis=1)
        )

    def store(ref, real, imag, sign):
        width = real[0].shape[1]
        for at, re, im in zip((0, W), real, imag):
            ref[at : at + HALF, 0:width] = re
            ref[at : at + HALF, width:] = im if sign > 0 else -im
            ref[at + HALF : at + W, 0:width] = -im if sign > 0 else im
            ref[at + HALF : at + W, width:] = re

    store(tw_ref, turned(tr_ref), turned(ti_ref), 1)
    store(lw_ref, turned(lr_ref), turned(li_ref), 1)
    store(fw_ref, beside(lr_ref), beside(li_ref), -1)


def target_ids(base, row_stride):
    spot = lax.broadcasted_iota(jnp.int32, (3 * PT, PT), 0)
    lane = spot % PT
    row, col = lane // 32, lane % 32
    shift = jnp.where(row < 2, row_stride, -row_stride)
    own = base + lane
    beside = base + row * 32
    lr = jnp.where(
        col < 14,
        beside + PT + col - 12,
        jnp.where(
            col < 16,
            beside + PT + shift + col - 14,
            jnp.where(col < 18, beside - PT + col + 14, beside - PT + shift + col + 12),
        ),
    )
    lr = jnp.where((col >= 12) & (col < 20), lr, -10)
    ids = jnp.where(spot < PT, own, jnp.where(spot < 2 * PT, own + shift, lr))
    return jnp.where(ids >= 0, ids + 1, -10).astype(F32)


def main_kernel(
    base_ref,
    b_ref,
    nb_ref,
    pt_ref,
    up_ref,
    dn_ref,
    lf_ref,
    rt_ref,
    fc_ref,
    inc_ref,
    tw_ref,
    lw_ref,
    fw_ref,
    vec_ref,
    ghi_ref,
    glo_ref,
):
    m = slice(W, ROWS)
    ids = target_ids(base_ref[0], base_ref[1])
    own_ids = ids[0:PT, :]
    first = lanes(META) < 64
    col = lanes(META) % 32
    b = b_ref[...]
    m_own, m_up, m_dn = meta_rows(nb_ref, pt_ref), up_ref[m, :], dn_ref[m, :]
    m_ud = jnp.where(first, m_dn, m_up)
    wide = lanes(W) % 32 >= 16
    m_lr = jnp.where(col >= 16, lf_ref[m, :], rt_ref[m, :])
    x_lr = jnp.where(wide, lf_ref[0:W, :], rt_ref[0:W, :])
    b_zone = (col < 12) | (col >= 20)
    row_id = lax.broadcasted_iota(jnp.int32, (META, PT), 0)
    m_b = jnp.where(b_zone | (row_id >= SLOTS), m_lr, 0.0)
    m_f = jnp.where(b_zone & (row_id < SLOTS), 0.0, m_lr)

    def product(w_ref, hi, lo):
        rows = dot(w_ref[...], hi)
        return rows[0:W] + rows[W : 2 * W] + dot(w_ref[0:W, :], lo)

    def scaled_by_type(blocks, metas):
        his, los = [], []
        for v, meta in zip(blocks, metas):
            hi, lo = split(v)
            kind = meta[SLOTS : SLOTS + 1, :]
            his.append([jnp.where(kind == float(k), hi, jnp.zeros_like(hi)) for k in range(KINDS)])
            los.append([jnp.where(kind == float(k), lo, jnp.zeros_like(lo)) for k in range(KINDS)])
        def by_part(pieces):
            whole = [jnp.concatenate([p[k] for p in pieces], axis=1) for k in range(KINDS)]
            return jnp.concatenate([w[0:HALF] for w in whole] + [w[HALF:W] for w in whole], axis=0)

        hi, lo = by_part(his), by_part(los)
        s_hi, s_lo = split(product(tw_ref, hi, lo))
        return jnp.concatenate([s_hi, s_lo], axis=0)

    def one_hot(at, meta, s):
        return jnp.where(at == meta[s : s + 1, :], 1.0, 0.0).astype(BF16)

    for ref in (ghi_ref, glo_ref):
        for at in (SLOTS * HALF, PART + SLOTS * HALF):
            ref[at : at + PART - SLOTS * HALF, :] = jnp.zeros((PART - SLOTS * HALF, 3 * PT), BF16)

    metas = (m_own, m_up, m_dn, m_b)
    stack = scaled_by_type((b, up_ref[0:W, :], dn_ref[0:W, :], x_lr), metas)
    for s in range(SLOTS):
        pick = jnp.concatenate([one_hot(ids, meta, s) for meta in metas], axis=1)
        g = dot_nt(stack, pick)
        hi, lo = split(g[0:W] + g[W : 2 * W])
        for ref, part in ((ghi_ref, hi), (glo_ref, lo)):
            ref[s * HALF : (s + 1) * HALF, :] = part[0:HALF]
            ref[PART + s * HALF : PART + (s + 1) * HALF, :] = part[HALF:W]
    u1_all = product(lw_ref, ghi_ref[...], glo_ref[...])
    u1 = u1_all[:, 0:PT]
    vec_ref[0:W, :] = b
    vec_ref[W : 2 * W, :] = u1

    metas = (m_own, m_ud, m_f)
    stack = scaled_by_type([u1_all[:, i * PT : (i + 1) * PT] for i in range(3)], metas)
    for s in range(0, SLOTS, 2):
        pick = jnp.concatenate(
            [
                jnp.concatenate([one_hot(own_ids, meta, t) for meta in metas], axis=1)
                for t in (s, s + 1)
            ],
            axis=0,
        )
        g = dot_nt(stack, pick)
        hi, lo = split(g[0:W] + g[W : 2 * W])
        for t in (0, 1):
            at = (s + t) * HALF
            for ref, part in ((ghi_ref, hi), (glo_ref, lo)):
                ref[at : at + HALF, 0:PT] = part[0:HALF, t * PT : (t + 1) * PT]
                ref[PART + at : PART + at + HALF, 0:PT] = part[HALF:W, t * PT : (t + 1) * PT]
    u2 = product(lw_ref, ghi_ref[:, 0:PT], glo_ref[:, 0:PT])

    fc_ud = unpack_fc(up_ref[ROWS : ROWS + HALF, :], dn_ref[ROWS : ROWS + HALF, :])
    f_hi, f_lo = split(jnp.concatenate([fc_ref[...], fc_ud, x_lr], axis=1))
    stack = jnp.concatenate([f_hi, f_lo], axis=0)
    for s in range(0, SLOTS, 2):
        pick = jnp.concatenate([one_hot(ids, m_own, s), one_hot(ids, m_own, s + 1)], axis=1)
        g = dot(stack, pick).astype(BF16)
        for t in (0, 1):
            at = (s + t) * HALF
            for ref, part in ((ghi_ref, g[0:W]), (glo_ref, g[W : 2 * W])):
                ref[at : at + HALF, PT : 2 * PT] = part[0:HALF, t * PT : (t + 1) * PT]
                ref[PART + at : PART + at + HALF, PT : 2 * PT] = part[
                    HALF:W, t * PT : (t + 1) * PT
                ]
    exc = inc_ref[...] + product(fw_ref, ghi_ref[:, PT : 2 * PT], glo_ref[:, PT : 2 * PT])

    vec_ref[2 * W : 3 * W, :] = exc

    lane, row = lanes(8), lax.broadcasted_iota(jnp.int32, (8, PT), 0)
    gram = jnp.zeros((8, PT), F32)
    for i, (p, q) in enumerate(((b, b), (b, u1), (u1, u1), (b, u2), (u1, u2), (u2, u2))):
        gram = jnp.where(lane == i, jnp.sum(p * q), gram)
    vec_ref[3 * W :, :] = jnp.where(row == 0, gram, m_own[SLOTS : SLOTS + 1, :])


def outer_kernel(base_ref, own_ref, other_ref, chunk_ref):
    def both(rows):
        return jnp.concatenate([own_ref[rows, :], other_ref[rows, :]], axis=1)

    exc = both(slice(2 * W, 3 * W))
    e_hi, e_lo = split(jnp.concatenate([exc, jnp.zeros((64, 2 * PT), F32)], axis=0))
    v_hi, v_lo = split(both(slice(0, 2 * W)))
    kind = both(slice(3 * W + 1, 3 * W + 2))
    for k in range(2):
        here = kind == (2 * base_ref[2] + k).astype(F32)
        k_hi = jnp.where(here, v_hi, jnp.zeros_like(v_hi))
        k_lo = jnp.where(here, v_lo, jnp.zeros_like(v_lo))
        out = dot_nt(k_hi, e_hi) + dot_nt(k_lo, e_hi) + dot_nt(k_hi, e_lo)
        for which in range(2):
            for h in range(2):
                block = out[which * W + h * HALF : which * W + (h + 1) * HALF, :]
                at = which * 144
                chunk_ref[2 * k + h, at : at + 96, :] = block[:, 0:PT]
                chunk_ref[2 * k + h, at + 96 : at + 144, :] = block[0:48, PT:] + pltpu.roll(
                    block[48:96, PT:], 64, 1
                )
    gram = own_ref[3 * W :, :] + other_ref[3 * W :, :]
    for g in range(4):
        chunk_ref[g, 288:296, :] = gram


def spread_kernel(in_ref, out_ref):
    total = in_ref[0]
    for i in range(1, 4):
        total = total + in_ref[i]
    out_ref[...] = jnp.zeros_like(out_ref)
    for which in range(2):
        for j in range(3):
            at = which * 144 + j * 48
            out_ref[pl.ds(3 * which + j, 48, 8), :] = total[at : at + 48, :]
    out_ref[pl.ds(6, 64, 8), :] = jnp.broadcast_to(total[288:289, :], (64, PT))


def combine_kernel(in_ref, vec_ref, out_ref, adj_ref):
    total = jnp.sum(in_ref[...].reshape(64, 8, PT), axis=0)
    lane = lanes(1)

    def entry(i):
        return jnp.sum(jnp.where(lane == i, total[6:7, :], 0.0), axis=1, keepdims=True)

    g00, g01, g11, g02, g12, g22 = [entry(i) for i in range(6)]
    alpha = g01 / g00
    beta = jnp.sqrt(g00)
    p2 = g11 - alpha * g01
    pn = jnp.sqrt(p2)
    h00 = 1.0 - alpha
    h10 = pn / beta
    h01 = (g02 - alpha * g01) / (beta * pn)
    qv1 = (g12 - alpha * g11 - alpha * g02 + alpha * alpha * g01) / p2
    h11 = 1.0 - qv1
    n00 = h00 * h00 + h10 * h10
    n01 = h00 * h01 + h10 * h11
    n11 = 1.0 - 2.0 * qv1 + (g22 - 2.0 * alpha * g12 + alpha * alpha * g11) / p2
    r0 = beta * h00
    r1 = beta * h01
    f00 = jnp.sqrt(n00)
    f10 = n01 / f00
    f11 = jnp.sqrt(n11 - f10 * f10)
    y0 = r0 / f00
    y1 = (r1 - f10 * y0) / f11
    w1 = y1 / f11
    w0 = (y0 - f10 * w1) / f00
    c1 = -w1 / pn
    c0 = w0 / beta - c1 * alpha
    mixed = c0 * total[0:3, :] + c1 * total[3:6, :]
    mixed = jnp.concatenate([mixed, jnp.zeros((1, PT), F32)] * 2, axis=0)
    for i in range(32):
        out_ref[8 * i : 8 * i + 8, :] = mixed
    adj_ref[...] = c0 * vec_ref[0:W, :] + c1 * vec_ref[W : 2 * W, :]


def copies_kernel(in_ref, out_ref):
    for j in range(3):
        rows = in_ref[pl.ds(j, 48, 4), :]
        for i in range(4):
            out_ref[i, 48 * j : 48 * (j + 1), :] = rows


def expand_kernel(base_ref, own_ref, other_ref, out_ref):
    core = base_ref[2]
    for ref, first in ((own_ref, 2 * core), (other_ref, 2 - 2 * core)):
        for k in range(2):
            for h in range(2):
                block = ref[2 * k + h]
                at = h * HALF
                edge = block[96:144, :]
                out_ref[first + k, at : at + HALF, 0:PT] = block[0:HALF, :]
                out_ref[first + k, at : at + 48, PT:W] = edge[:, 0:64]
                out_ref[first + k, at + 48 : at + HALF, PT:W] = pltpu.roll(edge, 64, 1)[:, 0:64]


def call(kernel, shapes, *args, smem=0, mib=6, dtype=F32, fetched=False, us=1, **kw):
    if fetched:
        kw["scratch_shapes"] = [pltpu.VMEM(a.shape, a.dtype) for a in args]
        kw["scratch_shapes"].append(pltpu.SemaphoreType.DMA((len(args),)))
    return pl.pallas_call(
        kernel,
        out_shape=[jax.ShapeDtypeStruct(s, dtype) for s in shapes],
        in_specs=[pl.BlockSpec(memory_space=pltpu.SMEM)] * smem
        + [pl.BlockSpec(memory_space=pltpu.HBM if fetched else pltpu.VMEM)] * (len(args) - smem),
        cost_estimate=pl.CostEstimate(
            flops=us * 10**9, bytes_accessed=us * 3 * 10**6, transcendentals=0
        ),
        compiler_params=pltpu.CompilerParams(vmem_limit_bytes=mib * MIB),
        **kw,
    )(*args)


def shifted(block, axis, step):
    n = lax.axis_size(axis)
    return lax.ppermute(block, axis, [(i, i + step) for i in range(n) if 0 <= i + step < n])


def body(
    forward_coeff,
    incident,
    cost_grad,
    tmat_real,
    tmat_imag,
    translation_real,
    translation_imaginary,
    neighbours,
    particle_type,
):
    n_short = lax.axis_size("gy")
    tile = lax.axis_index("gx") * n_short + lax.axis_index("gy")
    core = lax.axis_index("gy") % 2
    base = jnp.stack([tile * PT, jnp.int32(n_short * PT), core]).astype(jnp.int32)

    kinds = particle_type.reshape(1, PT)
    to_up, to_dn = call(
        pack_wide_kernel,
        [(ROWS + HALF, PT)] * 2,
        forward_coeff,
        cost_grad,
        neighbours,
        kinds,
        mib=60,
        us=4,
        fetched=True,
    )
    up = shifted(to_up, "gx", 1)
    dn = shifted(to_dn, "gx", -1)
    to_lo, to_hi = call(
        pack_short_kernel, [(ROWS, PT)] * 2, forward_coeff, cost_grad, neighbours, kinds, up, dn
    )
    lf = shifted(to_hi, "gy", 1)
    rt = shifted(to_lo, "gy", -1)

    tw, lw, fw = call(
        weight_kernel,
        [(2 * W, KINDS * W), (2 * W, 2 * PART), (2 * W, 2 * PART)],
        tmat_real,
        tmat_imag,
        translation_real,
        translation_imaginary,
        mib=16,
        dtype=BF16,
    )

    (vectors,) = call(
        main_kernel,
        [(3 * W + 8, PT)],
        base,
        cost_grad,
        neighbours,
        kinds,
        up,
        dn,
        lf,
        rt,
        forward_coeff,
        incident,
        tw,
        lw,
        fw,
        smem=1,
        mib=24,
        scratch_shapes=[pltpu.VMEM((2 * PART, 3 * PT), BF16)] * 2,
    )
    pairs = [(i, i ^ 1) for i in range(n_short)]
    lines = [list(range(c, n_short, 2)) for c in range(2)]
    partner = lax.ppermute(vectors, "gy", pairs)
    (chunks,) = call(outer_kernel, [(4, CHUNK, PT)], base, vectors, partner, smem=1)
    got = lax.all_to_all(chunks, "gy", 0, 0, axis_index_groups=lines)
    (pieces,) = call(spread_kernel, [(512, PT)], got)
    got = lax.all_to_all(pieces.reshape(64, 8, PT), "gx", 0, 0)
    mixed, adjoint = call(combine_kernel, [(256, PT), (W, PT)], got.reshape(512, PT), vectors)
    got = lax.all_to_all(mixed.reshape(64, 4, PT), "gx", 0, 0)
    (copies,) = call(copies_kernel, [(4, 144, PT)], got.reshape(256, PT))
    half = lax.all_to_all(copies, "gy", 0, 0, axis_index_groups=lines)
    other = lax.ppermute(half, "gy", pairs)
    (sensitivity,) = call(expand_kernel, [(KINDS, W, W)], base, half, other, smem=1)
    return (adjoint, sensitivity)


def solution(mesh):
    placed = (
        P(None, ("gx", "gy")),
        P(None, ("gx", "gy")),
        P(None, ("gx", "gy")),
        P(),
        P(),
        P(),
        P(),
        P(None, ("gx", "gy")),
        P(("gx", "gy")),
    )
    return jax.shard_map(
        body, mesh=mesh, in_specs=placed, out_specs=(P(None, ("gx", "gy")), P()), check_vma=False
    )
```

```python
import functools

import jax
import jax.numpy as jnp
from jax import lax
from jax.experimental import pallas as pl
from jax.experimental.pallas import tpu as pltpu
from jax.sharding import PartitionSpec as P

F32 = jnp.float32
BF16 = jnp.bfloat16
W = 192
HALF = 96
PT = 128
SLOTS = 10
KINDS = 4
META = 16
ROWS = W + META
CHUNK = 296
PART = 1024
MIB = 1024 * 1024


def split(x):
    hi = x.astype(BF16)
    return hi, (x - hi.astype(F32)).astype(BF16)


def dot(a, b):
    return lax.dot_general(a, b, (((1,), (0,)), ((), ())), preferred_element_type=F32)


def dot_nt(a, b):
    return lax.dot_general(a, b, (((1,), (1,)), ((), ())), preferred_element_type=F32)


def lanes(rows):
    return lax.broadcasted_iota(jnp.int32, (rows, PT), 1)


def fetch(sources, targets, sems):
    copies = [
        pltpu.make_async_copy(src, dst, sems.at[i])
        for i, (src, dst) in enumerate(zip(sources, targets))
    ]
    for copy in copies:
        copy.start()
    for copy in copies:
        copy.wait()


def meta_rows(nb_ref, pt_ref):
    return jnp.concatenate(
        [
            (nb_ref[...] + 1).astype(F32),
            pt_ref[...].astype(F32),
            jnp.zeros((META - SLOTS - 1, PT), F32),
        ],
        axis=0,
    )


def pack_wide_kernel(*refs):
    up_ref, dn_ref = refs[4:6]
    fc_ref, b_ref, nb_ref, pt_ref = refs[6:10]
    fetch(refs[0:4], refs[6:10], refs[10])
    meta = meta_rows(nb_ref, pt_ref)
    top, low = fc_ref[0:HALF, :], fc_ref[HALF:W, :]
    first = lanes(HALF) < 64
    for ref in (up_ref, dn_ref):
        ref[0:W, :] = b_ref[...]
        ref[W:ROWS, :] = meta
    up_ref[ROWS : ROWS + HALF, :] = jnp.where(first, pltpu.roll(top, 64, 1), low)
    dn_ref[ROWS : ROWS + HALF, :] = jnp.where(first, top, pltpu.roll(low, 64, 1))


def unpack_fc(up, dn):
    first = lanes(HALF) < 64
    return jnp.concatenate(
        [
            jnp.where(first, dn, pltpu.roll(up, 64, 1)),
            jnp.where(first, pltpu.roll(dn, 64, 1), up),
        ],
        axis=0,
    )


def pack_short_kernel(fc_ref, b_ref, nb_ref, pt_ref, up_ref, dn_ref, lo_ref, hi_ref):
    first = lanes(META) < 64
    meta = meta_rows(nb_ref, pt_ref)
    fc_ud = unpack_fc(up_ref[ROWS : ROWS + HALF, :], dn_ref[ROWS : ROWS + HALF, :])

    def part(rows, tiles):
        col = lanes(rows.stop - rows.start) % 32
        up, own, dn, edge, edge_ud = tiles

        def moved(x, shift):
            return pltpu.roll(x, shift, 1) if shift else x

        low = moved(up, 0)
        low = jnp.where(col < 4, low, moved(own, 4))
        low = jnp.where(col < 8, low, moved(dn, 8))
        low = jnp.where(col < 12, low, moved(edge, 12))
        lo_ref[rows, :] = jnp.where(col < 14, low, moved(edge_ud, 14))
        high = moved(edge, 114)
        high = jnp.where(col < 18, high, moved(edge_ud, 116))
        high = jnp.where(col < 20, high, moved(up, 120))
        high = jnp.where(col < 24, high, moved(own, 124))
        hi_ref[rows, :] = jnp.where(col < 28, high, dn)

    part(slice(0, W), (up_ref[0:W, :], b_ref[...], dn_ref[0:W, :], fc_ref[...], fc_ud))
    m = slice(W, ROWS)
    meta_ud = jnp.where(first, dn_ref[m, :], up_ref[m, :])
    part(m, (up_ref[m, :], meta, dn_ref[m, :], meta, meta_ud))


def weight_kernel(tr_ref, ti_ref, lr_ref, li_ref, tw_ref, lw_ref, fw_ref):
    def turned(ref):
        n = ref.shape[0]
        fill = -n * HALF % PT
        side = jnp.concatenate([ref[...].reshape(n * HALF, HALF), jnp.zeros((n * HALF, 32), F32)], axis=1)
        if fill:
            side = jnp.concatenate([side, jnp.zeros((fill, PT), F32)], axis=0)
        return split(jnp.transpose(side)[0:HALF, :])

    def beside(ref):
        n = ref.shape[0]
        return split(
            jnp.concatenate([ref[s] for s in range(n)] + [jnp.zeros((HALF, -n * HALF % PT), F32)], axis=1)
        )

    def store(ref, real, imag, sign):
        width = real[0].shape[1]
        for at, re, im in zip((0, W), real, imag):
            ref[at : at + HALF, 0:width] = re
            ref[at : at + HALF, width:] = im if sign > 0 else -im
            ref[at + HALF : at + W, 0:width] = -im if sign > 0 else im
            ref[at + HALF : at + W, width:] = re

    store(tw_ref, turned(tr_ref), turned(ti_ref), 1)
    store(lw_ref, turned(lr_ref), turned(li_ref), 1)
    store(fw_ref, beside(lr_ref), beside(li_ref), -1)


def target_ids(base, row_stride):
    spot = lax.broadcasted_iota(jnp.int32, (4 * PT, PT), 0)
    lane = spot % PT
    row, col = lane // 32, lane % 32
    shift = jnp.where(row < 2, row_stride, -row_stride)
    own = base + lane
    beside = base + row * 32
    lr = jnp.where(
        col < 14,
        beside + PT + col - 12,
        jnp.where(
            col < 16,
            beside + PT + shift + col - 14,
            jnp.where(col < 18, beside - PT + col + 14, beside - PT + shift + col + 12),
        ),
    )
    lr = jnp.where((col >= 12) & (col < 20), lr, -10)
    edge = jnp.where(
        (col < 2) | (col >= 30),
        own,
        jnp.where(col < 4, own - 2 + shift, jnp.where(col >= 28, own + 2 + shift, lr)),
    )
    ids = jnp.where(
        spot < PT,
        own,
        jnp.where(spot < 2 * PT, own + shift, jnp.where(spot < 3 * PT, lr, edge)),
    )
    return jnp.where(ids >= 0, ids + 1, -10).astype(F32)


def product(w_ref, hi, lo):
    rows = dot(w_ref[...], hi)
    return rows[0:W] + rows[W : 2 * W] + dot(w_ref[0:W, :], lo)


def scaled_by_type(tw_ref, blocks, metas):
    his, los = [], []
    for v, meta in zip(blocks, metas):
        hi, lo = split(v)
        kind = meta[SLOTS : SLOTS + 1, :]
        his.append([jnp.where(kind == float(k), hi, jnp.zeros_like(hi)) for k in range(KINDS)])
        los.append([jnp.where(kind == float(k), lo, jnp.zeros_like(lo)) for k in range(KINDS)])

    def by_part(pieces):
        whole = [jnp.concatenate([p[k] for p in pieces], axis=1) for k in range(KINDS)]
        return jnp.concatenate([w[0:HALF] for w in whole] + [w[HALF:W] for w in whole], axis=0)

    s_hi, s_lo = split(product(tw_ref, by_part(his), by_part(los)))
    return jnp.concatenate([s_hi, s_lo], axis=0)


def one_hot(at, meta, s):
    return jnp.where(at == meta[s : s + 1, :], 1.0, 0.0).astype(BF16)


def place(refs, parts, s, lanes_at, lanes_from):
    for ref, part in zip(refs, parts):
        for half in range(2):
            at = half * PART + s * HALF
            ref[at : at + HALF, lanes_at] = part[half * HALF : (half + 1) * HALF, lanes_from]


def clear_fill(refs):
    for ref in refs:
        for at in (SLOTS * HALF, PART + SLOTS * HALF):
            rows = PART - SLOTS * HALF
            ref[at : at + rows, :] = jnp.zeros((rows, ref.shape[1]), BF16)


def scatter_pairs(refs, stack, ids, metas, lanes_at):
    for s in range(0, SLOTS, 2):
        pick = jnp.concatenate(
            [
                jnp.concatenate([one_hot(ids, meta, t) for meta in metas], axis=1)
                for t in (s, s + 1)
            ],
            axis=0,
        )
        g = dot_nt(stack, pick)
        parts = split(g[0:W] + g[W : 2 * W])
        for t in (0, 1):
            place(refs, parts, s + t, lanes_at, slice(t * PT, (t + 1) * PT))


def gather_pairs(refs, blocks, ids, meta, lanes_at):
    stack = jnp.concatenate(split(jnp.concatenate(blocks, axis=1)), axis=0)
    for s in range(0, SLOTS, 2):
        pick = jnp.concatenate([one_hot(ids, meta, s), one_hot(ids, meta, s + 1)], axis=1)
        g = dot(stack, pick).astype(BF16)
        for t in (0, 1):
            place(
                refs, (g[0:W], g[W : 2 * W]), s + t, lanes_at, slice(t * PT, (t + 1) * PT)
            )


def early_kernel(
    stride,
    tile_ref,
    b_ref,
    nb_ref,
    pt_ref,
    up_ref,
    dn_ref,
    fc_ref,
    inc_ref,
    tw_ref,
    lw_ref,
    fw_ref,
    part_ref,
    exc_ref,
    ghi_ref,
    glo_ref,
):
    m = slice(W, ROWS)
    refs = (ghi_ref, glo_ref)
    ids = target_ids(tile_ref[0] * PT, stride)
    own = meta_rows(nb_ref, pt_ref)
    metas = (own, up_ref[m, :], dn_ref[m, :])
    clear_fill(refs)
    stack = scaled_by_type(tw_ref, (b_ref[...], up_ref[0:W, :], dn_ref[0:W, :]), metas)
    for s in range(SLOTS):
        pick = jnp.concatenate([one_hot(ids[0 : 3 * PT, :], meta, s) for meta in metas], axis=1)
        g = dot_nt(stack, pick)
        place(refs, split(g[0:W] + g[W : 2 * W]), s, slice(0, 3 * PT), slice(0, 3 * PT))
    part_ref[...] = product(lw_ref, ghi_ref[...], glo_ref[...])

    fc_ud = unpack_fc(up_ref[ROWS : ROWS + HALF, :], dn_ref[ROWS : ROWS + HALF, :])
    block = slice(0, PT)
    gather_pairs(refs, (fc_ref[...], fc_ud), ids[0 : 2 * PT, :], own, block)
    exc_ref[...] = inc_ref[...] + product(fw_ref, ghi_ref[:, block], glo_ref[:, block])


def main_kernel(
    stride,
    tile_ref,
    b_ref,
    nb_ref,
    pt_ref,
    up_ref,
    dn_ref,
    lf_ref,
    rt_ref,
    part_ref,
    exc_ref,
    tw_ref,
    lw_ref,
    fw_ref,
    vec_ref,
    ghi_ref,
    glo_ref,
):
    m = slice(W, ROWS)
    refs = (ghi_ref, glo_ref)
    ids = target_ids(tile_ref[0] * PT, stride)
    col = lanes(META) % 32
    b = b_ref[...]
    m_own = meta_rows(nb_ref, pt_ref)
    m_ud = jnp.where(lanes(META) < 64, dn_ref[m, :], up_ref[m, :])
    m_lr = jnp.where(col >= 16, lf_ref[m, :], rt_ref[m, :])
    wide = lanes(W) % 32
    x_lr = jnp.where(wide >= 16, lf_ref[0:W, :], rt_ref[0:W, :])
    b_zone = (col < 12) | (col >= 20)
    row_id = lax.broadcasted_iota(jnp.int32, (META, PT), 0)
    m_b = jnp.where(b_zone | (row_id >= SLOTS), m_lr, 0.0)
    m_f = jnp.where(b_zone & (row_id < SLOTS), 0.0, m_lr)
    clear_fill(refs)
    first, second = slice(0, PT), slice(PT, 2 * PT)

    stack = scaled_by_type(tw_ref, (x_lr,), (m_b,))
    scatter_pairs(refs, stack, ids[3 * PT :, :], (m_b,), first)
    edge = product(lw_ref, ghi_ref[:, first], glo_ref[:, first])
    gather_pairs(refs, (x_lr,), ids[2 * PT : 3 * PT, :], m_own, second)
    exc = exc_ref[...] + product(fw_ref, ghi_ref[:, second], glo_ref[:, second])
    left, right = wide < 2, wide >= 30
    u1 = part_ref[:, 0:PT] + jnp.where(left | right, edge, 0.0)
    u1_ud = part_ref[:, PT : 2 * PT] + jnp.where(
        left, pltpu.roll(edge, PT - 2, 1), jnp.where(right, pltpu.roll(edge, 2, 1), 0.0)
    )
    u1_lr = part_ref[:, 2 * PT :] + jnp.where((wide >= 12) & (wide < 20), edge, 0.0)
    vec_ref[0:W, :] = b
    vec_ref[W : 2 * W, :] = u1
    vec_ref[2 * W : 3 * W, :] = exc

    metas = (m_own, m_ud, m_f)
    stack = scaled_by_type(tw_ref, (u1, u1_ud, u1_lr), metas)
    scatter_pairs(refs, stack, ids[0:PT, :], metas, first)
    u2 = product(lw_ref, ghi_ref[:, first], glo_ref[:, first])

    lane, row = lanes(8), lax.broadcasted_iota(jnp.int32, (8, PT), 0)
    gram = jnp.zeros((8, PT), F32)
    for i, (p, q) in enumerate(((b, b), (b, u1), (u1, u1), (b, u2), (u1, u2), (u2, u2))):
        gram = jnp.where(lane == i, jnp.sum(p * q), gram)
    vec_ref[3 * W :, :] = jnp.where(row == 0, gram, m_own[SLOTS : SLOTS + 1, :])


def outer_kernel(tile_ref, own_ref, other_ref, chunk_ref):
    def both(rows):
        return jnp.concatenate([own_ref[rows, :], other_ref[rows, :]], axis=1)

    exc = both(slice(2 * W, 3 * W))
    e_hi, e_lo = split(jnp.concatenate([exc, jnp.zeros((64, 2 * PT), F32)], axis=0))
    v_hi, v_lo = split(both(slice(0, 2 * W)))
    kind = both(slice(3 * W + 1, 3 * W + 2))
    for k in range(2):
        here = kind == (2 * lax.rem(tile_ref[0], 2) + k).astype(F32)
        k_hi = jnp.where(here, v_hi, jnp.zeros_like(v_hi))
        k_lo = jnp.where(here, v_lo, jnp.zeros_like(v_lo))
        out = dot_nt(k_hi, e_hi) + dot_nt(k_lo, e_hi) + dot_nt(k_hi, e_lo)
        for which in range(2):
            for h in range(2):
                block = out[which * W + h * HALF : which * W + (h + 1) * HALF, :]
                at = which * 144
                chunk_ref[2 * k + h, at : at + 96, :] = block[:, 0:PT]
                chunk_ref[2 * k + h, at + 96 : at + 144, :] = block[0:48, PT:] + pltpu.roll(
                    block[48:96, PT:], 64, 1
                )
    gram = own_ref[3 * W :, :] + other_ref[3 * W :, :]
    for g in range(4):
        chunk_ref[g, 288:296, :] = gram


def spread_kernel(in_ref, out_ref):
    total = in_ref[0]
    for i in range(1, 4):
        total = total + in_ref[i]
    out_ref[...] = jnp.zeros_like(out_ref)
    for which in range(2):
        for j in range(3):
            at = which * 144 + j * 48
            out_ref[pl.ds(3 * which + j, 48, 8), :] = total[at : at + 48, :]
    out_ref[pl.ds(6, 64, 8), :] = jnp.broadcast_to(total[288:289, :], (64, PT))


def combine_kernel(in_ref, vec_ref, out_ref, adj_ref):
    total = jnp.sum(in_ref[...].reshape(64, 8, PT), axis=0)
    lane = lanes(1)

    def entry(i):
        return jnp.sum(jnp.where(lane == i, total[6:7, :], 0.0), axis=1, keepdims=True)

    g00, g01, g11, g02, g12, g22 = [entry(i) for i in range(6)]
    alpha = g01 / g00
    beta = jnp.sqrt(g00)
    p2 = g11 - alpha * g01
    pn = jnp.sqrt(p2)
    h00 = 1.0 - alpha
    h10 = pn / beta
    h01 = (g02 - alpha * g01) / (beta * pn)
    qv1 = (g12 - alpha * g11 - alpha * g02 + alpha * alpha * g01) / p2
    h11 = 1.0 - qv1
    n00 = h00 * h00 + h10 * h10
    n01 = h00 * h01 + h10 * h11
    n11 = 1.0 - 2.0 * qv1 + (g22 - 2.0 * alpha * g12 + alpha * alpha * g11) / p2
    r0 = beta * h00
    r1 = beta * h01
    f00 = jnp.sqrt(n00)
    f10 = n01 / f00
    f11 = jnp.sqrt(n11 - f10 * f10)
    y0 = r0 / f00
    y1 = (r1 - f10 * y0) / f11
    w1 = y1 / f11
    w0 = (y0 - f10 * w1) / f00
    c1 = -w1 / pn
    c0 = w0 / beta - c1 * alpha
    mixed = c0 * total[0:3, :] + c1 * total[3:6, :]
    mixed = jnp.concatenate([mixed, jnp.zeros((1, PT), F32)] * 2, axis=0)
    for i in range(32):
        out_ref[8 * i : 8 * i + 8, :] = mixed
    adj_ref[...] = c0 * vec_ref[0:W, :] + c1 * vec_ref[W : 2 * W, :]


def copies_kernel(in_ref, out_ref):
    for j in range(3):
        rows = in_ref[pl.ds(j, 48, 4), :]
        for i in range(4):
            out_ref[i, 48 * j : 48 * (j + 1), :] = rows


def expand_kernel(tile_ref, own_ref, other_ref, out_ref):
    core = lax.rem(tile_ref[0], 2)
    for ref, first in ((own_ref, 2 * core), (other_ref, 2 - 2 * core)):
        for k in range(2):
            for h in range(2):
                block = ref[2 * k + h]
                at = h * HALF
                edge = block[96:144, :]
                out_ref[first + k, at : at + HALF, 0:PT] = block[0:HALF, :]
                out_ref[first + k, at : at + 48, PT:W] = edge[:, 0:64]
                out_ref[first + k, at + 48 : at + HALF, PT:W] = pltpu.roll(edge, 64, 1)[:, 0:64]


def call(kernel, shapes, *args, smem=0, mib=6, dtype=F32, fetched=False, us=1, **kw):
    if fetched:
        kw["scratch_shapes"] = [pltpu.VMEM(a.shape, a.dtype) for a in args]
        kw["scratch_shapes"].append(pltpu.SemaphoreType.DMA((len(args),)))
    return pl.pallas_call(
        kernel,
        out_shape=[jax.ShapeDtypeStruct(s, dtype) for s in shapes],
        in_specs=[pl.BlockSpec(memory_space=pltpu.SMEM)] * smem
        + [pl.BlockSpec(memory_space=pltpu.HBM if fetched else pltpu.VMEM)] * (len(args) - smem),
        cost_estimate=pl.CostEstimate(
            flops=us * 10**9, bytes_accessed=us * 3 * 10**6, transcendentals=0
        ),
        compiler_params=pltpu.CompilerParams(vmem_limit_bytes=mib * MIB),
        **kw,
    )(*args)


def shifted(block, axis, step):
    n = lax.axis_size(axis)
    return lax.ppermute(block, axis, [(i, i + step) for i in range(n) if 0 <= i + step < n])


def body(
    forward_coeff,
    incident,
    cost_grad,
    tmat_real,
    tmat_imag,
    translation_real,
    translation_imaginary,
    neighbours,
    particle_type,
):
    n_short = lax.axis_size("gy")
    tile = lax.axis_index("gx") * n_short + lax.axis_index("gy")
    tile = tile.astype(jnp.int32).reshape(1)
    stride = n_short * PT
    kinds = particle_type.reshape(1, PT)
    to_up, to_dn = call(
        pack_wide_kernel,
        [(ROWS + HALF, PT)] * 2,
        forward_coeff,
        cost_grad,
        neighbours,
        kinds,
        mib=60,
        us=4,
        fetched=True,
    )
    up = shifted(to_up, "gx", 1)
    dn = shifted(to_dn, "gx", -1)
    to_lo, to_hi = call(
        pack_short_kernel, [(ROWS, PT)] * 2, forward_coeff, cost_grad, neighbours, kinds, up, dn
    )
    lf = shifted(to_hi, "gy", 1)
    rt = shifted(to_lo, "gy", -1)

    tw, lw, fw = call(
        weight_kernel,
        [(2 * W, KINDS * W), (2 * W, 2 * PART), (2 * W, 2 * PART)],
        tmat_real,
        tmat_imag,
        translation_real,
        translation_imaginary,
        mib=16,
        dtype=BF16,
    )

    scratch = pltpu.VMEM((2 * PART, 3 * PT), BF16)
    part, exc = call(
        functools.partial(early_kernel, stride),
        [(W, 3 * PT), (W, PT)],
        tile,
        cost_grad,
        neighbours,
        kinds,
        up,
        dn,
        forward_coeff,
        incident,
        tw,
        lw,
        fw,
        smem=1,
        mib=24,
        us=4,
        scratch_shapes=[scratch] * 2,
    )
    scratch = pltpu.VMEM((2 * PART, 2 * PT), BF16)
    (vectors,) = call(
        functools.partial(main_kernel, stride),
        [(3 * W + 8, PT)],
        tile,
        cost_grad,
        neighbours,
        kinds,
        up,
        dn,
        lf,
        rt,
        part,
        exc,
        tw,
        lw,
        fw,
        smem=1,
        mib=24,
        us=4,
        scratch_shapes=[scratch] * 2,
    )
    pairs = [(i, i ^ 1) for i in range(n_short)]
    lines = [list(range(c, n_short, 2)) for c in range(2)]
    partner = lax.ppermute(vectors, "gy", pairs)
    (chunks,) = call(outer_kernel, [(4, CHUNK, PT)], tile, vectors, partner, smem=1)
    got = lax.all_to_all(chunks, "gy", 0, 0, axis_index_groups=lines)
    (pieces,) = call(spread_kernel, [(512, PT)], got)
    got = lax.all_to_all(pieces.reshape(64, 8, PT), "gx", 0, 0)
    mixed, adjoint = call(combine_kernel, [(256, PT), (W, PT)], got.reshape(512, PT), vectors)
    got = lax.all_to_all(mixed.reshape(64, 4, PT), "gx", 0, 0)
    (copies,) = call(copies_kernel, [(4, 144, PT)], got.reshape(256, PT))
    half = lax.all_to_all(copies, "gy", 0, 0, axis_index_groups=lines)
    other = lax.ppermute(half, "gy", pairs)
    (sensitivity,) = call(expand_kernel, [(KINDS, W, W)], tile, half, other, smem=1)
    return (adjoint, sensitivity)


def solution(mesh):
    placed = (
        P(None, ("gx", "gy")),
        P(None, ("gx", "gy")),
        P(None, ("gx", "gy")),
        P(),
        P(),
        P(),
        P(),
        P(None, ("gx", "gy")),
        P(("gx", "gy")),
    )
    return jax.shard_map(
        body, mesh=mesh, in_specs=placed, out_specs=(P(None, ("gx", "gy")), P()), check_vma=False
    )
```

```python
import functools

import jax
import jax.numpy as jnp
from jax import lax
from jax.experimental import pallas as pl
from jax.experimental.pallas import tpu as pltpu
from jax.sharding import PartitionSpec as P

F32 = jnp.float32
BF16 = jnp.bfloat16
W = 192
HALF = 96
PT = 128
SLOTS = 10
KINDS = 4
META = 16
ROWS = W + META
CHUNK = 296
PART = 1024
MIB = 1024 * 1024


def split(x):
    hi = x.astype(BF16)
    return hi, (x - hi.astype(F32)).astype(BF16)


def dot(a, b):
    return lax.dot_general(a, b, (((1,), (0,)), ((), ())), preferred_element_type=F32)


def dot_nt(a, b):
    return lax.dot_general(a, b, (((1,), (1,)), ((), ())), preferred_element_type=F32)


def lanes(rows):
    return lax.broadcasted_iota(jnp.int32, (rows, PT), 1)


def fetch(sources, targets, sems):
    copies = [
        pltpu.make_async_copy(src, dst, sems.at[i])
        for i, (src, dst) in enumerate(zip(sources, targets))
    ]
    for copy in copies:
        copy.start()
    for copy in copies:
        copy.wait()


def meta_rows(nb_ref, pt_ref):
    return jnp.concatenate(
        [
            (nb_ref[...] + 1).astype(F32),
            pt_ref[...].astype(F32),
            jnp.zeros((META - SLOTS - 1, PT), F32),
        ],
        axis=0,
    )


def even_row(short, tile_ref):
    return lax.rem(lax.div(tile_ref[0], short), 2) == 0


def even_col(tile_ref):
    return lax.rem(tile_ref[0], 2) == 0


def pack_wide_kernel(short, *refs):
    even = even_row(short, refs[0])
    one_ref, two_ref = refs[5:7]
    fc_ref, b_ref, nb_ref, pt_ref = refs[7:11]
    fetch(refs[1:5], refs[7:11], refs[11])
    meta = meta_rows(nb_ref, pt_ref)
    top, low = fc_ref[0:HALF, :], fc_ref[HALF:W, :]
    first = lanes(HALF) < 64
    for ref in (one_ref, two_ref):
        ref[0:W, :] = b_ref[...]
        ref[W:ROWS, :] = meta
    up = jnp.where(first, pltpu.roll(top, 64, 1), low)
    dn = jnp.where(first, top, pltpu.roll(low, 64, 1))
    one_ref[ROWS : ROWS + HALF, :] = jnp.where(even, up, dn)
    two_ref[ROWS : ROWS + HALF, :] = jnp.where(even, dn, up)


def unpack_fc(up, dn):
    first = lanes(HALF) < 64
    return jnp.concatenate(
        [
            jnp.where(first, dn, pltpu.roll(up, 64, 1)),
            jnp.where(first, pltpu.roll(dn, 64, 1), up),
        ],
        axis=0,
    )


class Tiles:
    def __init__(self, even, one_ref, two_ref):
        self.even, self.one, self.two = even, one_ref, two_ref

    def below(self, rows):
        return jnp.where(self.even, self.two[rows, :], self.one[rows, :])

    def above(self, rows):
        return jnp.where(self.even, self.one[rows, :], self.two[rows, :])


def pack_short_kernel(
    short, tile_ref, fc_ref, b_ref, nb_ref, pt_ref, x1_ref, x2_ref, one_ref, two_ref
):
    wide = Tiles(even_row(short, tile_ref), x1_ref, x2_ref)
    even = even_col(tile_ref)
    half = slice(ROWS, ROWS + HALF)
    first = lanes(META) < 64
    meta = meta_rows(nb_ref, pt_ref)
    fc_ud = unpack_fc(wide.below(half), wide.above(half))

    def part(rows, tiles):
        col = lanes(rows.stop - rows.start) % 32
        up, own, dn, edge, edge_ud = tiles

        def moved(x, shift):
            return pltpu.roll(x, shift, 1) if shift else x

        low = moved(up, 0)
        low = jnp.where(col < 4, low, moved(own, 4))
        low = jnp.where(col < 8, low, moved(dn, 8))
        low = jnp.where(col < 12, low, moved(edge, 12))
        low = jnp.where(col < 14, low, moved(edge_ud, 14))
        high = moved(edge, 114)
        high = jnp.where(col < 18, high, moved(edge_ud, 116))
        high = jnp.where(col < 20, high, moved(up, 120))
        high = jnp.where(col < 24, high, moved(own, 124))
        high = jnp.where(col < 28, high, dn)
        one_ref[rows, :] = jnp.where(even, high, low)
        two_ref[rows, :] = jnp.where(even, low, high)

    v, m = slice(0, W), slice(W, ROWS)
    part(v, (wide.below(v), b_ref[...], wide.above(v), fc_ref[...], fc_ud))
    meta_up, meta_dn = wide.below(m), wide.above(m)
    part(m, (meta_up, meta, meta_dn, meta, jnp.where(first, meta_dn, meta_up)))


def weight_kernel(tr_ref, ti_ref, lr_ref, li_ref, tw_ref, lw_ref, fw_ref):
    def turned(ref):
        n = ref.shape[0]
        fill = -n * HALF % PT
        side = jnp.concatenate([ref[...].reshape(n * HALF, HALF), jnp.zeros((n * HALF, 32), F32)], axis=1)
        if fill:
            side = jnp.concatenate([side, jnp.zeros((fill, PT), F32)], axis=0)
        return split(jnp.transpose(side)[0:HALF, :])

    def beside(ref):
        n = ref.shape[0]
        return split(
            jnp.concatenate([ref[s] for s in range(n)] + [jnp.zeros((HALF, -n * HALF % PT), F32)], axis=1)
        )

    def store(ref, real, imag, sign):
        width = real[0].shape[1]
        for at, re, im in zip((0, W), real, imag):
            ref[at : at + HALF, 0:width] = re
            ref[at : at + HALF, width:] = im if sign > 0 else -im
            ref[at + HALF : at + W, 0:width] = -im if sign > 0 else im
            ref[at + HALF : at + W, width:] = re

    store(tw_ref, turned(tr_ref), turned(ti_ref), 1)
    store(lw_ref, turned(lr_ref), turned(li_ref), 1)
    store(fw_ref, beside(lr_ref), beside(li_ref), -1)


def target_ids(base, row_stride):
    spot = lax.broadcasted_iota(jnp.int32, (4 * PT, PT), 0)
    lane = spot % PT
    row, col = lane // 32, lane % 32
    shift = jnp.where(row < 2, row_stride, -row_stride)
    own = base + lane
    beside = base + row * 32
    lr = jnp.where(
        col < 14,
        beside + PT + col - 12,
        jnp.where(
            col < 16,
            beside + PT + shift + col - 14,
            jnp.where(col < 18, beside - PT + col + 14, beside - PT + shift + col + 12),
        ),
    )
    lr = jnp.where((col >= 12) & (col < 20), lr, -10)
    edge = jnp.where(
        (col < 2) | (col >= 30),
        own,
        jnp.where(col < 4, own - 2 + shift, jnp.where(col >= 28, own + 2 + shift, lr)),
    )
    ids = jnp.where(
        spot < PT,
        own,
        jnp.where(spot < 2 * PT, own + shift, jnp.where(spot < 3 * PT, lr, edge)),
    )
    return jnp.where(ids >= 0, ids + 1, -10).astype(F32)


def product(w_ref, hi, lo):
    rows = dot(w_ref[...], hi)
    return rows[0:W] + rows[W : 2 * W] + dot(w_ref[0:W, :], lo)


def scaled_by_type(tw_ref, blocks, metas):
    his, los = [], []
    for v, meta in zip(blocks, metas):
        hi, lo = split(v)
        kind = meta[SLOTS : SLOTS + 1, :]
        his.append([jnp.where(kind == float(k), hi, jnp.zeros_like(hi)) for k in range(KINDS)])
        los.append([jnp.where(kind == float(k), lo, jnp.zeros_like(lo)) for k in range(KINDS)])

    def by_part(pieces):
        whole = [jnp.concatenate([p[k] for p in pieces], axis=1) for k in range(KINDS)]
        return jnp.concatenate([w[0:HALF] for w in whole] + [w[HALF:W] for w in whole], axis=0)

    s_hi, s_lo = split(product(tw_ref, by_part(his), by_part(los)))
    return jnp.concatenate([s_hi, s_lo], axis=0)


def one_hot(at, meta, s):
    return jnp.where(at == meta[s : s + 1, :], 1.0, 0.0).astype(BF16)


def place(refs, parts, s, lanes_at, lanes_from):
    for ref, part in zip(refs, parts):
        for half in range(2):
            at = half * PART + s * HALF
            ref[at : at + HALF, lanes_at] = part[half * HALF : (half + 1) * HALF, lanes_from]


def clear_fill(refs):
    for ref in refs:
        for at in (SLOTS * HALF, PART + SLOTS * HALF):
            rows = PART - SLOTS * HALF
            ref[at : at + rows, :] = jnp.zeros((rows, ref.shape[1]), BF16)


def scatter_pairs(refs, stack, ids, metas, lanes_at):
    for s in range(0, SLOTS, 2):
        pick = jnp.concatenate(
            [
                jnp.concatenate([one_hot(at, meta, t) for at, meta in zip(ids, metas)], axis=1)
                for t in (s, s + 1)
            ],
            axis=0,
        )
        g = dot_nt(stack, pick)
        parts = split(g[0:W] + g[W : 2 * W])
        for t in (0, 1):
            place(refs, parts, s + t, lanes_at, slice(t * PT, (t + 1) * PT))


def gather_pairs(refs, blocks, ids, meta, lanes_at):
    stack = jnp.concatenate(split(jnp.concatenate(blocks, axis=1)), axis=0)
    for s in range(0, SLOTS, 2):
        pick = jnp.concatenate([one_hot(ids, meta, s), one_hot(ids, meta, s + 1)], axis=1)
        g = dot(stack, pick).astype(BF16)
        for t in (0, 1):
            place(
                refs, (g[0:W], g[W : 2 * W]), s + t, lanes_at, slice(t * PT, (t + 1) * PT)
            )


def early_kernel(
    short,
    tile_ref,
    b_ref,
    nb_ref,
    pt_ref,
    x1_ref,
    x2_ref,
    fc_ref,
    tw_ref,
    lw_ref,
    part_ref,
    stack_ref,
    fhi_ref,
    flo_ref,
    ghi_ref,
    glo_ref,
):
    wide = Tiles(even_row(short, tile_ref), x1_ref, x2_ref)
    v, m, half = slice(0, W), slice(W, ROWS), slice(ROWS, ROWS + HALF)
    refs, gathered = (ghi_ref, glo_ref), (fhi_ref, flo_ref)
    ids = target_ids(tile_ref[0] * PT, short * PT)[0 : 2 * PT, :]
    own = meta_rows(nb_ref, pt_ref)
    metas = (own, wide.below(m), wide.above(m))
    clear_fill(refs + gathered)
    stack = scaled_by_type(tw_ref, (b_ref[...], wide.below(v), wide.above(v)), metas)
    stack_ref[...] = stack
    for s in range(SLOTS):
        pick = jnp.concatenate([one_hot(ids, meta, s) for meta in metas], axis=1)
        g = dot_nt(stack, pick)
        place(refs, split(g[0:W] + g[W : 2 * W]), s, slice(0, 2 * PT), slice(0, 2 * PT))
    part_ref[...] = product(lw_ref, ghi_ref[...], glo_ref[...])
    fc_ud = unpack_fc(wide.below(half), wide.above(half))
    gather_pairs(gathered, (fc_ref[...], fc_ud), ids, own, slice(0, PT))


def main_kernel(
    short,
    tile_ref,
    b_ref,
    nb_ref,
    pt_ref,
    inc_ref,
    x1_ref,
    x2_ref,
    y1_ref,
    y2_ref,
    part_ref,
    stack_ref,
    fhi_ref,
    flo_ref,
    tw_ref,
    lw_ref,
    fw_ref,
    vec_ref,
    ghi_ref,
    glo_ref,
):
    rows = Tiles(even_row(short, tile_ref), x1_ref, x2_ref)
    cols = Tiles(even_col(tile_ref), y1_ref, y2_ref)
    v, m = slice(0, W), slice(W, ROWS)
    refs = (ghi_ref, glo_ref)
    ids = target_ids(tile_ref[0] * PT, short * PT)
    col = lanes(META) % 32
    b = b_ref[...]
    m_own = meta_rows(nb_ref, pt_ref)
    m_up, m_dn = rows.below(m), rows.above(m)
    m_ud = jnp.where(lanes(META) < 64, m_dn, m_up)
    m_lr = jnp.where(col >= 16, cols.below(m), cols.above(m))
    spot = lanes(W) % 32
    x_lr = jnp.where(spot >= 16, cols.below(v), cols.above(v))
    b_zone = (col < 12) | (col >= 20)
    row_id = lax.broadcasted_iota(jnp.int32, (META, PT), 0)
    m_b = jnp.where(b_zone | (row_id >= SLOTS), m_lr, 0.0)
    m_f = jnp.where(b_zone & (row_id < SLOTS), 0.0, m_lr)
    clear_fill(refs)
    first, second = slice(0, PT), slice(PT, 2 * PT)
    own_ids, lr_ids, edge_ids = ids[0:PT, :], ids[2 * PT : 3 * PT, :], ids[3 * PT :, :]

    stack = jnp.concatenate([stack_ref[...], scaled_by_type(tw_ref, (x_lr,), (m_b,))], axis=1)
    scatter_pairs(
        refs, stack, (lr_ids, lr_ids, lr_ids, edge_ids), (m_own, m_up, m_dn, m_b), first
    )
    edge = product(lw_ref, ghi_ref[:, first], glo_ref[:, first])
    left, right = spot < 2, spot >= 30
    u1 = part_ref[:, first] + jnp.where(left | right, edge, 0.0)
    u1_ud = part_ref[:, second] + jnp.where(
        left, pltpu.roll(edge, PT - 2, 1), jnp.where(right, pltpu.roll(edge, 2, 1), 0.0)
    )
    u1_lr = jnp.where((spot >= 12) & (spot < 20), edge, 0.0)

    gather_pairs(refs, (x_lr,), lr_ids, m_own, second)
    exc = inc_ref[...] + product(
        fw_ref, ghi_ref[:, second] + fhi_ref[...], glo_ref[:, second] + flo_ref[...]
    )
    vec_ref[0:W, :] = b
    vec_ref[W : 2 * W, :] = u1
    vec_ref[2 * W : 3 * W, :] = exc

    metas = (m_own, m_ud, m_f)
    stack = scaled_by_type(tw_ref, (u1, u1_ud, u1_lr), metas)
    scatter_pairs(refs, stack, (own_ids,) * 3, metas, first)
    u2 = product(lw_ref, ghi_ref[:, first], glo_ref[:, first])

    lane, row = lanes(8), lax.broadcasted_iota(jnp.int32, (8, PT), 0)
    gram = jnp.zeros((8, PT), F32)
    for i, (p, q) in enumerate(((b, b), (b, u1), (u1, u1), (b, u2), (u1, u2), (u2, u2))):
        gram = jnp.where(lane == i, jnp.sum(p * q), gram)
    vec_ref[3 * W :, :] = jnp.where(row == 0, gram, m_own[SLOTS : SLOTS + 1, :])


def outer_kernel(tile_ref, own_ref, other_ref, chunk_ref):
    def both(rows):
        return jnp.concatenate([own_ref[rows, :], other_ref[rows, :]], axis=1)

    exc = both(slice(2 * W, 3 * W))
    e_hi, e_lo = split(jnp.concatenate([exc, jnp.zeros((64, 2 * PT), F32)], axis=0))
    v_hi, v_lo = split(both(slice(0, 2 * W)))
    kind = both(slice(3 * W + 1, 3 * W + 2))
    for k in range(2):
        here = kind == (2 * lax.rem(tile_ref[0], 2) + k).astype(F32)
        k_hi = jnp.where(here, v_hi, jnp.zeros_like(v_hi))
        k_lo = jnp.where(here, v_lo, jnp.zeros_like(v_lo))
        out = dot_nt(k_hi, e_hi) + dot_nt(k_lo, e_hi) + dot_nt(k_hi, e_lo)
        for which in range(2):
            for h in range(2):
                block = out[which * W + h * HALF : which * W + (h + 1) * HALF, :]
                at = which * 144
                chunk_ref[2 * k + h, at : at + 96, :] = block[:, 0:PT]
                chunk_ref[2 * k + h, at + 96 : at + 144, :] = block[0:48, PT:] + pltpu.roll(
                    block[48:96, PT:], 64, 1
                )
    gram = own_ref[3 * W :, :] + other_ref[3 * W :, :]
    for g in range(4):
        chunk_ref[g, 288:296, :] = gram


def spread_kernel(in_ref, out_ref):
    total = in_ref[0]
    for i in range(1, 4):
        total = total + in_ref[i]
    out_ref[...] = jnp.zeros_like(out_ref)
    for which in range(2):
        for j in range(3):
            at = which * 144 + j * 48
            out_ref[pl.ds(3 * which + j, 48, 8), :] = total[at : at + 48, :]
    out_ref[pl.ds(6, 64, 8), :] = jnp.broadcast_to(total[288:289, :], (64, PT))


def combine_kernel(in_ref, vec_ref, out_ref, adj_ref):
    total = jnp.sum(in_ref[...].reshape(64, 8, PT), axis=0)
    lane = lanes(1)

    def entry(i):
        return jnp.sum(jnp.where(lane == i, total[6:7, :], 0.0), axis=1, keepdims=True)

    g00, g01, g11, g02, g12, g22 = [entry(i) for i in range(6)]
    alpha = g01 / g00
    beta = jnp.sqrt(g00)
    p2 = g11 - alpha * g01
    pn = jnp.sqrt(p2)
    h00 = 1.0 - alpha
    h10 = pn / beta
    h01 = (g02 - alpha * g01) / (beta * pn)
    qv1 = (g12 - alpha * g11 - alpha * g02 + alpha * alpha * g01) / p2
    h11 = 1.0 - qv1
    n00 = h00 * h00 + h10 * h10
    n01 = h00 * h01 + h10 * h11
    n11 = 1.0 - 2.0 * qv1 + (g22 - 2.0 * alpha * g12 + alpha * alpha * g11) / p2
    r0 = beta * h00
    r1 = beta * h01
    f00 = jnp.sqrt(n00)
    f10 = n01 / f00
    f11 = jnp.sqrt(n11 - f10 * f10)
    y0 = r0 / f00
    y1 = (r1 - f10 * y0) / f11
    w1 = y1 / f11
    w0 = (y0 - f10 * w1) / f00
    c1 = -w1 / pn
    c0 = w0 / beta - c1 * alpha
    mixed = c0 * total[0:3, :] + c1 * total[3:6, :]
    mixed = jnp.concatenate([mixed, jnp.zeros((1, PT), F32)] * 2, axis=0)
    for i in range(32):
        out_ref[8 * i : 8 * i + 8, :] = mixed
    adj_ref[...] = c0 * vec_ref[0:W, :] + c1 * vec_ref[W : 2 * W, :]


def copies_kernel(in_ref, out_ref):
    for j in range(3):
        rows = in_ref[pl.ds(j, 48, 4), :]
        for i in range(4):
            out_ref[i, 48 * j : 48 * (j + 1), :] = rows


def expand_kernel(tile_ref, own_ref, other_ref, out_ref):
    core = lax.rem(tile_ref[0], 2)
    for ref, first in ((own_ref, 2 * core), (other_ref, 2 - 2 * core)):
        for k in range(2):
            for h in range(2):
                block = ref[2 * k + h]
                at = h * HALF
                edge = block[96:144, :]
                out_ref[first + k, at : at + HALF, 0:PT] = block[0:HALF, :]
                out_ref[first + k, at : at + 48, PT:W] = edge[:, 0:64]
                out_ref[first + k, at + 48 : at + HALF, PT:W] = pltpu.roll(edge, 64, 1)[:, 0:64]


def call(kernel, shapes, *args, smem=0, mib=6, dtype=F32, fetched=False, us=1, **kw):
    if fetched:
        kw["scratch_shapes"] = [pltpu.VMEM(a.shape, a.dtype) for a in args[smem:]]
        kw["scratch_shapes"].append(pltpu.SemaphoreType.DMA((len(args) - smem,)))
    return pl.pallas_call(
        kernel,
        out_shape=[
            s if isinstance(s, jax.ShapeDtypeStruct) else jax.ShapeDtypeStruct(s, dtype)
            for s in shapes
        ],
        in_specs=[pl.BlockSpec(memory_space=pltpu.SMEM)] * smem
        + [pl.BlockSpec(memory_space=pltpu.HBM if fetched else pltpu.VMEM)] * (len(args) - smem),
        cost_estimate=pl.CostEstimate(
            flops=us * 10**9, bytes_accessed=us * 3 * 10**6, transcendentals=0
        ),
        compiler_params=pltpu.CompilerParams(vmem_limit_bytes=mib * MIB),
        **kw,
    )(*args)


def swapped(one, two, axis):
    n = lax.axis_size(axis)
    near = [(i, i ^ 1) for i in range(n)]
    far = [(i, i - 1 if i % 2 == 0 else i + 1) for i in range(1, n - 1)]
    return lax.ppermute(one, axis, near), lax.ppermute(two, axis, far)


def body(
    forward_coeff,
    incident,
    cost_grad,
    tmat_real,
    tmat_imag,
    translation_real,
    translation_imaginary,
    neighbours,
    particle_type,
):
    n_short = lax.axis_size("gy")
    tile = lax.axis_index("gx") * n_short + lax.axis_index("gy")
    tile = tile.astype(jnp.int32).reshape(1)
    kinds = particle_type.reshape(1, PT)
    one, two = call(
        functools.partial(pack_wide_kernel, n_short),
        [(ROWS + HALF, PT)] * 2,
        tile,
        forward_coeff,
        cost_grad,
        neighbours,
        kinds,
        smem=1,
        mib=60,
        us=4,
        fetched=True,
    )
    x1, x2 = swapped(one, two, "gx")
    one, two = call(
        functools.partial(pack_short_kernel, n_short),
        [(ROWS, PT)] * 2,
        tile,
        forward_coeff,
        cost_grad,
        neighbours,
        kinds,
        x1,
        x2,
        smem=1,
    )
    y1, y2 = swapped(one, two, "gy")

    tw, lw, fw = call(
        weight_kernel,
        [(2 * W, KINDS * W), (2 * W, 2 * PART), (2 * W, 2 * PART)],
        tmat_real,
        tmat_imag,
        translation_real,
        translation_imaginary,
        mib=16,
        dtype=BF16,
    )

    scratch = [pltpu.VMEM((2 * PART, 2 * PT), BF16)] * 2
    early = call(
        functools.partial(early_kernel, n_short),
        [(W, 2 * PT), jax.ShapeDtypeStruct((2 * W, 3 * PT), BF16)]
        + [jax.ShapeDtypeStruct((2 * PART, PT), BF16)] * 2,
        tile,
        cost_grad,
        neighbours,
        kinds,
        x1,
        x2,
        forward_coeff,
        tw,
        lw,
        smem=1,
        mib=24,
        us=4,
        scratch_shapes=scratch,
    )
    (vectors,) = call(
        functools.partial(main_kernel, n_short),
        [(3 * W + 8, PT)],
        tile,
        cost_grad,
        neighbours,
        kinds,
        incident,
        x1,
        x2,
        y1,
        y2,
        *early,
        tw,
        lw,
        fw,
        smem=1,
        mib=24,
        us=4,
        scratch_shapes=scratch,
    )
    pairs = [(i, i ^ 1) for i in range(n_short)]
    lines = [list(range(c, n_short, 2)) for c in range(2)]
    partner = lax.ppermute(vectors, "gy", pairs)
    (chunks,) = call(outer_kernel, [(4, CHUNK, PT)], tile, vectors, partner, smem=1)
    got = lax.all_to_all(chunks, "gy", 0, 0, axis_index_groups=lines)
    (pieces,) = call(spread_kernel, [(512, PT)], got)
    got = lax.all_to_all(pieces.reshape(64, 8, PT), "gx", 0, 0)
    mixed, adjoint = call(combine_kernel, [(256, PT), (W, PT)], got.reshape(512, PT), vectors)
    got = lax.all_to_all(mixed.reshape(64, 4, PT), "gx", 0, 0)
    (copies,) = call(copies_kernel, [(4, 144, PT)], got.reshape(256, PT))
    half = lax.all_to_all(copies, "gy", 0, 0, axis_index_groups=lines)
    other = lax.ppermute(half, "gy", pairs)
    (sensitivity,) = call(expand_kernel, [(KINDS, W, W)], tile, half, other, smem=1)
    return (adjoint, sensitivity)


def solution(mesh):
    placed = (
        P(None, ("gx", "gy")),
        P(None, ("gx", "gy")),
        P(None, ("gx", "gy")),
        P(),
        P(),
        P(),
        P(),
        P(None, ("gx", "gy")),
        P(("gx", "gy")),
    )
    return jax.shard_map(
        body, mesh=mesh, in_specs=placed, out_specs=(P(None, ("gx", "gy")), P()), check_vma=False
    )
```

```python
import functools

import jax
import jax.numpy as jnp
from jax import lax
from jax.experimental import pallas as pl
from jax.experimental.pallas import tpu as pltpu
from jax.sharding import PartitionSpec as P

F32 = jnp.float32
BF16 = jnp.bfloat16
W = 192
HALF = 96
PT = 128
SLOTS = 10
KINDS = 4
META = 16
ROWS = W + META
CHUNK = 296
PART = 1024
MIB = 1024 * 1024


def split(x):
    hi = x.astype(BF16)
    return hi, (x - hi.astype(F32)).astype(BF16)


def dot(a, b):
    return lax.dot_general(a, b, (((1,), (0,)), ((), ())), preferred_element_type=F32)


def dot_nt(a, b):
    return lax.dot_general(a, b, (((1,), (1,)), ((), ())), preferred_element_type=F32)


def lanes(rows):
    return lax.broadcasted_iota(jnp.int32, (rows, PT), 1)


def meta_rows(nb_ref, pt_ref):
    return jnp.concatenate(
        [
            (nb_ref[...] + 1).astype(F32),
            pt_ref[...].astype(F32),
            jnp.zeros((META - SLOTS - 1, PT), F32),
        ],
        axis=0,
    )


def even_row(short, tile_ref):
    return lax.rem(lax.div(tile_ref[0], short), 2) == 0


def even_col(tile_ref):
    return lax.rem(tile_ref[0], 2) == 0


def pack_wide_kernel(short, tile_ref, fc_ref, b_ref, nb_ref, pt_ref, _, one_ref, two_ref):
    even = even_row(short, tile_ref)
    meta = meta_rows(nb_ref, pt_ref)
    top, low = fc_ref[0:HALF, :], fc_ref[HALF:W, :]
    first = lanes(HALF) < 64
    for ref in (one_ref, two_ref):
        ref[0:W, :] = b_ref[...]
        ref[W:ROWS, :] = meta
    up = jnp.where(first, pltpu.roll(top, 64, 1), low)
    dn = jnp.where(first, top, pltpu.roll(low, 64, 1))
    one_ref[ROWS : ROWS + HALF, :] = jnp.where(even, up, dn)
    two_ref[ROWS : ROWS + HALF, :] = jnp.where(even, dn, up)


def unpack_fc(up, dn):
    first = lanes(HALF) < 64
    return jnp.concatenate(
        [
            jnp.where(first, dn, pltpu.roll(up, 64, 1)),
            jnp.where(first, pltpu.roll(dn, 64, 1), up),
        ],
        axis=0,
    )


class Tiles:
    def __init__(self, even, one_ref, two_ref):
        self.even, self.one, self.two = even, one_ref, two_ref

    def below(self, rows):
        return jnp.where(self.even, self.two[rows, :], self.one[rows, :])

    def above(self, rows):
        return jnp.where(self.even, self.one[rows, :], self.two[rows, :])


def pack_short_kernel(
    short, tile_ref, fc_ref, b_ref, nb_ref, pt_ref, x1_ref, x2_ref, one_ref, two_ref
):
    wide = Tiles(even_row(short, tile_ref), x1_ref, x2_ref)
    even = even_col(tile_ref)
    half = slice(ROWS, ROWS + HALF)
    first = lanes(META) < 64
    meta = meta_rows(nb_ref, pt_ref)
    fc_ud = unpack_fc(wide.below(half), wide.above(half))

    def part(rows, tiles):
        col = lanes(rows.stop - rows.start) % 32
        up, own, dn, edge, edge_ud = tiles

        def moved(x, shift):
            return pltpu.roll(x, shift, 1) if shift else x

        low = moved(up, 0)
        low = jnp.where(col < 4, low, moved(own, 4))
        low = jnp.where(col < 8, low, moved(dn, 8))
        low = jnp.where(col < 12, low, moved(edge, 12))
        low = jnp.where(col < 14, low, moved(edge_ud, 14))
        high = moved(edge, 114)
        high = jnp.where(col < 18, high, moved(edge_ud, 116))
        high = jnp.where(col < 20, high, moved(up, 120))
        high = jnp.where(col < 24, high, moved(own, 124))
        high = jnp.where(col < 28, high, dn)
        one_ref[rows, :] = jnp.where(even, high, low)
        two_ref[rows, :] = jnp.where(even, low, high)

    v, m = slice(0, W), slice(W, ROWS)
    part(v, (wide.below(v), b_ref[...], wide.above(v), fc_ref[...], fc_ud))
    meta_up, meta_dn = wide.below(m), wide.above(m)
    part(m, (meta_up, meta, meta_dn, meta, jnp.where(first, meta_dn, meta_up)))


def weight_kernel(tr_ref, ti_ref, lr_ref, li_ref, tw_ref, lw_ref, fw_ref):
    def turned(ref):
        n = ref.shape[0]
        fill = -n * HALF % PT
        side = jnp.concatenate([ref[...].reshape(n * HALF, HALF), jnp.zeros((n * HALF, 32), F32)], axis=1)
        if fill:
            side = jnp.concatenate([side, jnp.zeros((fill, PT), F32)], axis=0)
        return split(jnp.transpose(side)[0:HALF, :])

    def beside(ref):
        n = ref.shape[0]
        return split(
            jnp.concatenate([ref[s] for s in range(n)] + [jnp.zeros((HALF, -n * HALF % PT), F32)], axis=1)
        )

    def store(ref, real, imag, sign):
        width = real[0].shape[1]
        for at, re, im in zip((0, W), real, imag):
            ref[at : at + HALF, 0:width] = re
            ref[at : at + HALF, width:] = im if sign > 0 else -im
            ref[at + HALF : at + W, 0:width] = -im if sign > 0 else im
            ref[at + HALF : at + W, width:] = re

    store(tw_ref, turned(tr_ref), turned(ti_ref), 1)
    store(lw_ref, turned(lr_ref), turned(li_ref), 1)
    store(fw_ref, beside(lr_ref), beside(li_ref), -1)


def target_ids(base, row_stride):
    spot = lax.broadcasted_iota(jnp.int32, (4 * PT, PT), 0)
    lane = spot % PT
    row, col = lane // 32, lane % 32
    shift = jnp.where(row < 2, row_stride, -row_stride)
    own = base + lane
    beside = base + row * 32
    lr = jnp.where(
        col < 14,
        beside + PT + col - 12,
        jnp.where(
            col < 16,
            beside + PT + shift + col - 14,
            jnp.where(col < 18, beside - PT + col + 14, beside - PT + shift + col + 12),
        ),
    )
    lr = jnp.where((col >= 12) & (col < 20), lr, -10)
    edge = jnp.where(
        (col < 2) | (col >= 30),
        own,
        jnp.where(col < 4, own - 2 + shift, jnp.where(col >= 28, own + 2 + shift, lr)),
    )
    ids = jnp.where(
        spot < PT,
        own,
        jnp.where(spot < 2 * PT, own + shift, jnp.where(spot < 3 * PT, lr, edge)),
    )
    return jnp.where(ids >= 0, ids + 1, -10).astype(F32)


def target_ids_kernel(short, tile_ref, ids_ref):
    ids_ref[...] = target_ids(tile_ref[0] * PT, short * PT)


def narrow_product(w_ref, both):
    rows = dot(w_ref[0:W, :], both)
    return rows[:, 0:PT] + rows[:, PT:] + dot(w_ref[W : 2 * W, :], both[:, 0:PT])


def product(w_ref, hi, lo):
    rows = dot(w_ref[...], hi)
    return rows[0:W] + rows[W : 2 * W] + dot(w_ref[0:W, :], lo)


def scaled_by_type(tw_ref, blocks, metas):
    his, los = [], []
    for v, meta in zip(blocks, metas):
        hi, lo = split(v)
        kind = meta[SLOTS : SLOTS + 1, :]
        his.append([jnp.where(kind == float(k), hi, jnp.zeros_like(hi)) for k in range(KINDS)])
        los.append([jnp.where(kind == float(k), lo, jnp.zeros_like(lo)) for k in range(KINDS)])

    def by_part(pieces):
        whole = [jnp.concatenate([p[k] for p in pieces], axis=1) for k in range(KINDS)]
        return jnp.concatenate([w[0:HALF] for w in whole] + [w[HALF:W] for w in whole], axis=0)

    s_hi, s_lo = split(product(tw_ref, by_part(his), by_part(los)))
    return jnp.concatenate([s_hi, s_lo], axis=0)


def one_hot(at, meta, s):
    return jnp.where(at == meta[s : s + 1, :], 1.0, 0.0).astype(BF16)


def place(spots, parts, s, lanes_from):
    for (ref, lanes_at), part in zip(spots, parts):
        for half in range(2):
            at = half * PART + s * HALF
            ref[at : at + HALF, lanes_at] = part[half * HALF : (half + 1) * HALF, lanes_from]


def beside(ref):
    return ((ref, slice(0, PT)), (ref, slice(PT, 2 * PT)))


def clear_fill(refs):
    for ref in refs:
        for at in (SLOTS * HALF, PART + SLOTS * HALF):
            rows = PART - SLOTS * HALF
            ref[at : at + rows, :] = jnp.zeros((rows, ref.shape[1]), BF16)


def scatter_pairs(ref, stack, ids, metas):
    for s in range(0, SLOTS, 2):
        pick = jnp.concatenate(
            [
                jnp.concatenate([one_hot(at, meta, t) for at, meta in zip(ids, metas)], axis=1)
                for t in (s, s + 1)
            ],
            axis=0,
        )
        g = dot_nt(stack, pick)
        parts = split(g[0:W] + g[W : 2 * W])
        for t in (0, 1):
            place(beside(ref), parts, s + t, slice(t * PT, (t + 1) * PT))


def gather_pairs(ref, blocks, ids, meta):
    stack = jnp.concatenate(split(jnp.concatenate(blocks, axis=1)), axis=0)
    for s in range(0, SLOTS, 2):
        pick = jnp.concatenate([one_hot(ids, meta, s), one_hot(ids, meta, s + 1)], axis=1)
        g = dot(stack, pick).astype(BF16)
        for t in (0, 1):
            parts = (g[0:W], g[W : 2 * W])
            place(beside(ref), parts, s + t, slice(t * PT, (t + 1) * PT))


def early_kernel(
    short,
    tile_ref,
    ids_ref,
    b_ref,
    nb_ref,
    pt_ref,
    x1_ref,
    x2_ref,
    fc_ref,
    tw_ref,
    lw_ref,
    part_ref,
    stack_ref,
    f_ref,
    ghi_ref,
    glo_ref,
):
    wide = Tiles(even_row(short, tile_ref), x1_ref, x2_ref)
    v, m, half = slice(0, W), slice(W, ROWS), slice(ROWS, ROWS + HALF)
    refs = (ghi_ref, glo_ref)
    ids = ids_ref[0 : 2 * PT, :]
    own = meta_rows(nb_ref, pt_ref)
    metas = (own, wide.below(m), wide.above(m))
    clear_fill(refs + (f_ref,))
    stack = scaled_by_type(tw_ref, (b_ref[...], wide.below(v), wide.above(v)), metas)
    stack_ref[...] = stack
    for s in range(SLOTS):
        pick = jnp.concatenate([one_hot(ids, meta, s) for meta in metas], axis=1)
        g = dot_nt(stack, pick)
        place([(ref, slice(None)) for ref in refs], split(g[0:W] + g[W : 2 * W]), s, slice(None))
    part_ref[...] = product(lw_ref, ghi_ref[...], glo_ref[...])
    fc_ud = unpack_fc(wide.below(half), wide.above(half))
    gather_pairs(f_ref, (fc_ref[...], fc_ud), ids, own)


def main_kernel(
    short,
    tile_ref,
    ids_ref,
    b_ref,
    nb_ref,
    pt_ref,
    inc_ref,
    x1_ref,
    x2_ref,
    y1_ref,
    y2_ref,
    part_ref,
    stack_ref,
    f_ref,
    tw_ref,
    lw_ref,
    fw_ref,
    vec_ref,
    g_ref,
    h_ref,
):
    rows = Tiles(even_row(short, tile_ref), x1_ref, x2_ref)
    cols = Tiles(even_col(tile_ref), y1_ref, y2_ref)
    v, m = slice(0, W), slice(W, ROWS)
    ids = ids_ref[...]
    col = lanes(META) % 32
    b = b_ref[...]
    m_own = meta_rows(nb_ref, pt_ref)
    m_up, m_dn = rows.below(m), rows.above(m)
    m_ud = jnp.where(lanes(META) < 64, m_dn, m_up)
    m_lr = jnp.where(col >= 16, cols.below(m), cols.above(m))
    spot = lanes(W) % 32
    x_lr = jnp.where(spot >= 16, cols.below(v), cols.above(v))
    b_zone = (col < 12) | (col >= 20)
    row_id = lax.broadcasted_iota(jnp.int32, (META, PT), 0)
    m_b = jnp.where(b_zone | (row_id >= SLOTS), m_lr, 0.0)
    m_f = jnp.where(b_zone & (row_id < SLOTS), 0.0, m_lr)
    clear_fill((g_ref, h_ref))
    first, second = slice(0, PT), slice(PT, 2 * PT)
    own_ids, lr_ids, edge_ids = ids[0:PT, :], ids[2 * PT : 3 * PT, :], ids[3 * PT :, :]

    stack = jnp.concatenate([stack_ref[...], scaled_by_type(tw_ref, (x_lr,), (m_b,))], axis=1)
    scatter_pairs(g_ref, stack, (lr_ids, lr_ids, lr_ids, edge_ids), (m_own, m_up, m_dn, m_b))
    edge = narrow_product(lw_ref, g_ref[...])
    left, right = spot < 2, spot >= 30
    u1 = part_ref[:, first] + jnp.where(left | right, edge, 0.0)
    u1_ud = part_ref[:, second] + jnp.where(
        left, pltpu.roll(edge, PT - 2, 1), jnp.where(right, pltpu.roll(edge, 2, 1), 0.0)
    )
    u1_lr = jnp.where((spot >= 12) & (spot < 20), edge, 0.0)

    gather_pairs(h_ref, (x_lr,), lr_ids, m_own)
    exc = inc_ref[...] + narrow_product(fw_ref, h_ref[...] + f_ref[...])
    vec_ref[0:W, :] = b
    vec_ref[W : 2 * W, :] = u1
    vec_ref[2 * W : 3 * W, :] = exc

    metas = (m_own, m_ud, m_f)
    stack = scaled_by_type(tw_ref, (u1, u1_ud, u1_lr), metas)
    scatter_pairs(g_ref, stack, (own_ids,) * 3, metas)
    u2 = narrow_product(lw_ref, g_ref[...])

    lane, row = lanes(8), lax.broadcasted_iota(jnp.int32, (8, PT), 0)
    gram = jnp.zeros((8, PT), F32)
    for i, (p, q) in enumerate(((b, b), (b, u1), (u1, u1), (b, u2), (u1, u2), (u2, u2))):
        gram = jnp.where(lane == i, jnp.sum(p * q), gram)
    vec_ref[3 * W :, :] = jnp.where(row == 0, gram, m_own[SLOTS : SLOTS + 1, :])


def outer_kernel(tile_ref, own_ref, other_ref, chunk_ref):
    def both(rows):
        return jnp.concatenate([own_ref[rows, :], other_ref[rows, :]], axis=1)

    exc = both(slice(2 * W, 3 * W))
    e_hi, e_lo = split(jnp.concatenate([exc, jnp.zeros((64, 2 * PT), F32)], axis=0))
    v_hi, v_lo = split(both(slice(0, 2 * W)))
    kind = both(slice(3 * W + 1, 3 * W + 2))
    for k in range(2):
        here = kind == (2 * lax.rem(tile_ref[0], 2) + k).astype(F32)
        k_hi = jnp.where(here, v_hi, jnp.zeros_like(v_hi))
        k_lo = jnp.where(here, v_lo, jnp.zeros_like(v_lo))
        out = dot_nt(k_hi, e_hi) + dot_nt(k_lo, e_hi) + dot_nt(k_hi, e_lo)
        for which in range(2):
            for h in range(2):
                block = out[which * W + h * HALF : which * W + (h + 1) * HALF, :]
                at = which * 144
                chunk_ref[2 * k + h, at : at + 96, :] = block[:, 0:PT]
                chunk_ref[2 * k + h, at + 96 : at + 144, :] = block[0:48, PT:] + pltpu.roll(
                    block[48:96, PT:], 64, 1
                )
    gram = own_ref[3 * W :, :] + other_ref[3 * W :, :]
    for g in range(4):
        chunk_ref[g, 288:296, :] = gram


def spread_kernel(in_ref, out_ref):
    total = in_ref[0]
    for i in range(1, 4):
        total = total + in_ref[i]
    out_ref[...] = jnp.zeros_like(out_ref)
    for which in range(2):
        for j in range(3):
            at = which * 144 + j * 48
            out_ref[pl.ds(3 * which + j, 48, 8), :] = total[at : at + 48, :]
    out_ref[pl.ds(6, 64, 8), :] = jnp.broadcast_to(total[288:289, :], (64, PT))


def combine_kernel(in_ref, out_ref, coef_ref):
    total = jnp.sum(in_ref[...].reshape(64, 8, PT), axis=0)
    lane = lanes(1)

    def entry(i):
        return jnp.sum(jnp.where(lane == i, total[6:7, :], 0.0), axis=1, keepdims=True)

    g00, g01, g11, g02, g12, g22 = [entry(i) for i in range(6)]
    alpha = g01 / g00
    beta = jnp.sqrt(g00)
    p2 = g11 - alpha * g01
    pn = jnp.sqrt(p2)
    h00 = 1.0 - alpha
    h10 = pn / beta
    h01 = (g02 - alpha * g01) / (beta * pn)
    qv1 = (g12 - alpha * g11 - alpha * g02 + alpha * alpha * g01) / p2
    h11 = 1.0 - qv1
    n00 = h00 * h00 + h10 * h10
    n01 = h00 * h01 + h10 * h11
    n11 = 1.0 - 2.0 * qv1 + (g22 - 2.0 * alpha * g12 + alpha * alpha * g11) / p2
    r0 = beta * h00
    r1 = beta * h01
    f00 = jnp.sqrt(n00)
    f10 = n01 / f00
    f11 = jnp.sqrt(n11 - f10 * f10)
    y0 = r0 / f00
    y1 = (r1 - f10 * y0) / f11
    w1 = y1 / f11
    w0 = (y0 - f10 * w1) / f00
    c1 = -w1 / pn
    c0 = w0 / beta - c1 * alpha
    mixed = c0 * total[0:3, :] + c1 * total[3:6, :]
    mixed = jnp.concatenate([mixed, jnp.zeros((1, PT), F32)] * 2, axis=0)
    for i in range(32):
        out_ref[8 * i : 8 * i + 8, :] = mixed
    coef_ref[0:4, :] = jnp.broadcast_to(c0, (4, PT))
    coef_ref[4:8, :] = jnp.broadcast_to(c1, (4, PT))


def copies_kernel(in_ref, out_ref):
    for j in range(3):
        rows = in_ref[pl.ds(j, 48, 4), :]
        for i in range(4):
            out_ref[i, 48 * j : 48 * (j + 1), :] = rows


def expand_kernel(tile_ref, own_ref, other_ref, vec_ref, coef_ref, out_ref, adj_ref):
    adj_ref[...] = coef_ref[0:1, :] * vec_ref[0:W, :] + coef_ref[4:5, :] * vec_ref[W : 2 * W, :]
    core = lax.rem(tile_ref[0], 2)
    for ref, first in ((own_ref, 2 * core), (other_ref, 2 - 2 * core)):
        for k in range(2):
            for h in range(2):
                block = ref[2 * k + h]
                at = h * HALF
                edge = block[96:144, :]
                out_ref[first + k, at : at + HALF, 0:PT] = block[0:HALF, :]
                out_ref[first + k, at : at + 48, PT:W] = edge[:, 0:64]
                out_ref[first + k, at + 48 : at + HALF, PT:W] = pltpu.roll(edge, 64, 1)[:, 0:64]


def call(kernel, shapes, *args, smem=0, whole=0, mib=6, dtype=F32, us=1, **kw):
    return pl.pallas_call(
        kernel,
        out_shape=[
            s if isinstance(s, jax.ShapeDtypeStruct) else jax.ShapeDtypeStruct(s, dtype)
            for s in shapes
        ],
        in_specs=[pl.BlockSpec(memory_space=pltpu.SMEM)] * smem
        + [pl.BlockSpec(memory_space=pltpu.VMEM)] * (len(args) - smem - whole)
        + [pl.BlockSpec(memory_space=pl.ANY)] * whole,
        cost_estimate=pl.CostEstimate(
            flops=us * 10**9, bytes_accessed=us * 3 * 10**6, transcendentals=0
        ),
        compiler_params=pltpu.CompilerParams(vmem_limit_bytes=mib * MIB),
        **kw,
    )(*args)


def swapped(one, two, axis):
    n = lax.axis_size(axis)
    near = [(i, i ^ 1) for i in range(n)]
    far = [(i, i - 1 if i % 2 == 0 else i + 1) for i in range(1, n - 1)]
    return lax.ppermute(one, axis, near), lax.ppermute(two, axis, far)


def body(
    forward_coeff,
    incident,
    cost_grad,
    tmat_real,
    tmat_imag,
    translation_real,
    translation_imaginary,
    neighbours,
    particle_type,
):
    n_short = lax.axis_size("gy")
    tile = lax.axis_index("gx") * n_short + lax.axis_index("gy")
    tile = tile.astype(jnp.int32).reshape(1)
    kinds = particle_type.reshape(1, PT)
    (ids,) = call(
        functools.partial(target_ids_kernel, n_short), [(4 * PT, PT)], tile, smem=1, us=4
    )
    one, two = call(
        functools.partial(pack_wide_kernel, n_short),
        [(ROWS + HALF, PT)] * 2,
        tile,
        forward_coeff,
        cost_grad,
        neighbours,
        kinds,
        ids,
        smem=1,
        whole=1,
    )
    x1, x2 = swapped(one, two, "gx")
    one, two = call(
        functools.partial(pack_short_kernel, n_short),
        [(ROWS, PT)] * 2,
        tile,
        forward_coeff,
        cost_grad,
        neighbours,
        kinds,
        x1,
        x2,
        smem=1,
    )
    y1, y2 = swapped(one, two, "gy")

    tw, lw, fw = call(
        weight_kernel,
        [(2 * W, KINDS * W), (2 * W, 2 * PART), (2 * W, 2 * PART)],
        tmat_real,
        tmat_imag,
        translation_real,
        translation_imaginary,
        mib=16,
        dtype=BF16,
    )

    scratch = [pltpu.VMEM((2 * PART, 2 * PT), BF16)] * 2
    early = call(
        functools.partial(early_kernel, n_short),
        [(W, 2 * PT), jax.ShapeDtypeStruct((2 * W, 3 * PT), BF16)]
        + [jax.ShapeDtypeStruct((2 * PART, 2 * PT), BF16)],
        tile,
        ids,
        cost_grad,
        neighbours,
        kinds,
        x1,
        x2,
        forward_coeff,
        tw,
        lw,
        smem=1,
        mib=24,
        us=4,
        scratch_shapes=scratch,
    )
    (vectors,) = call(
        functools.partial(main_kernel, n_short),
        [(3 * W + 8, PT)],
        tile,
        ids,
        cost_grad,
        neighbours,
        kinds,
        incident,
        x1,
        x2,
        y1,
        y2,
        *early,
        tw,
        lw,
        fw,
        smem=1,
        mib=24,
        us=4,
        scratch_shapes=scratch,
    )
    pairs = [(i, i ^ 1) for i in range(n_short)]
    lines = [list(range(c, n_short, 2)) for c in range(2)]
    partner = lax.ppermute(vectors, "gy", pairs)
    (chunks,) = call(outer_kernel, [(4, CHUNK, PT)], tile, vectors, partner, smem=1)
    got = lax.all_to_all(chunks, "gy", 0, 0, axis_index_groups=lines)
    (pieces,) = call(spread_kernel, [(512, PT)], got)
    got = lax.all_to_all(pieces.reshape(64, 8, PT), "gx", 0, 0)
    mixed, coefs = call(combine_kernel, [(256, PT), (8, PT)], got.reshape(512, PT))
    got = lax.all_to_all(mixed.reshape(64, 4, PT), "gx", 0, 0)
    (copies,) = call(copies_kernel, [(4, 144, PT)], got.reshape(256, PT))
    half = lax.all_to_all(copies, "gy", 0, 0, axis_index_groups=lines)
    other = lax.ppermute(half, "gy", pairs)
    sensitivity, adjoint = call(
        expand_kernel,
        [(KINDS, W, W), (W, PT)],
        tile,
        half,
        other,
        vectors,
        coefs,
        smem=1,
    )
    return (adjoint, sensitivity)


def solution(mesh):
    placed = (
        P(None, ("gx", "gy")),
        P(None, ("gx", "gy")),
        P(None, ("gx", "gy")),
        P(),
        P(),
        P(),
        P(),
        P(None, ("gx", "gy")),
        P(("gx", "gy")),
    )
    return jax.shard_map(
        body, mesh=mesh, in_specs=placed, out_specs=(P(None, ("gx", "gy")), P()), check_vma=False
    )
```

```python
import functools
import math

import jax
import jax.numpy as jnp
from jax import lax
from jax.experimental import pallas as pl
from jax.experimental.pallas import tpu as pltpu
from jax.sharding import Mesh
from jax.sharding import PartitionSpec as P

F32 = jnp.float32
BF16 = jnp.bfloat16
W = 192
HALF = 96
PT = 128
SLOTS = 10
KINDS = 4
META = 16
ROWS = W + META
CHUNK = 40
BACK = 24
TALL = ("z", "y")
FLAT = ("x", "c")
PART = 1024
MIB = 1024 * 1024


def split(x):
    hi = x.astype(BF16)
    return hi, (x - hi.astype(F32)).astype(BF16)


def dot(a, b):
    return lax.dot_general(a, b, (((1,), (0,)), ((), ())), preferred_element_type=F32)


def dot_nt(a, b):
    return lax.dot_general(a, b, (((1,), (1,)), ((), ())), preferred_element_type=F32)


def lanes(rows):
    return lax.broadcasted_iota(jnp.int32, (rows, PT), 1)


def meta_rows(nb_ref, pt_ref):
    return jnp.concatenate(
        [
            (nb_ref[...] + 1).astype(F32),
            pt_ref[...].astype(F32),
            jnp.zeros((META - SLOTS - 1, PT), F32),
        ],
        axis=0,
    )


def even_row(short, tile_ref):
    return lax.rem(lax.div(tile_ref[0], short), 2) == 0


def even_col(tile_ref):
    return lax.rem(tile_ref[0], 2) == 0


def pack_wide_kernel(short, tile_ref, fc_ref, b_ref, nb_ref, pt_ref, _, one_ref, two_ref):
    even = even_row(short, tile_ref)
    meta = meta_rows(nb_ref, pt_ref)
    top, low = fc_ref[0:HALF, :], fc_ref[HALF:W, :]
    first = lanes(HALF) < 64
    for ref in (one_ref, two_ref):
        ref[0:W, :] = b_ref[...]
        ref[W:ROWS, :] = meta
    up = jnp.where(first, pltpu.roll(top, 64, 1), low)
    dn = jnp.where(first, top, pltpu.roll(low, 64, 1))
    one_ref[ROWS : ROWS + HALF, :] = jnp.where(even, up, dn)
    two_ref[ROWS : ROWS + HALF, :] = jnp.where(even, dn, up)


def unpack_fc(up, dn):
    first = lanes(HALF) < 64
    return jnp.concatenate(
        [
            jnp.where(first, dn, pltpu.roll(up, 64, 1)),
            jnp.where(first, pltpu.roll(dn, 64, 1), up),
        ],
        axis=0,
    )


class Tiles:
    def __init__(self, even, one_ref, two_ref):
        self.even, self.one, self.two = even, one_ref, two_ref

    def below(self, rows):
        return jnp.where(self.even, self.two[rows, :], self.one[rows, :])

    def above(self, rows):
        return jnp.where(self.even, self.one[rows, :], self.two[rows, :])


def pack_short_kernel(
    short, tile_ref, fc_ref, b_ref, nb_ref, pt_ref, x1_ref, x2_ref, one_ref, two_ref
):
    wide = Tiles(even_row(short, tile_ref), x1_ref, x2_ref)
    even = even_col(tile_ref)
    half = slice(ROWS, ROWS + HALF)
    first = lanes(META) < 64
    meta = meta_rows(nb_ref, pt_ref)
    fc_ud = unpack_fc(wide.below(half), wide.above(half))

    def part(rows, tiles):
        col = lanes(rows.stop - rows.start) % 32
        up, own, dn, edge, edge_ud = tiles

        def moved(x, shift):
            return pltpu.roll(x, shift, 1) if shift else x

        low = moved(up, 0)
        low = jnp.where(col < 4, low, moved(own, 4))
        low = jnp.where(col < 8, low, moved(dn, 8))
        low = jnp.where(col < 12, low, moved(edge, 12))
        low = jnp.where(col < 14, low, moved(edge_ud, 14))
        high = moved(edge, 114)
        high = jnp.where(col < 18, high, moved(edge_ud, 116))
        high = jnp.where(col < 20, high, moved(up, 120))
        high = jnp.where(col < 24, high, moved(own, 124))
        high = jnp.where(col < 28, high, dn)
        one_ref[rows, :] = jnp.where(even, high, low)
        two_ref[rows, :] = jnp.where(even, low, high)

    v, m = slice(0, W), slice(W, ROWS)
    part(v, (wide.below(v), b_ref[...], wide.above(v), fc_ref[...], fc_ud))
    meta_up, meta_dn = wide.below(m), wide.above(m)
    part(m, (meta_up, meta, meta_dn, meta, jnp.where(first, meta_dn, meta_up)))


def weight_kernel(tr_ref, ti_ref, lr_ref, li_ref, tw_ref, lw_ref, fw_ref):
    def turned(ref):
        n = ref.shape[0]
        fill = -n * HALF % PT
        side = jnp.concatenate([ref[...].reshape(n * HALF, HALF), jnp.zeros((n * HALF, 32), F32)], axis=1)
        if fill:
            side = jnp.concatenate([side, jnp.zeros((fill, PT), F32)], axis=0)
        return split(jnp.transpose(side)[0:HALF, :])

    def beside(ref):
        n = ref.shape[0]
        return split(
            jnp.concatenate([ref[s] for s in range(n)] + [jnp.zeros((HALF, -n * HALF % PT), F32)], axis=1)
        )

    def store(ref, real, imag, sign):
        width = real[0].shape[1]
        for at, re, im in zip((0, W), real, imag):
            ref[at : at + HALF, 0:width] = re
            ref[at : at + HALF, width:] = im if sign > 0 else -im
            ref[at + HALF : at + W, 0:width] = -im if sign > 0 else im
            ref[at + HALF : at + W, width:] = re

    store(tw_ref, turned(tr_ref), turned(ti_ref), 1)
    store(lw_ref, turned(lr_ref), turned(li_ref), 1)
    store(fw_ref, beside(lr_ref), beside(li_ref), -1)


def target_ids(base, row_stride):
    spot = lax.broadcasted_iota(jnp.int32, (4 * PT, PT), 0)
    lane = spot % PT
    row, col = lane // 32, lane % 32
    shift = jnp.where(row < 2, row_stride, -row_stride)
    own = base + lane
    beside = base + row * 32
    lr = jnp.where(
        col < 14,
        beside + PT + col - 12,
        jnp.where(
            col < 16,
            beside + PT + shift + col - 14,
            jnp.where(col < 18, beside - PT + col + 14, beside - PT + shift + col + 12),
        ),
    )
    lr = jnp.where((col >= 12) & (col < 20), lr, -10)
    edge = jnp.where(
        (col < 2) | (col >= 30),
        own,
        jnp.where(col < 4, own - 2 + shift, jnp.where(col >= 28, own + 2 + shift, lr)),
    )
    ids = jnp.where(
        spot < PT,
        own,
        jnp.where(spot < 2 * PT, own + shift, jnp.where(spot < 3 * PT, lr, edge)),
    )
    return jnp.where(ids >= 0, ids + 1, -10).astype(F32)


def target_ids_kernel(short, tile_ref, ids_ref):
    ids_ref[...] = target_ids(tile_ref[0] * PT, short * PT)


def narrow_product(w_ref, both):
    rows = dot(w_ref[0:W, :], both)
    return rows[:, 0:PT] + rows[:, PT:] + dot(w_ref[W : 2 * W, :], both[:, 0:PT])


def product(w_ref, hi, lo):
    rows = dot(w_ref[...], hi)
    return rows[0:W] + rows[W : 2 * W] + dot(w_ref[0:W, :], lo)


def scaled_by_type(tw_ref, blocks, metas):
    his, los = [], []
    for v, meta in zip(blocks, metas):
        hi, lo = split(v)
        kind = meta[SLOTS : SLOTS + 1, :]
        his.append([jnp.where(kind == float(k), hi, jnp.zeros_like(hi)) for k in range(KINDS)])
        los.append([jnp.where(kind == float(k), lo, jnp.zeros_like(lo)) for k in range(KINDS)])

    def by_part(pieces):
        whole = [jnp.concatenate([p[k] for p in pieces], axis=1) for k in range(KINDS)]
        return jnp.concatenate([w[0:HALF] for w in whole] + [w[HALF:W] for w in whole], axis=0)

    s_hi, s_lo = split(product(tw_ref, by_part(his), by_part(los)))
    return jnp.concatenate([s_hi, s_lo], axis=0)


def one_hot(at, meta, s):
    return jnp.where(at == meta[s : s + 1, :], 1.0, 0.0).astype(BF16)


def place(spots, parts, s, lanes_from):
    for (ref, lanes_at), part in zip(spots, parts):
        for half in range(2):
            at = half * PART + s * HALF
            ref[at : at + HALF, lanes_at] = part[half * HALF : (half + 1) * HALF, lanes_from]


def beside(ref):
    return ((ref, slice(0, PT)), (ref, slice(PT, 2 * PT)))


def clear_fill(refs):
    for ref in refs:
        for at in (SLOTS * HALF, PART + SLOTS * HALF):
            rows = PART - SLOTS * HALF
            ref[at : at + rows, :] = jnp.zeros((rows, ref.shape[1]), BF16)


def scatter_pairs(ref, stack, ids, metas):
    for s in range(0, SLOTS, 2):
        pick = jnp.concatenate(
            [
                jnp.concatenate([one_hot(at, meta, t) for at, meta in zip(ids, metas)], axis=1)
                for t in (s, s + 1)
            ],
            axis=0,
        )
        g = dot_nt(stack, pick)
        parts = split(g[0:W] + g[W : 2 * W])
        for t in (0, 1):
            place(beside(ref), parts, s + t, slice(t * PT, (t + 1) * PT))


def gather_pairs(ref, blocks, ids, meta):
    stack = jnp.concatenate(split(jnp.concatenate(blocks, axis=1)), axis=0)
    for s in range(0, SLOTS, 2):
        pick = jnp.concatenate([one_hot(ids, meta, s), one_hot(ids, meta, s + 1)], axis=1)
        g = dot(stack, pick).astype(BF16)
        for t in (0, 1):
            parts = (g[0:W], g[W : 2 * W])
            place(beside(ref), parts, s + t, slice(t * PT, (t + 1) * PT))


def early_kernel(
    short,
    tile_ref,
    ids_ref,
    b_ref,
    nb_ref,
    pt_ref,
    x1_ref,
    x2_ref,
    fc_ref,
    tw_ref,
    lw_ref,
    part_ref,
    stack_ref,
    f_ref,
    ghi_ref,
    glo_ref,
):
    wide = Tiles(even_row(short, tile_ref), x1_ref, x2_ref)
    v, m, half = slice(0, W), slice(W, ROWS), slice(ROWS, ROWS + HALF)
    refs = (ghi_ref, glo_ref)
    ids = ids_ref[0 : 2 * PT, :]
    own = meta_rows(nb_ref, pt_ref)
    metas = (own, wide.below(m), wide.above(m))
    clear_fill(refs + (f_ref,))
    stack = scaled_by_type(tw_ref, (b_ref[...], wide.below(v), wide.above(v)), metas)
    stack_ref[...] = stack
    for s in range(SLOTS):
        pick = jnp.concatenate([one_hot(ids, meta, s) for meta in metas], axis=1)
        g = dot_nt(stack, pick)
        place([(ref, slice(None)) for ref in refs], split(g[0:W] + g[W : 2 * W]), s, slice(None))
    part_ref[...] = product(lw_ref, ghi_ref[...], glo_ref[...])
    fc_ud = unpack_fc(wide.below(half), wide.above(half))
    gather_pairs(f_ref, (fc_ref[...], fc_ud), ids, own)


def main_kernel(
    short,
    tile_ref,
    ids_ref,
    b_ref,
    nb_ref,
    pt_ref,
    inc_ref,
    x1_ref,
    x2_ref,
    y1_ref,
    y2_ref,
    part_ref,
    stack_ref,
    f_ref,
    tw_ref,
    lw_ref,
    fw_ref,
    vec_ref,
    g_ref,
    h_ref,
):
    rows = Tiles(even_row(short, tile_ref), x1_ref, x2_ref)
    cols = Tiles(even_col(tile_ref), y1_ref, y2_ref)
    v, m = slice(0, W), slice(W, ROWS)
    ids = ids_ref[...]
    col = lanes(META) % 32
    b = b_ref[...]
    m_own = meta_rows(nb_ref, pt_ref)
    m_up, m_dn = rows.below(m), rows.above(m)
    m_ud = jnp.where(lanes(META) < 64, m_dn, m_up)
    m_lr = jnp.where(col >= 16, cols.below(m), cols.above(m))
    spot = lanes(W) % 32
    x_lr = jnp.where(spot >= 16, cols.below(v), cols.above(v))
    b_zone = (col < 12) | (col >= 20)
    row_id = lax.broadcasted_iota(jnp.int32, (META, PT), 0)
    m_b = jnp.where(b_zone | (row_id >= SLOTS), m_lr, 0.0)
    m_f = jnp.where(b_zone & (row_id < SLOTS), 0.0, m_lr)
    clear_fill((g_ref, h_ref))
    first, second = slice(0, PT), slice(PT, 2 * PT)
    own_ids, lr_ids, edge_ids = ids[0:PT, :], ids[2 * PT : 3 * PT, :], ids[3 * PT :, :]

    stack = jnp.concatenate([stack_ref[...], scaled_by_type(tw_ref, (x_lr,), (m_b,))], axis=1)
    scatter_pairs(g_ref, stack, (lr_ids, lr_ids, lr_ids, edge_ids), (m_own, m_up, m_dn, m_b))
    edge = narrow_product(lw_ref, g_ref[...])
    left, right = spot < 2, spot >= 30
    u1 = part_ref[:, first] + jnp.where(left | right, edge, 0.0)
    u1_ud = part_ref[:, second] + jnp.where(
        left, pltpu.roll(edge, PT - 2, 1), jnp.where(right, pltpu.roll(edge, 2, 1), 0.0)
    )
    u1_lr = jnp.where((spot >= 12) & (spot < 20), edge, 0.0)

    gather_pairs(h_ref, (x_lr,), lr_ids, m_own)
    exc = inc_ref[...] + narrow_product(fw_ref, h_ref[...] + f_ref[...])
    vec_ref[0:W, :] = b
    vec_ref[W : 2 * W, :] = u1
    vec_ref[2 * W : 3 * W, :] = exc

    metas = (m_own, m_ud, m_f)
    stack = scaled_by_type(tw_ref, (u1, u1_ud, u1_lr), metas)
    scatter_pairs(g_ref, stack, (own_ids,) * 3, metas)
    u2 = narrow_product(lw_ref, g_ref[...])

    lane, row = lanes(8), lax.broadcasted_iota(jnp.int32, (8, PT), 0)
    gram = jnp.zeros((8, PT), F32)
    for i, (p, q) in enumerate(((b, b), (b, u1), (u1, u1), (b, u2), (u1, u2), (u2, u2))):
        gram = jnp.where(lane == i, jnp.sum(p * q), gram)
    vec_ref[3 * W :, :] = jnp.where(row == 0, gram, m_own[SLOTS : SLOTS + 1, :])


def outer_kernel(tile_ref, own_ref, other_ref, chunk_ref):
    def both(rows):
        return jnp.concatenate([own_ref[rows, :], other_ref[rows, :]], axis=1)

    exc = both(slice(2 * W, 3 * W))
    e_hi, e_lo = split(jnp.concatenate([exc, jnp.zeros((64, 2 * PT), F32)], axis=0))
    v_hi, v_lo = split(both(slice(0, 2 * W)))
    kind = both(slice(3 * W + 1, 3 * W + 2))
    for k in range(2):
        here = kind == (2 * lax.rem(tile_ref[0], 2) + k).astype(F32)
        k_hi = jnp.where(here, v_hi, jnp.zeros_like(v_hi))
        k_lo = jnp.where(here, v_lo, jnp.zeros_like(v_lo))
        out = dot_nt(k_hi, e_hi) + dot_nt(k_lo, e_hi) + dot_nt(k_hi, e_lo)
        for which in range(2):
            for h in range(2):
                block = out[which * W + h * HALF : which * W + (h + 1) * HALF, :]
                edge = block[0:48, PT:] + pltpu.roll(block[48:96, PT:], 64, 1)
                at = (2 * k + h) * 8 * CHUNK + which * 18
                for i in range(18):
                    rows = block[8 * i : 8 * i + 8, 0:PT] if i < 12 else edge[8 * i - 96 : 8 * i - 88]
                    chunk_ref[pl.ds(at + i, 8, CHUNK), :] = rows
    gram = own_ref[3 * W : 3 * W + 1, :] + other_ref[3 * W : 3 * W + 1, :]
    for i in range(36, CHUNK):
        row = gram if i == 36 else jnp.zeros((1, PT), F32)
        chunk_ref[pl.ds(i, 32, CHUNK), :] = jnp.broadcast_to(row, (32, PT))


def spread_kernel(in_ref, out_ref):
    total = jnp.sum(in_ref[...], axis=0)
    for i in range(8):
        out_ref[i] = total


def combine_kernel(in_ref, out_ref, coef_ref):
    total = jnp.sum(in_ref[...], axis=0)
    lane = lanes(1)

    def entry(i):
        return jnp.sum(jnp.where(lane == i, total[36:37, :], 0.0), axis=1, keepdims=True)

    g00, g01, g11, g02, g12, g22 = [entry(i) for i in range(6)]
    alpha = g01 / g00
    beta = jnp.sqrt(g00)
    p2 = g11 - alpha * g01
    pn = jnp.sqrt(p2)
    h00 = 1.0 - alpha
    h10 = pn / beta
    h01 = (g02 - alpha * g01) / (beta * pn)
    qv1 = (g12 - alpha * g11 - alpha * g02 + alpha * alpha * g01) / p2
    h11 = 1.0 - qv1
    n00 = h00 * h00 + h10 * h10
    n01 = h00 * h01 + h10 * h11
    n11 = 1.0 - 2.0 * qv1 + (g22 - 2.0 * alpha * g12 + alpha * alpha * g11) / p2
    r0 = beta * h00
    r1 = beta * h01
    f00 = jnp.sqrt(n00)
    f10 = n01 / f00
    f11 = jnp.sqrt(n11 - f10 * f10)
    y0 = r0 / f00
    y1 = (r1 - f10 * y0) / f11
    w1 = y1 / f11
    w0 = (y0 - f10 * w1) / f00
    c1 = -w1 / pn
    c0 = w0 / beta - c1 * alpha
    mixed = c0 * total[0:18, :] + c1 * total[18:36, :]
    mixed = jnp.concatenate([mixed, jnp.zeros((BACK - 18, PT), F32)] * 2, axis=0)
    for i in range(16):
        out_ref[2 * BACK * i : 2 * BACK * (i + 1), :] = mixed
    coef_ref[0:4, :] = jnp.broadcast_to(c0, (4, PT))
    coef_ref[4:8, :] = jnp.broadcast_to(c1, (4, PT))


def expand_kernel(tile_ref, own_ref, other_ref, vec_ref, coef_ref, out_ref, adj_ref):
    adj_ref[...] = coef_ref[0:1, :] * vec_ref[0:W, :] + coef_ref[4:5, :] * vec_ref[W : 2 * W, :]
    core = lax.rem(tile_ref[0], 2)
    for ref, first in ((own_ref, 2 * core), (other_ref, 2 - 2 * core)):
        for k in range(2):
            for h in range(2):
                base, at = (2 * k + h) * 8 * BACK, h * HALF
                block = jnp.concatenate(
                    [ref[pl.ds(base + i, 8, BACK), :] for i in range(18)], axis=0
                )
                edge = block[96:144, :]
                out_ref[first + k, at : at + HALF, 0:PT] = block[0:HALF, :]
                out_ref[first + k, at : at + 48, PT:W] = edge[:, 0:64]
                out_ref[first + k, at + 48 : at + HALF, PT:W] = pltpu.roll(edge, 64, 1)[:, 0:64]


def call(kernel, shapes, *args, smem=0, whole=0, mib=6, dtype=F32, us=1, **kw):
    return pl.pallas_call(
        kernel,
        out_shape=[
            s if isinstance(s, jax.ShapeDtypeStruct) else jax.ShapeDtypeStruct(s, dtype)
            for s in shapes
        ],
        in_specs=[pl.BlockSpec(memory_space=pltpu.SMEM)] * smem
        + [pl.BlockSpec(memory_space=pltpu.VMEM)] * (len(args) - smem - whole)
        + [pl.BlockSpec(memory_space=pl.ANY)] * whole,
        cost_estimate=pl.CostEstimate(
            flops=us * 10**9, bytes_accessed=us * 3 * 10**6, transcendentals=0
        ),
        compiler_params=pltpu.CompilerParams(vmem_limit_bytes=mib * MIB),
        **kw,
    )(*args)


def swapped(one, two, axis):
    n = math.prod(lax.axis_size(name) for name in axis)
    near = [(i, i ^ 1) for i in range(n)]
    far = [(i, i - 1 if i % 2 == 0 else i + 1) for i in range(1, n - 1)]
    return lax.ppermute(one, axis, near), lax.ppermute(two, axis, far)


def body(
    forward_coeff,
    incident,
    cost_grad,
    tmat_real,
    tmat_imag,
    translation_real,
    translation_imaginary,
    neighbours,
    particle_type,
):
    n_short = lax.axis_size("x") * lax.axis_size("c")
    tile = lax.axis_index(TALL) * n_short + lax.axis_index(FLAT)
    tile = tile.astype(jnp.int32).reshape(1)
    kinds = particle_type.reshape(1, PT)
    (ids,) = call(
        functools.partial(target_ids_kernel, n_short), [(4 * PT, PT)], tile, smem=1, us=4
    )
    one, two = call(
        functools.partial(pack_wide_kernel, n_short),
        [(ROWS + HALF, PT)] * 2,
        tile,
        forward_coeff,
        cost_grad,
        neighbours,
        kinds,
        ids,
        smem=1,
        whole=1,
    )
    x1, x2 = swapped(one, two, TALL)
    one, two = call(
        functools.partial(pack_short_kernel, n_short),
        [(ROWS, PT)] * 2,
        tile,
        forward_coeff,
        cost_grad,
        neighbours,
        kinds,
        x1,
        x2,
        smem=1,
    )
    y1, y2 = swapped(one, two, FLAT)

    tw, lw, fw = call(
        weight_kernel,
        [(2 * W, KINDS * W), (2 * W, 2 * PART), (2 * W, 2 * PART)],
        tmat_real,
        tmat_imag,
        translation_real,
        translation_imaginary,
        mib=16,
        dtype=BF16,
    )

    scratch = [pltpu.VMEM((2 * PART, 2 * PT), BF16)] * 2
    early = call(
        functools.partial(early_kernel, n_short),
        [(W, 2 * PT), jax.ShapeDtypeStruct((2 * W, 3 * PT), BF16)]
        + [jax.ShapeDtypeStruct((2 * PART, 2 * PT), BF16)],
        tile,
        ids,
        cost_grad,
        neighbours,
        kinds,
        x1,
        x2,
        forward_coeff,
        tw,
        lw,
        smem=1,
        mib=24,
        us=4,
        scratch_shapes=scratch,
    )
    (vectors,) = call(
        functools.partial(main_kernel, n_short),
        [(3 * W + 8, PT)],
        tile,
        ids,
        cost_grad,
        neighbours,
        kinds,
        incident,
        x1,
        x2,
        y1,
        y2,
        *early,
        tw,
        lw,
        fw,
        smem=1,
        mib=24,
        us=4,
        scratch_shapes=scratch,
    )
    pair = [(0, 1), (1, 0)]
    partner = lax.ppermute(vectors, "c", pair)
    (chunks,) = call(outer_kernel, [(32 * CHUNK, PT)], tile, vectors, partner, smem=1)
    got = lax.all_to_all(chunks.reshape(32, CHUNK, PT), ("y", "x"), 0, 0)
    (pieces,) = call(spread_kernel, [(8, CHUNK, PT)], got)
    got = lax.all_to_all(pieces, "z", 0, 0)
    mixed, coefs = call(combine_kernel, [(32 * BACK, PT), (8, PT)], got)
    got = lax.all_to_all(mixed.reshape(32, BACK, PT), ("y", "x"), 0, 0)
    half = got.reshape(32 * BACK, PT)
    other = lax.ppermute(half, "c", pair)
    sensitivity, adjoint = call(
        expand_kernel,
        [(KINDS, W, W), (W, PT)],
        tile,
        half,
        other,
        vectors,
        coefs,
        smem=1,
    )
    return (adjoint, sensitivity)


def solution(mesh):
    fine = Mesh(mesh.devices.reshape(8, 8, 4, 2), TALL + FLAT)
    split_in = P(None, TALL + FLAT)
    placed = (split_in, split_in, split_in, P(), P(), P(), P(), split_in, P(TALL + FLAT))
    return jax.shard_map(
        body, mesh=fine, in_specs=placed, out_specs=(split_in, P()), check_vma=False
    )
```

```python
import functools
import math

import jax
import jax.numpy as jnp
from jax import lax
from jax.experimental import pallas as pl
from jax.experimental.pallas import tpu as pltpu
from jax.sharding import Mesh
from jax.sharding import PartitionSpec as P

F32 = jnp.float32
BF16 = jnp.bfloat16
W = 192
HALF = 96
PT = 128
SLOTS = 10
KINDS = 4
META = 16
ROWS = W + META
CHUNK = 40
BACK = 24
TALL = ("z", "y")
FLAT = ("x", "c")
PART = 1024
MIB = 1024 * 1024


def split(x):
    hi = x.astype(BF16)
    return hi, (x - hi.astype(F32)).astype(BF16)


def dot(a, b):
    return lax.dot_general(a, b, (((1,), (0,)), ((), ())), preferred_element_type=F32)


def dot_nt(a, b):
    return lax.dot_general(a, b, (((1,), (1,)), ((), ())), preferred_element_type=F32)


def lanes(rows):
    return lax.broadcasted_iota(jnp.int32, (rows, PT), 1)


def meta_rows(nb_ref, pt_ref):
    return jnp.concatenate(
        [
            (nb_ref[...] + 1).astype(F32),
            pt_ref[...].astype(F32),
            jnp.zeros((META - SLOTS - 1, PT), F32),
        ],
        axis=0,
    )


def even_row(short, tile_ref):
    return lax.rem(lax.div(tile_ref[0], short), 2) == 0


def even_col(tile_ref):
    return lax.rem(tile_ref[0], 2) == 0


def pack_wide_kernel(short, tile_ref, fc_ref, b_ref, nb_ref, pt_ref, _, one_ref, two_ref):
    even = even_row(short, tile_ref)
    meta = meta_rows(nb_ref, pt_ref)
    top, low = fc_ref[0:HALF, :], fc_ref[HALF:W, :]
    first = lanes(HALF) < 64
    for ref in (one_ref, two_ref):
        ref[0:W, :] = b_ref[...]
        ref[W:ROWS, :] = meta
    up = jnp.where(first, pltpu.roll(top, 64, 1), low)
    dn = jnp.where(first, top, pltpu.roll(low, 64, 1))
    one_ref[ROWS : ROWS + HALF, :] = jnp.where(even, up, dn)
    two_ref[ROWS : ROWS + HALF, :] = jnp.where(even, dn, up)


def unpack_fc(up, dn):
    first = lanes(HALF) < 64
    return jnp.concatenate(
        [
            jnp.where(first, dn, pltpu.roll(up, 64, 1)),
            jnp.where(first, pltpu.roll(dn, 64, 1), up),
        ],
        axis=0,
    )


class Tiles:
    def __init__(self, even, one_ref, two_ref):
        self.even, self.one, self.two = even, one_ref, two_ref

    def below(self, rows):
        return jnp.where(self.even, self.two[rows, :], self.one[rows, :])

    def above(self, rows):
        return jnp.where(self.even, self.one[rows, :], self.two[rows, :])


def pack_short_kernel(
    short, tile_ref, fc_ref, b_ref, nb_ref, pt_ref, x1_ref, x2_ref, one_ref, two_ref
):
    wide = Tiles(even_row(short, tile_ref), x1_ref, x2_ref)
    even = even_col(tile_ref)
    half = slice(ROWS, ROWS + HALF)
    first = lanes(META) < 64
    meta = meta_rows(nb_ref, pt_ref)
    fc_ud = unpack_fc(wide.below(half), wide.above(half))

    def part(rows, tiles):
        col = lanes(rows.stop - rows.start) % 32
        up, own, dn, edge, edge_ud = tiles

        def moved(x, shift):
            return pltpu.roll(x, shift, 1) if shift else x

        low = moved(up, 0)
        low = jnp.where(col < 4, low, moved(own, 4))
        low = jnp.where(col < 8, low, moved(dn, 8))
        low = jnp.where(col < 12, low, moved(edge, 12))
        low = jnp.where(col < 14, low, moved(edge_ud, 14))
        high = moved(edge, 114)
        high = jnp.where(col < 18, high, moved(edge_ud, 116))
        high = jnp.where(col < 20, high, moved(up, 120))
        high = jnp.where(col < 24, high, moved(own, 124))
        high = jnp.where(col < 28, high, dn)
        one_ref[rows, :] = jnp.where(even, high, low)
        two_ref[rows, :] = jnp.where(even, low, high)

    v, m = slice(0, W), slice(W, ROWS)
    part(v, (wide.below(v), b_ref[...], wide.above(v), fc_ref[...], fc_ud))
    meta_up, meta_dn = wide.below(m), wide.above(m)
    part(m, (meta_up, meta, meta_dn, meta, jnp.where(first, meta_dn, meta_up)))


def weight_kernel(tr_ref, ti_ref, lr_ref, li_ref, tw_ref, lw_ref, fw_ref):
    def turned(ref):
        n = ref.shape[0]
        fill = -n * HALF % PT
        side = jnp.concatenate([ref[...].reshape(n * HALF, HALF), jnp.zeros((n * HALF, 32), F32)], axis=1)
        if fill:
            side = jnp.concatenate([side, jnp.zeros((fill, PT), F32)], axis=0)
        return split(jnp.transpose(side)[0:HALF, :])

    def beside(ref):
        n = ref.shape[0]
        return split(
            jnp.concatenate([ref[s] for s in range(n)] + [jnp.zeros((HALF, -n * HALF % PT), F32)], axis=1)
        )

    def store(ref, real, imag, sign):
        width = real[0].shape[1]
        for at, re, im in zip((0, W), real, imag):
            ref[at : at + HALF, 0:width] = re
            ref[at : at + HALF, width:] = im if sign > 0 else -im
            ref[at + HALF : at + W, 0:width] = -im if sign > 0 else im
            ref[at + HALF : at + W, width:] = re

    store(tw_ref, turned(tr_ref), turned(ti_ref), 1)
    store(lw_ref, turned(lr_ref), turned(li_ref), 1)
    store(fw_ref, beside(lr_ref), beside(li_ref), -1)


def target_ids(base, row_stride):
    spot = lax.broadcasted_iota(jnp.int32, (4 * PT, PT), 0)
    lane = spot % PT
    row, col = lane // 32, lane % 32
    shift = jnp.where(row < 2, row_stride, -row_stride)
    own = base + lane
    beside = base + row * 32
    lr = jnp.where(
        col < 14,
        beside + PT + col - 12,
        jnp.where(
            col < 16,
            beside + PT + shift + col - 14,
            jnp.where(col < 18, beside - PT + col + 14, beside - PT + shift + col + 12),
        ),
    )
    lr = jnp.where((col >= 12) & (col < 20), lr, -10)
    edge = jnp.where(
        (col < 2) | (col >= 30),
        own,
        jnp.where(col < 4, own - 2 + shift, jnp.where(col >= 28, own + 2 + shift, lr)),
    )
    ids = jnp.where(
        spot < PT,
        own,
        jnp.where(spot < 2 * PT, own + shift, jnp.where(spot < 3 * PT, lr, edge)),
    )
    return jnp.where(ids >= 0, ids + 1, -10).astype(F32)


def target_ids_kernel(short, tile_ref, ids_ref):
    ids_ref[...] = target_ids(tile_ref[0] * PT, short * PT)


def narrow_product(w_ref, both):
    rows = dot(w_ref[0:W, :], both)
    return rows[:, 0:PT] + rows[:, PT:] + dot(w_ref[W : 2 * W, :], both[:, 0:PT])


def product(w_ref, hi, lo):
    rows = dot(w_ref[...], hi)
    return rows[0:W] + rows[W : 2 * W] + dot(w_ref[0:W, :], lo)


def scaled_by_type(tw_ref, blocks, metas):
    his, los = [], []
    for v, meta in zip(blocks, metas):
        hi, lo = split(v)
        kind = meta[SLOTS : SLOTS + 1, :]
        his.append([jnp.where(kind == float(k), hi, jnp.zeros_like(hi)) for k in range(KINDS)])
        los.append([jnp.where(kind == float(k), lo, jnp.zeros_like(lo)) for k in range(KINDS)])

    def by_part(pieces):
        whole = [jnp.concatenate([p[k] for p in pieces], axis=1) for k in range(KINDS)]
        return jnp.concatenate([w[0:HALF] for w in whole] + [w[HALF:W] for w in whole], axis=0)

    s_hi, s_lo = split(product(tw_ref, by_part(his), by_part(los)))
    return jnp.concatenate([s_hi, s_lo], axis=0)


def one_hot(at, meta, s):
    return jnp.where(at == meta[s : s + 1, :], 1.0, 0.0).astype(BF16)


def place(spots, parts, s, lanes_from):
    for (ref, lanes_at), part in zip(spots, parts):
        for half in range(2):
            at = half * PART + s * HALF
            ref[at : at + HALF, lanes_at] = part[half * HALF : (half + 1) * HALF, lanes_from]


def beside(ref):
    return ((ref, slice(0, PT)), (ref, slice(PT, 2 * PT)))


def clear_fill(refs):
    for ref in refs:
        for at in (SLOTS * HALF, PART + SLOTS * HALF):
            rows = PART - SLOTS * HALF
            ref[at : at + rows, :] = jnp.zeros((rows, ref.shape[1]), BF16)


def scatter_pairs(ref, stack, ids, metas):
    for s in range(0, SLOTS, 2):
        pick = jnp.concatenate(
            [
                jnp.concatenate([one_hot(at, meta, t) for at, meta in zip(ids, metas)], axis=1)
                for t in (s, s + 1)
            ],
            axis=0,
        )
        g = dot_nt(stack, pick)
        parts = split(g[0:W] + g[W : 2 * W])
        for t in (0, 1):
            place(beside(ref), parts, s + t, slice(t * PT, (t + 1) * PT))


def gather_pairs(ref, blocks, ids, meta):
    stack = jnp.concatenate(split(jnp.concatenate(blocks, axis=1)), axis=0)
    for s in range(0, SLOTS, 2):
        pick = jnp.concatenate([one_hot(ids, meta, s), one_hot(ids, meta, s + 1)], axis=1)
        g = dot(stack, pick).astype(BF16)
        for t in (0, 1):
            parts = (g[0:W], g[W : 2 * W])
            place(beside(ref), parts, s + t, slice(t * PT, (t + 1) * PT))


def early_kernel(
    short,
    tile_ref,
    ids_ref,
    b_ref,
    nb_ref,
    pt_ref,
    x1_ref,
    x2_ref,
    fc_ref,
    tw_ref,
    lw_ref,
    part_ref,
    stack_ref,
    f_ref,
    ghi_ref,
    glo_ref,
):
    wide = Tiles(even_row(short, tile_ref), x1_ref, x2_ref)
    v, m, half = slice(0, W), slice(W, ROWS), slice(ROWS, ROWS + HALF)
    refs = (ghi_ref, glo_ref)
    ids = ids_ref[0 : 2 * PT, :]
    own = meta_rows(nb_ref, pt_ref)
    metas = (own, wide.below(m), wide.above(m))
    clear_fill(refs + (f_ref,))
    stack = scaled_by_type(tw_ref, (b_ref[...], wide.below(v), wide.above(v)), metas)
    stack_ref[...] = stack
    for s in range(SLOTS):
        pick = jnp.concatenate([one_hot(ids, meta, s) for meta in metas], axis=1)
        g = dot_nt(stack, pick)
        place([(ref, slice(None)) for ref in refs], split(g[0:W] + g[W : 2 * W]), s, slice(None))
    part_ref[...] = product(lw_ref, ghi_ref[...], glo_ref[...])
    fc_ud = unpack_fc(wide.below(half), wide.above(half))
    gather_pairs(f_ref, (fc_ref[...], fc_ud), ids, own)


def main_kernel(
    short,
    tile_ref,
    ids_ref,
    b_ref,
    nb_ref,
    pt_ref,
    inc_ref,
    x1_ref,
    x2_ref,
    y1_ref,
    y2_ref,
    part_ref,
    stack_ref,
    f_ref,
    tw_ref,
    lw_ref,
    fw_ref,
    vec_ref,
    g_ref,
    h_ref,
):
    rows = Tiles(even_row(short, tile_ref), x1_ref, x2_ref)
    cols = Tiles(even_col(tile_ref), y1_ref, y2_ref)
    v, m = slice(0, W), slice(W, ROWS)
    ids = ids_ref[...]
    col = lanes(META) % 32
    b = b_ref[...]
    m_own = meta_rows(nb_ref, pt_ref)
    m_up, m_dn = rows.below(m), rows.above(m)
    m_ud = jnp.where(lanes(META) < 64, m_dn, m_up)
    m_lr = jnp.where(col >= 16, cols.below(m), cols.above(m))
    spot = lanes(W) % 32
    x_lr = jnp.where(spot >= 16, cols.below(v), cols.above(v))
    b_zone = (col < 12) | (col >= 20)
    row_id = lax.broadcasted_iota(jnp.int32, (META, PT), 0)
    m_b = jnp.where(b_zone | (row_id >= SLOTS), m_lr, 0.0)
    m_f = jnp.where(b_zone & (row_id < SLOTS), 0.0, m_lr)
    clear_fill((g_ref, h_ref))
    first, second = slice(0, PT), slice(PT, 2 * PT)
    own_ids, lr_ids, edge_ids = ids[0:PT, :], ids[2 * PT : 3 * PT, :], ids[3 * PT :, :]

    stack = jnp.concatenate([stack_ref[...], scaled_by_type(tw_ref, (x_lr,), (m_b,))], axis=1)
    scatter_pairs(g_ref, stack, (lr_ids, lr_ids, lr_ids, edge_ids), (m_own, m_up, m_dn, m_b))
    edge = narrow_product(lw_ref, g_ref[...])
    left, right = spot < 2, spot >= 30
    u1 = part_ref[:, first] + jnp.where(left | right, edge, 0.0)
    u1_ud = part_ref[:, second] + jnp.where(
        left, pltpu.roll(edge, PT - 2, 1), jnp.where(right, pltpu.roll(edge, 2, 1), 0.0)
    )
    u1_lr = jnp.where((spot >= 12) & (spot < 20), edge, 0.0)

    gather_pairs(h_ref, (x_lr,), lr_ids, m_own)
    exc = inc_ref[...] + narrow_product(fw_ref, h_ref[...] + f_ref[...])
    vec_ref[0:W, :] = b
    vec_ref[W : 2 * W, :] = u1
    vec_ref[2 * W : 3 * W, :] = exc

    metas = (m_own, m_ud, m_f)
    stack = scaled_by_type(tw_ref, (u1, u1_ud, u1_lr), metas)
    scatter_pairs(g_ref, stack, (own_ids,) * 3, metas)
    u2 = narrow_product(lw_ref, g_ref[...])

    lane, row = lanes(8), lax.broadcasted_iota(jnp.int32, (8, PT), 0)
    gram = jnp.zeros((8, PT), F32)
    for i, (p, q) in enumerate(((b, b), (b, u1), (u1, u1), (b, u2), (u1, u2), (u2, u2))):
        gram = jnp.where(lane == i, jnp.sum(p * q), gram)
    vec_ref[3 * W :, :] = jnp.where(row == 0, gram, m_own[SLOTS : SLOTS + 1, :])


def outer_kernel(tile_ref, own_ref, other_ref, chunk_ref):
    def both(rows):
        return jnp.concatenate([own_ref[rows, :], other_ref[rows, :]], axis=1)

    exc = both(slice(2 * W, 3 * W))
    e_hi, e_lo = split(jnp.concatenate([exc, jnp.zeros((64, 2 * PT), F32)], axis=0))
    v_hi, v_lo = split(both(slice(0, 2 * W)))
    kind = both(slice(3 * W + 1, 3 * W + 2))
    for k in range(2):
        here = kind == (2 * lax.rem(tile_ref[0], 2) + k).astype(F32)
        k_hi = jnp.where(here, v_hi, jnp.zeros_like(v_hi))
        k_lo = jnp.where(here, v_lo, jnp.zeros_like(v_lo))
        out = dot_nt(k_hi, e_hi) + dot_nt(k_lo, e_hi) + dot_nt(k_hi, e_lo)
        for which in range(2):
            for h in range(2):
                block = out[which * W + h * HALF : which * W + (h + 1) * HALF, :]
                edge = block[0:48, PT:] + pltpu.roll(block[48:96, PT:], 64, 1)
                at = (2 * k + h) * 2 * CHUNK + which * 18
                for i in range(18):
                    rows = block[8 * i : 8 * i + 8, 0:PT] if i < 12 else edge[8 * i - 96 : 8 * i - 88]
                    chunk_ref[pl.ds(at + i, 4, 8 * CHUNK), :] = rows[0:4]
                    chunk_ref[pl.ds(at + CHUNK + i, 4, 8 * CHUNK), :] = rows[4:8]
    gram = own_ref[3 * W : 3 * W + 1, :] + other_ref[3 * W : 3 * W + 1, :]
    for i in range(36, CHUNK):
        row = gram if i == 36 else jnp.zeros((1, PT), F32)
        chunk_ref[pl.ds(i, 32, CHUNK), :] = jnp.broadcast_to(row, (32, PT))


def spread_kernel(in_ref, out_ref):
    total = jnp.sum(in_ref[...], axis=0)
    for i in range(8):
        out_ref[i] = total


def sum_kernel(in_ref, out_ref):
    out_ref[...] = jnp.sum(in_ref[...], axis=0)


def combine_kernel(in_ref, out_ref, coef_ref):
    total = jnp.sum(in_ref[...], axis=0)
    lane = lanes(1)

    def entry(i):
        return jnp.sum(jnp.where(lane == i, total[36:37, :], 0.0), axis=1, keepdims=True)

    g00, g01, g11, g02, g12, g22 = [entry(i) for i in range(6)]
    alpha = g01 / g00
    beta = jnp.sqrt(g00)
    p2 = g11 - alpha * g01
    pn = jnp.sqrt(p2)
    h00 = 1.0 - alpha
    h10 = pn / beta
    h01 = (g02 - alpha * g01) / (beta * pn)
    qv1 = (g12 - alpha * g11 - alpha * g02 + alpha * alpha * g01) / p2
    h11 = 1.0 - qv1
    n00 = h00 * h00 + h10 * h10
    n01 = h00 * h01 + h10 * h11
    n11 = 1.0 - 2.0 * qv1 + (g22 - 2.0 * alpha * g12 + alpha * alpha * g11) / p2
    r0 = beta * h00
    r1 = beta * h01
    f00 = jnp.sqrt(n00)
    f10 = n01 / f00
    f11 = jnp.sqrt(n11 - f10 * f10)
    y0 = r0 / f00
    y1 = (r1 - f10 * y0) / f11
    w1 = y1 / f11
    w0 = (y0 - f10 * w1) / f00
    c1 = -w1 / pn
    c0 = w0 / beta - c1 * alpha
    mixed = c0 * total[0:18, :] + c1 * total[18:36, :]
    mixed = jnp.concatenate([mixed, jnp.zeros((BACK - 18, PT), F32)] * 2, axis=0)
    for i in range(16):
        out_ref[2 * BACK * i : 2 * BACK * (i + 1), :] = mixed
    coef_ref[0:4, :] = jnp.broadcast_to(c0, (4, PT))
    coef_ref[4:8, :] = jnp.broadcast_to(c1, (4, PT))


def expand_kernel(tile_ref, own_ref, other_ref, vec_ref, coef_ref, out_ref, adj_ref):
    adj_ref[...] = coef_ref[0:1, :] * vec_ref[0:W, :] + coef_ref[4:5, :] * vec_ref[W : 2 * W, :]
    core = lax.rem(tile_ref[0], 2)
    for ref, first in ((own_ref, 2 * core), (other_ref, 2 - 2 * core)):
        for k in range(2):
            for h in range(2):
                base, at = (2 * k + h) * 8 * BACK, h * HALF
                block = jnp.concatenate(
                    [ref[pl.ds(base + i, 8, BACK), :] for i in range(18)], axis=0
                )
                edge = block[96:144, :]
                out_ref[first + k, at : at + HALF, 0:PT] = block[0:HALF, :]
                out_ref[first + k, at : at + 48, PT:W] = edge[:, 0:64]
                out_ref[first + k, at + 48 : at + HALF, PT:W] = pltpu.roll(edge, 64, 1)[:, 0:64]


def call(kernel, shapes, *args, smem=0, whole=0, mib=6, dtype=F32, us=1, **kw):
    return pl.pallas_call(
        kernel,
        out_shape=[
            s if isinstance(s, jax.ShapeDtypeStruct) else jax.ShapeDtypeStruct(s, dtype)
            for s in shapes
        ],
        in_specs=[pl.BlockSpec(memory_space=pltpu.SMEM)] * smem
        + [pl.BlockSpec(memory_space=pltpu.VMEM)] * (len(args) - smem - whole)
        + [pl.BlockSpec(memory_space=pl.ANY)] * whole,
        cost_estimate=pl.CostEstimate(
            flops=us * 10**9, bytes_accessed=us * 3 * 10**6, transcendentals=0
        ),
        compiler_params=pltpu.CompilerParams(vmem_limit_bytes=mib * MIB),
        **kw,
    )(*args)


def swapped(one, two, axis):
    n = math.prod(lax.axis_size(name) for name in axis)
    near = [(i, i ^ 1) for i in range(n)]
    far = [(i, i - 1 if i % 2 == 0 else i + 1) for i in range(1, n - 1)]
    return lax.ppermute(one, axis, near), lax.ppermute(two, axis, far)


def body(
    forward_coeff,
    incident,
    cost_grad,
    tmat_real,
    tmat_imag,
    translation_real,
    translation_imaginary,
    neighbours,
    particle_type,
):
    n_short = lax.axis_size("x") * lax.axis_size("c")
    tile = lax.axis_index(TALL) * n_short + lax.axis_index(FLAT)
    tile = tile.astype(jnp.int32).reshape(1)
    kinds = particle_type.reshape(1, PT)
    (ids,) = call(
        functools.partial(target_ids_kernel, n_short), [(4 * PT, PT)], tile, smem=1, us=4
    )
    one, two = call(
        functools.partial(pack_wide_kernel, n_short),
        [(ROWS + HALF, PT)] * 2,
        tile,
        forward_coeff,
        cost_grad,
        neighbours,
        kinds,
        ids,
        smem=1,
        whole=1,
    )
    x1, x2 = swapped(one, two, TALL)
    one, two = call(
        functools.partial(pack_short_kernel, n_short),
        [(ROWS, PT)] * 2,
        tile,
        forward_coeff,
        cost_grad,
        neighbours,
        kinds,
        x1,
        x2,
        smem=1,
    )
    y1, y2 = swapped(one, two, FLAT)

    tw, lw, fw = call(
        weight_kernel,
        [(2 * W, KINDS * W), (2 * W, 2 * PART), (2 * W, 2 * PART)],
        tmat_real,
        tmat_imag,
        translation_real,
        translation_imaginary,
        mib=16,
        dtype=BF16,
    )

    scratch = [pltpu.VMEM((2 * PART, 2 * PT), BF16)] * 2
    early = call(
        functools.partial(early_kernel, n_short),
        [(W, 2 * PT), jax.ShapeDtypeStruct((2 * W, 3 * PT), BF16)]
        + [jax.ShapeDtypeStruct((2 * PART, 2 * PT), BF16)],
        tile,
        ids,
        cost_grad,
        neighbours,
        kinds,
        x1,
        x2,
        forward_coeff,
        tw,
        lw,
        smem=1,
        mib=24,
        us=4,
        scratch_shapes=scratch,
    )
    (vectors,) = call(
        functools.partial(main_kernel, n_short),
        [(3 * W + 8, PT)],
        tile,
        ids,
        cost_grad,
        neighbours,
        kinds,
        incident,
        x1,
        x2,
        y1,
        y2,
        *early,
        tw,
        lw,
        fw,
        smem=1,
        mib=24,
        us=4,
        scratch_shapes=scratch,
    )
    pair = [(0, 1), (1, 0)]
    partner = lax.ppermute(vectors, "c", pair)
    (chunks,) = call(outer_kernel, [(32 * CHUNK, PT)], tile, vectors, partner, smem=1)
    got = lax.all_to_all(chunks.reshape(4, 8 * CHUNK, PT), "x", 0, 0)
    (part,) = call(sum_kernel, [(8 * CHUNK, PT)], got)
    got = lax.all_to_all(part.reshape(8, CHUNK, PT), "y", 0, 0)
    (pieces,) = call(spread_kernel, [(8, CHUNK, PT)], got)
    got = lax.all_to_all(pieces, "z", 0, 0)
    mixed, coefs = call(combine_kernel, [(32 * BACK, PT), (8, PT)], got)
    got = lax.all_to_all(mixed.reshape(32, BACK, PT), ("y", "x"), 0, 0)
    half = got.reshape(32 * BACK, PT)
    other = lax.ppermute(half, "c", pair)
    sensitivity, adjoint = call(
        expand_kernel,
        [(KINDS, W, W), (W, PT)],
        tile,
        half,
        other,
        vectors,
        coefs,
        smem=1,
    )
    return (adjoint, sensitivity)


def solution(mesh):
    fine = Mesh(mesh.devices.reshape(8, 8, 4, 2), TALL + FLAT)
    split_in = P(None, TALL + FLAT)
    placed = (split_in, split_in, split_in, P(), P(), P(), P(), split_in, P(TALL + FLAT))
    return jax.shard_map(
        body, mesh=fine, in_specs=placed, out_specs=(split_in, P()), check_vma=False
    )
```

```python
import functools
import math

import jax
import jax.numpy as jnp
from jax import lax
from jax.experimental import pallas as pl
from jax.experimental.pallas import tpu as pltpu
from jax.sharding import Mesh
from jax.sharding import PartitionSpec as P

F32 = jnp.float32
BF16 = jnp.bfloat16
W = 192
HALF = 96
PT = 128
SLOTS = 10
KINDS = 4
META = 16
ROWS = W + META
CHUNK = 40
BACK = 24
TALL = ("z", "y")
FLAT = ("x", "c")
PART = 1024
MIB = 1024 * 1024


def split(x):
    hi = x.astype(BF16)
    return hi, (x - hi.astype(F32)).astype(BF16)


def dot(a, b):
    return lax.dot_general(a, b, (((1,), (0,)), ((), ())), preferred_element_type=F32)


def dot_nt(a, b):
    return lax.dot_general(a, b, (((1,), (1,)), ((), ())), preferred_element_type=F32)


def lanes(rows):
    return lax.broadcasted_iota(jnp.int32, (rows, PT), 1)


def meta_rows(nb_ref, pt_ref):
    return jnp.concatenate(
        [
            (nb_ref[...] + 1).astype(F32),
            pt_ref[...].astype(F32),
            jnp.zeros((META - SLOTS - 1, PT), F32),
        ],
        axis=0,
    )


def even_row(short, tile_ref):
    return lax.rem(lax.div(tile_ref[0], short), 2) == 0


def even_col(tile_ref):
    return lax.rem(tile_ref[0], 2) == 0


def pack_wide_kernel(short, tile_ref, fc_ref, b_ref, nb_ref, pt_ref, _, one_ref, two_ref):
    even = even_row(short, tile_ref)
    meta = meta_rows(nb_ref, pt_ref)
    top, low = fc_ref[0:HALF, :], fc_ref[HALF:W, :]
    first = lanes(HALF) < 64
    for ref in (one_ref, two_ref):
        ref[0:W, :] = b_ref[...]
        ref[W:ROWS, :] = meta
    up = jnp.where(first, pltpu.roll(top, 64, 1), low)
    dn = jnp.where(first, top, pltpu.roll(low, 64, 1))
    one_ref[ROWS : ROWS + HALF, :] = jnp.where(even, up, dn)
    two_ref[ROWS : ROWS + HALF, :] = jnp.where(even, dn, up)


def unpack_fc(up, dn):
    first = lanes(HALF) < 64
    return jnp.concatenate(
        [
            jnp.where(first, dn, pltpu.roll(up, 64, 1)),
            jnp.where(first, pltpu.roll(dn, 64, 1), up),
        ],
        axis=0,
    )


class Tiles:
    def __init__(self, even, one_ref, two_ref):
        self.even, self.one, self.two = even, one_ref, two_ref

    def below(self, rows):
        return jnp.where(self.even, self.two[rows, :], self.one[rows, :])

    def above(self, rows):
        return jnp.where(self.even, self.one[rows, :], self.two[rows, :])


def pack_short_kernel(
    short, tile_ref, fc_ref, b_ref, nb_ref, pt_ref, x1_ref, x2_ref, one_ref, two_ref
):
    wide = Tiles(even_row(short, tile_ref), x1_ref, x2_ref)
    even = even_col(tile_ref)
    half = slice(ROWS, ROWS + HALF)
    first = lanes(META) < 64
    meta = meta_rows(nb_ref, pt_ref)
    fc_ud = unpack_fc(wide.below(half), wide.above(half))

    def part(rows, tiles):
        col = lanes(rows.stop - rows.start) % 32
        up, own, dn, edge, edge_ud = tiles

        def moved(x, shift):
            return pltpu.roll(x, shift, 1) if shift else x

        low = moved(up, 0)
        low = jnp.where(col < 4, low, moved(own, 4))
        low = jnp.where(col < 8, low, moved(dn, 8))
        low = jnp.where(col < 12, low, moved(edge, 12))
        low = jnp.where(col < 14, low, moved(edge_ud, 14))
        high = moved(edge, 114)
        high = jnp.where(col < 18, high, moved(edge_ud, 116))
        high = jnp.where(col < 20, high, moved(up, 120))
        high = jnp.where(col < 24, high, moved(own, 124))
        high = jnp.where(col < 28, high, dn)
        one_ref[rows, :] = jnp.where(even, high, low)
        two_ref[rows, :] = jnp.where(even, low, high)

    v, m = slice(0, W), slice(W, ROWS)
    part(v, (wide.below(v), b_ref[...], wide.above(v), fc_ref[...], fc_ud))
    meta_up, meta_dn = wide.below(m), wide.above(m)
    part(m, (meta_up, meta, meta_dn, meta, jnp.where(first, meta_dn, meta_up)))


def weight_kernel(tr_ref, ti_ref, lr_ref, li_ref, tw_ref, lw_ref, fw_ref):
    def turned(ref):
        n = ref.shape[0]
        fill = -n * HALF % PT
        side = jnp.concatenate([ref[...].reshape(n * HALF, HALF), jnp.zeros((n * HALF, 32), F32)], axis=1)
        if fill:
            side = jnp.concatenate([side, jnp.zeros((fill, PT), F32)], axis=0)
        return split(jnp.transpose(side)[0:HALF, :])

    def beside(ref):
        n = ref.shape[0]
        return split(
            jnp.concatenate([ref[s] for s in range(n)] + [jnp.zeros((HALF, -n * HALF % PT), F32)], axis=1)
        )

    def store(ref, real, imag, sign):
        width = real[0].shape[1]
        for at, re, im in zip((0, W), real, imag):
            ref[at : at + HALF, 0:width] = re
            ref[at : at + HALF, width:] = im if sign > 0 else -im
            ref[at + HALF : at + W, 0:width] = -im if sign > 0 else im
            ref[at + HALF : at + W, width:] = re

    store(tw_ref, turned(tr_ref), turned(ti_ref), 1)
    store(lw_ref, turned(lr_ref), turned(li_ref), 1)
    store(fw_ref, beside(lr_ref), beside(li_ref), -1)


def target_ids(base, row_stride):
    spot = lax.broadcasted_iota(jnp.int32, (4 * PT, PT), 0)
    lane = spot % PT
    row, col = lane // 32, lane % 32
    shift = jnp.where(row < 2, row_stride, -row_stride)
    own = base + lane
    beside = base + row * 32
    lr = jnp.where(
        col < 14,
        beside + PT + col - 12,
        jnp.where(
            col < 16,
            beside + PT + shift + col - 14,
            jnp.where(col < 18, beside - PT + col + 14, beside - PT + shift + col + 12),
        ),
    )
    lr = jnp.where((col >= 12) & (col < 20), lr, -10)
    edge = jnp.where(
        (col < 2) | (col >= 30),
        own,
        jnp.where(col < 4, own - 2 + shift, jnp.where(col >= 28, own + 2 + shift, lr)),
    )
    ids = jnp.where(
        spot < PT,
        own,
        jnp.where(spot < 2 * PT, own + shift, jnp.where(spot < 3 * PT, lr, edge)),
    )
    return jnp.where(ids >= 0, ids + 1, -10).astype(F32)


def target_ids_kernel(short, tile_ref, ids_ref):
    ids_ref[...] = target_ids(tile_ref[0] * PT, short * PT)


def narrow_product(w_ref, both):
    n = both.shape[1] // 2
    rows = dot(w_ref[0:W, :], both)
    return rows[:, 0:n] + rows[:, n:] + dot(w_ref[W : 2 * W, :], both[:, 0:n])


def product(w_ref, hi, lo):
    rows = dot(w_ref[...], hi)
    return rows[0:W] + rows[W : 2 * W] + dot(w_ref[0:W, :], lo)


def scaled_by_type(tw_ref, blocks, metas):
    his, los = [], []
    for v, meta in zip(blocks, metas):
        hi, lo = split(v)
        kind = meta[SLOTS : SLOTS + 1, :]
        his.append([jnp.where(kind == float(k), hi, jnp.zeros_like(hi)) for k in range(KINDS)])
        los.append([jnp.where(kind == float(k), lo, jnp.zeros_like(lo)) for k in range(KINDS)])

    def by_part(pieces):
        whole = [jnp.concatenate([p[k] for p in pieces], axis=1) for k in range(KINDS)]
        return jnp.concatenate([w[0:HALF] for w in whole] + [w[HALF:W] for w in whole], axis=0)

    s_hi, s_lo = split(narrow_product(tw_ref, jnp.concatenate([by_part(his), by_part(los)], axis=1)))
    return jnp.concatenate([s_hi, s_lo], axis=0)


def one_hot(at, meta, s):
    return jnp.where(at == meta[s : s + 1, :], 1.0, 0.0).astype(BF16)


def place(spots, parts, s, lanes_from):
    for (ref, lanes_at), part in zip(spots, parts):
        for half in range(2):
            at = half * PART + s * HALF
            ref[at : at + HALF, lanes_at] = part[half * HALF : (half + 1) * HALF, lanes_from]


def beside(ref):
    return ((ref, slice(0, PT)), (ref, slice(PT, 2 * PT)))


def clear_fill(refs):
    for ref in refs:
        for at in (SLOTS * HALF, PART + SLOTS * HALF):
            rows = PART - SLOTS * HALF
            ref[at : at + rows, :] = jnp.zeros((rows, ref.shape[1]), BF16)


def scatter_pairs(ref, stack, ids, metas, start_ref=None):
    for s in range(0, SLOTS, 2):
        pick = jnp.concatenate(
            [
                jnp.concatenate([one_hot(at, meta, t) for at, meta in zip(ids, metas)], axis=1)
                for t in (s, s + 1)
            ],
            axis=0,
        )
        g = dot_nt(stack, pick)
        g = g[0:W] + g[W : 2 * W]
        if start_ref is not None:
            g = g + start_ref[s * HALF : s * HALF + W, :]
        parts = split(g)
        for t in (0, 1):
            place(beside(ref), parts, s + t, slice(t * PT, (t + 1) * PT))


def gather_pairs(ref, blocks, ids, meta):
    stack = jnp.concatenate(split(jnp.concatenate(blocks, axis=1)), axis=0)
    for s in range(0, SLOTS, 2):
        pick = jnp.concatenate([one_hot(ids, meta, s), one_hot(ids, meta, s + 1)], axis=1)
        g = dot(stack, pick).astype(BF16)
        for t in (0, 1):
            parts = (g[0:W], g[W : 2 * W])
            place(beside(ref), parts, s + t, slice(t * PT, (t + 1) * PT))


def first_kernel(ids_ref, b_ref, nb_ref, pt_ref, tw_ref, stack_ref, sum_ref):
    ids = ids_ref[0 : 2 * PT, :]
    own = meta_rows(nb_ref, pt_ref)
    stack = scaled_by_type(tw_ref, (b_ref[...],), (own,))
    stack_ref[...] = stack
    for s in range(SLOTS):
        g = dot_nt(stack, one_hot(ids, own, s))
        sum_ref[s * W : (s + 1) * W, :] = g[0:W] + g[W : 2 * W]


def early_kernel(
    short,
    tile_ref,
    ids_ref,
    own_ref,
    sum_ref,
    nb_ref,
    pt_ref,
    x1_ref,
    x2_ref,
    fc_ref,
    tw_ref,
    lw_ref,
    part_ref,
    edge_ref,
    f_ref,
    ghi_ref,
    glo_ref,
):
    wide = Tiles(even_row(short, tile_ref), x1_ref, x2_ref)
    v, m, half = slice(0, W), slice(W, ROWS), slice(ROWS, ROWS + HALF)
    refs = (ghi_ref, glo_ref)
    ids, lr_ids = ids_ref[0 : 2 * PT, :], ids_ref[2 * PT : 3 * PT, :]
    own = meta_rows(nb_ref, pt_ref)
    metas = (wide.below(m), wide.above(m))
    clear_fill(refs + (f_ref,))
    stack = scaled_by_type(tw_ref, (wide.below(v), wide.above(v)), metas)
    for s in range(SLOTS):
        pick = jnp.concatenate([one_hot(ids, meta, s) for meta in metas], axis=1)
        g = dot_nt(stack, pick)
        g = g[0:W] + g[W : 2 * W] + sum_ref[s * W : (s + 1) * W, :]
        place([(ref, slice(None)) for ref in refs], split(g), s, slice(None))
    part_ref[...] = product(lw_ref, ghi_ref[...], glo_ref[...])
    stack = jnp.concatenate([own_ref[...], stack], axis=1)
    for s in range(0, SLOTS, 2):
        pick = jnp.concatenate(
            [
                jnp.concatenate([one_hot(lr_ids, meta, t) for meta in (own,) + metas], axis=1)
                for t in (s, s + 1)
            ],
            axis=0,
        )
        g = dot_nt(stack, pick)
        edge_ref[s * HALF : s * HALF + W, :] = g[0:W] + g[W : 2 * W]
    fc_ud = unpack_fc(wide.below(half), wide.above(half))
    gather_pairs(f_ref, (fc_ref[...], fc_ud), ids, own)


def main_kernel(
    short,
    tile_ref,
    ids_ref,
    b_ref,
    nb_ref,
    pt_ref,
    inc_ref,
    x1_ref,
    x2_ref,
    y1_ref,
    y2_ref,
    part_ref,
    edge_ref,
    f_ref,
    tw_ref,
    lw_ref,
    fw_ref,
    vec_ref,
    g_ref,
    h_ref,
):
    rows = Tiles(even_row(short, tile_ref), x1_ref, x2_ref)
    cols = Tiles(even_col(tile_ref), y1_ref, y2_ref)
    v, m = slice(0, W), slice(W, ROWS)
    ids = ids_ref[...]
    col = lanes(META) % 32
    b = b_ref[...]
    m_own = meta_rows(nb_ref, pt_ref)
    m_up, m_dn = rows.below(m), rows.above(m)
    m_ud = jnp.where(lanes(META) < 64, m_dn, m_up)
    m_lr = jnp.where(col >= 16, cols.below(m), cols.above(m))
    spot = lanes(W) % 32
    x_lr = jnp.where(spot >= 16, cols.below(v), cols.above(v))
    b_zone = (col < 12) | (col >= 20)
    row_id = lax.broadcasted_iota(jnp.int32, (META, PT), 0)
    m_b = jnp.where(b_zone | (row_id >= SLOTS), m_lr, 0.0)
    m_f = jnp.where(b_zone & (row_id < SLOTS), 0.0, m_lr)
    clear_fill((g_ref, h_ref))
    first, second = slice(0, PT), slice(PT, 2 * PT)
    own_ids, lr_ids, edge_ids = ids[0:PT, :], ids[2 * PT : 3 * PT, :], ids[3 * PT :, :]

    stack = scaled_by_type(tw_ref, (x_lr,), (m_b,))
    scatter_pairs(g_ref, stack, (edge_ids,), (m_b,), edge_ref)
    edge = narrow_product(lw_ref, g_ref[...])
    left, right = spot < 2, spot >= 30
    u1 = part_ref[:, first] + jnp.where(left | right, edge, 0.0)
    u1_ud = part_ref[:, second] + jnp.where(
        left, pltpu.roll(edge, PT - 2, 1), jnp.where(right, pltpu.roll(edge, 2, 1), 0.0)
    )
    u1_lr = jnp.where((spot >= 12) & (spot < 20), edge, 0.0)

    gather_pairs(h_ref, (x_lr,), lr_ids, m_own)
    exc = inc_ref[...] + narrow_product(fw_ref, h_ref[...] + f_ref[...])
    vec_ref[0:W, :] = b
    vec_ref[W : 2 * W, :] = u1
    vec_ref[2 * W : 3 * W, :] = exc

    metas = (m_own, m_ud, m_f)
    stack = scaled_by_type(tw_ref, (u1, u1_ud, u1_lr), metas)
    scatter_pairs(g_ref, stack, (own_ids,) * 3, metas)
    u2 = narrow_product(lw_ref, g_ref[...])

    lane, row = lanes(8), lax.broadcasted_iota(jnp.int32, (8, PT), 0)
    gram = jnp.zeros((8, PT), F32)
    for i, (p, q) in enumerate(((b, b), (b, u1), (u1, u1), (b, u2), (u1, u2), (u2, u2))):
        gram = jnp.where(lane == i, jnp.sum(p * q), gram)
    vec_ref[3 * W :, :] = jnp.where(row == 0, gram, m_own[SLOTS : SLOTS + 1, :])


def outer_kernel(tile_ref, own_ref, other_ref, chunk_ref):
    def both(rows):
        return jnp.concatenate([own_ref[rows, :], other_ref[rows, :]], axis=1)

    exc = both(slice(2 * W, 3 * W))
    e_hi, e_lo = split(jnp.concatenate([exc, jnp.zeros((64, 2 * PT), F32)], axis=0))
    v_hi, v_lo = split(both(slice(0, 2 * W)))
    kind = both(slice(3 * W + 1, 3 * W + 2))
    for k in range(2):
        here = kind == (2 * lax.rem(tile_ref[0], 2) + k).astype(F32)
        k_hi = jnp.where(here, v_hi, jnp.zeros_like(v_hi))
        k_lo = jnp.where(here, v_lo, jnp.zeros_like(v_lo))
        out = dot_nt(k_hi, e_hi) + dot_nt(k_lo, e_hi) + dot_nt(k_hi, e_lo)
        for which in range(2):
            for h in range(2):
                block = out[which * W + h * HALF : which * W + (h + 1) * HALF, :]
                edge = block[0:48, PT:] + pltpu.roll(block[48:96, PT:], 64, 1)
                at = (2 * k + h) * 2 * CHUNK + which * 18
                for i in range(18):
                    rows = block[8 * i : 8 * i + 8, 0:PT] if i < 12 else edge[8 * i - 96 : 8 * i - 88]
                    chunk_ref[pl.ds(at + i, 4, 8 * CHUNK), :] = rows[0:4]
                    chunk_ref[pl.ds(at + CHUNK + i, 4, 8 * CHUNK), :] = rows[4:8]
    gram = own_ref[3 * W : 3 * W + 1, :] + other_ref[3 * W : 3 * W + 1, :]
    for i in range(36, CHUNK):
        row = gram if i == 36 else jnp.zeros((1, PT), F32)
        chunk_ref[pl.ds(i, 32, CHUNK), :] = jnp.broadcast_to(row, (32, PT))


def spread_kernel(in_ref, out_ref):
    total = jnp.sum(in_ref[...], axis=0)
    for i in range(8):
        out_ref[i] = total


def sum_kernel(in_ref, out_ref):
    out_ref[...] = jnp.sum(in_ref[...], axis=0)


def combine_kernel(in_ref, out_ref, coef_ref):
    total = jnp.sum(in_ref[...], axis=0)
    lane = lanes(1)

    def entry(i):
        return jnp.sum(jnp.where(lane == i, total[36:37, :], 0.0), axis=1, keepdims=True)

    g00, g01, g11, g02, g12, g22 = [entry(i) for i in range(6)]
    alpha = g01 / g00
    beta = jnp.sqrt(g00)
    p2 = g11 - alpha * g01
    pn = jnp.sqrt(p2)
    h00 = 1.0 - alpha
    h10 = pn / beta
    h01 = (g02 - alpha * g01) / (beta * pn)
    qv1 = (g12 - alpha * g11 - alpha * g02 + alpha * alpha * g01) / p2
    h11 = 1.0 - qv1
    n00 = h00 * h00 + h10 * h10
    n01 = h00 * h01 + h10 * h11
    n11 = 1.0 - 2.0 * qv1 + (g22 - 2.0 * alpha * g12 + alpha * alpha * g11) / p2
    r0 = beta * h00
    r1 = beta * h01
    f00 = jnp.sqrt(n00)
    f10 = n01 / f00
    f11 = jnp.sqrt(n11 - f10 * f10)
    y0 = r0 / f00
    y1 = (r1 - f10 * y0) / f11
    w1 = y1 / f11
    w0 = (y0 - f10 * w1) / f00
    c1 = -w1 / pn
    c0 = w0 / beta - c1 * alpha
    mixed = c0 * total[0:18, :] + c1 * total[18:36, :]
    mixed = jnp.concatenate([mixed, jnp.zeros((BACK - 18, PT), F32)] * 2, axis=0)
    for i in range(16):
        out_ref[2 * BACK * i : 2 * BACK * (i + 1), :] = mixed
    coef_ref[0:4, :] = jnp.broadcast_to(c0, (4, PT))
    coef_ref[4:8, :] = jnp.broadcast_to(c1, (4, PT))


def expand_kernel(tile_ref, own_ref, other_ref, vec_ref, coef_ref, out_ref, adj_ref):
    adj_ref[...] = coef_ref[0:1, :] * vec_ref[0:W, :] + coef_ref[4:5, :] * vec_ref[W : 2 * W, :]
    core = lax.rem(tile_ref[0], 2)
    for ref, first in ((own_ref, 2 * core), (other_ref, 2 - 2 * core)):
        for k in range(2):
            for h in range(2):
                base, at = (2 * k + h) * 8 * BACK, h * HALF
                block = jnp.concatenate(
                    [ref[pl.ds(base + i, 8, BACK), :] for i in range(18)], axis=0
                )
                edge = block[96:144, :]
                out_ref[first + k, at : at + HALF, 0:PT] = block[0:HALF, :]
                out_ref[first + k, at : at + 48, PT:W] = edge[:, 0:64]
                out_ref[first + k, at + 48 : at + HALF, PT:W] = pltpu.roll(edge, 64, 1)[:, 0:64]


def call(kernel, shapes, *args, smem=0, whole=0, mib=6, dtype=F32, us=1, **kw):
    return pl.pallas_call(
        kernel,
        out_shape=[
            s if isinstance(s, jax.ShapeDtypeStruct) else jax.ShapeDtypeStruct(s, dtype)
            for s in shapes
        ],
        in_specs=[pl.BlockSpec(memory_space=pltpu.SMEM)] * smem
        + [pl.BlockSpec(memory_space=pltpu.VMEM)] * (len(args) - smem - whole)
        + [pl.BlockSpec(memory_space=pl.ANY)] * whole,
        cost_estimate=pl.CostEstimate(
            flops=us * 10**9, bytes_accessed=us * 3 * 10**6, transcendentals=0
        ),
        compiler_params=pltpu.CompilerParams(vmem_limit_bytes=mib * MIB),
        **kw,
    )(*args)


def swapped(one, two, axis):
    n = math.prod(lax.axis_size(name) for name in axis)
    near = [(i, i ^ 1) for i in range(n)]
    far = [(i, i - 1 if i % 2 == 0 else i + 1) for i in range(1, n - 1)]
    return lax.ppermute(one, axis, near), lax.ppermute(two, axis, far)


def body(
    forward_coeff,
    incident,
    cost_grad,
    tmat_real,
    tmat_imag,
    translation_real,
    translation_imaginary,
    neighbours,
    particle_type,
):
    n_short = lax.axis_size("x") * lax.axis_size("c")
    tile = lax.axis_index(TALL) * n_short + lax.axis_index(FLAT)
    tile = tile.astype(jnp.int32).reshape(1)
    kinds = particle_type.reshape(1, PT)
    (ids,) = call(
        functools.partial(target_ids_kernel, n_short), [(4 * PT, PT)], tile, smem=1, us=4
    )
    one, two = call(
        functools.partial(pack_wide_kernel, n_short),
        [(ROWS + HALF, PT)] * 2,
        tile,
        forward_coeff,
        cost_grad,
        neighbours,
        kinds,
        ids,
        smem=1,
        whole=1,
    )
    x1, x2 = swapped(one, two, TALL)
    one, two = call(
        functools.partial(pack_short_kernel, n_short),
        [(ROWS, PT)] * 2,
        tile,
        forward_coeff,
        cost_grad,
        neighbours,
        kinds,
        x1,
        x2,
        smem=1,
    )
    y1, y2 = swapped(one, two, FLAT)

    tw, lw, fw = call(
        weight_kernel,
        [(2 * W, KINDS * W), (2 * W, 2 * PART), (2 * W, 2 * PART)],
        tmat_real,
        tmat_imag,
        translation_real,
        translation_imaginary,
        mib=16,
        dtype=BF16,
    )

    own = call(
        first_kernel,
        [jax.ShapeDtypeStruct((2 * W, PT), BF16), (SLOTS * W, 2 * PT)],
        ids,
        cost_grad,
        neighbours,
        kinds,
        tw,
        mib=16,
        us=2,
    )
    scratch = [pltpu.VMEM((2 * PART, 2 * PT), BF16)] * 2
    early = call(
        functools.partial(early_kernel, n_short),
        [(W, 2 * PT), (SLOTS * HALF, 2 * PT)]
        + [jax.ShapeDtypeStruct((2 * PART, 2 * PT), BF16)],
        tile,
        ids,
        *own,
        neighbours,
        kinds,
        x1,
        x2,
        forward_coeff,
        tw,
        lw,
        smem=1,
        mib=24,
        us=4,
        scratch_shapes=scratch,
    )
    (vectors,) = call(
        functools.partial(main_kernel, n_short),
        [(3 * W + 8, PT)],
        tile,
        ids,
        cost_grad,
        neighbours,
        kinds,
        incident,
        x1,
        x2,
        y1,
        y2,
        *early,
        tw,
        lw,
        fw,
        smem=1,
        mib=24,
        us=4,
        scratch_shapes=scratch,
    )
    pair = [(0, 1), (1, 0)]
    partner = lax.ppermute(vectors, "c", pair)
    (chunks,) = call(outer_kernel, [(32 * CHUNK, PT)], tile, vectors, partner, smem=1)
    got = lax.all_to_all(chunks.reshape(4, 8 * CHUNK, PT), "x", 0, 0)
    (part,) = call(sum_kernel, [(8 * CHUNK, PT)], got)
    got = lax.all_to_all(part.reshape(8, CHUNK, PT), "y", 0, 0)
    (pieces,) = call(spread_kernel, [(8, CHUNK, PT)], got)
    got = lax.all_to_all(pieces, "z", 0, 0)
    mixed, coefs = call(combine_kernel, [(32 * BACK, PT), (8, PT)], got)
    got = lax.all_to_all(mixed.reshape(32, BACK, PT), ("y", "x"), 0, 0)
    half = got.reshape(32 * BACK, PT)
    other = lax.ppermute(half, "c", pair)
    sensitivity, adjoint = call(
        expand_kernel,
        [(KINDS, W, W), (W, PT)],
        tile,
        half,
        other,
        vectors,
        coefs,
        smem=1,
    )
    return (adjoint, sensitivity)


def solution(mesh):
    fine = Mesh(mesh.devices.reshape(8, 8, 4, 2), TALL + FLAT)
    split_in = P(None, TALL + FLAT)
    placed = (split_in, split_in, split_in, P(), P(), P(), P(), split_in, P(TALL + FLAT))
    return jax.shard_map(
        body, mesh=fine, in_specs=placed, out_specs=(split_in, P()), check_vma=False
    )
```

```python
import functools
import math

import jax
import jax.numpy as jnp
from jax import lax
from jax.experimental import pallas as pl
from jax.experimental.pallas import tpu as pltpu
from jax.sharding import Mesh
from jax.sharding import PartitionSpec as P

F32 = jnp.float32
BF16 = jnp.bfloat16
W = 192
HALF = 96
PT = 128
SLOTS = 10
KINDS = 4
META = 16
ROWS = W + META
CHUNK = 40
BACK = 24
TALL = ("z", "y")
FLAT = ("x", "c")
PART = 1024
MIB = 1024 * 1024


def split(x):
    hi = x.astype(BF16)
    return hi, (x - hi.astype(F32)).astype(BF16)


def dot(a, b):
    return lax.dot_general(a, b, (((1,), (0,)), ((), ())), preferred_element_type=F32)


def dot_nt(a, b):
    return lax.dot_general(a, b, (((1,), (1,)), ((), ())), preferred_element_type=F32)


def lanes(rows):
    return lax.broadcasted_iota(jnp.int32, (rows, PT), 1)


def meta_rows(nb_ref, pt_ref):
    return jnp.concatenate(
        [
            (nb_ref[...] + 1).astype(F32),
            pt_ref[...].astype(F32),
            jnp.zeros((META - SLOTS - 1, PT), F32),
        ],
        axis=0,
    )


def even_row(short, tile_ref):
    return lax.rem(lax.div(tile_ref[0], short), 2) == 0


def even_col(tile_ref):
    return lax.rem(tile_ref[0], 2) == 0


def pack_wide_kernel(short, tile_ref, fc_ref, b_ref, nb_ref, pt_ref, _, one_ref, two_ref):
    even = even_row(short, tile_ref)
    meta = meta_rows(nb_ref, pt_ref)
    top, low = fc_ref[0:HALF, :], fc_ref[HALF:W, :]
    first = lanes(HALF) < 64
    for ref in (one_ref, two_ref):
        ref[0:W, :] = b_ref[...]
        ref[W:ROWS, :] = meta
    up = jnp.where(first, pltpu.roll(top, 64, 1), low)
    dn = jnp.where(first, top, pltpu.roll(low, 64, 1))
    one_ref[ROWS : ROWS + HALF, :] = jnp.where(even, up, dn)
    two_ref[ROWS : ROWS + HALF, :] = jnp.where(even, dn, up)


def unpack_fc(up, dn):
    first = lanes(HALF) < 64
    return jnp.concatenate(
        [
            jnp.where(first, dn, pltpu.roll(up, 64, 1)),
            jnp.where(first, pltpu.roll(dn, 64, 1), up),
        ],
        axis=0,
    )


class Tiles:
    def __init__(self, even, one_ref, two_ref):
        self.even, self.one, self.two = even, one_ref, two_ref

    def below(self, rows):
        return jnp.where(self.even, self.two[rows, :], self.one[rows, :])

    def above(self, rows):
        return jnp.where(self.even, self.one[rows, :], self.two[rows, :])


def pack_short_kernel(
    short, tile_ref, fc_ref, b_ref, nb_ref, pt_ref, x1_ref, x2_ref, one_ref, two_ref
):
    wide = Tiles(even_row(short, tile_ref), x1_ref, x2_ref)
    even = even_col(tile_ref)
    half = slice(ROWS, ROWS + HALF)
    first = lanes(META) < 64
    meta = meta_rows(nb_ref, pt_ref)
    fc_ud = unpack_fc(wide.below(half), wide.above(half))

    def part(rows, tiles):
        col = lanes(rows.stop - rows.start) % 32
        up, own, dn, edge, edge_ud = tiles

        def moved(x, shift):
            return pltpu.roll(x, shift, 1) if shift else x

        low = moved(up, 0)
        low = jnp.where(col < 4, low, moved(own, 4))
        low = jnp.where(col < 8, low, moved(dn, 8))
        low = jnp.where(col < 12, low, moved(edge, 12))
        low = jnp.where(col < 14, low, moved(edge_ud, 14))
        high = moved(edge, 114)
        high = jnp.where(col < 18, high, moved(edge_ud, 116))
        high = jnp.where(col < 20, high, moved(up, 120))
        high = jnp.where(col < 24, high, moved(own, 124))
        high = jnp.where(col < 28, high, dn)
        one_ref[rows, :] = jnp.where(even, high, low)
        two_ref[rows, :] = jnp.where(even, low, high)

    v, m = slice(0, W), slice(W, ROWS)
    part(v, (wide.below(v), b_ref[...], wide.above(v), fc_ref[...], fc_ud))
    meta_up, meta_dn = wide.below(m), wide.above(m)
    part(m, (meta_up, meta, meta_dn, meta, jnp.where(first, meta_dn, meta_up)))


def weight_kernel(tr_ref, ti_ref, lr_ref, li_ref, tw_ref, lw_ref, fw_ref):
    def turned(ref):
        n = ref.shape[0]
        fill = -n * HALF % PT
        side = jnp.concatenate([ref[...].reshape(n * HALF, HALF), jnp.zeros((n * HALF, 32), F32)], axis=1)
        if fill:
            side = jnp.concatenate([side, jnp.zeros((fill, PT), F32)], axis=0)
        return split(jnp.transpose(side)[0:HALF, :])

    def beside(ref):
        n = ref.shape[0]
        return split(
            jnp.concatenate([ref[s] for s in range(n)] + [jnp.zeros((HALF, -n * HALF % PT), F32)], axis=1)
        )

    def store(ref, real, imag, sign):
        width = real[0].shape[1]
        for at, re, im in zip((0, W), real, imag):
            ref[at : at + HALF, 0:width] = re
            ref[at : at + HALF, width:] = im if sign > 0 else -im
            ref[at + HALF : at + W, 0:width] = -im if sign > 0 else im
            ref[at + HALF : at + W, width:] = re

    store(tw_ref, turned(tr_ref), turned(ti_ref), 1)
    store(lw_ref, turned(lr_ref), turned(li_ref), 1)
    store(fw_ref, beside(lr_ref), beside(li_ref), -1)


def target_ids(base, row_stride):
    spot = lax.broadcasted_iota(jnp.int32, (4 * PT, PT), 0)
    lane = spot % PT
    row, col = lane // 32, lane % 32
    shift = jnp.where(row < 2, row_stride, -row_stride)
    own = base + lane
    beside = base + row * 32
    lr = jnp.where(
        col < 14,
        beside + PT + col - 12,
        jnp.where(
            col < 16,
            beside + PT + shift + col - 14,
            jnp.where(col < 18, beside - PT + col + 14, beside - PT + shift + col + 12),
        ),
    )
    lr = jnp.where((col >= 12) & (col < 20), lr, -10)
    edge = jnp.where(
        (col < 2) | (col >= 30),
        own,
        jnp.where(col < 4, own - 2 + shift, jnp.where(col >= 28, own + 2 + shift, lr)),
    )
    ids = jnp.where(
        spot < PT,
        own,
        jnp.where(spot < 2 * PT, own + shift, jnp.where(spot < 3 * PT, lr, edge)),
    )
    return jnp.where(ids >= 0, ids + 1, -10).astype(F32)


def target_ids_kernel(short, tile_ref, ids_ref):
    ids_ref[...] = target_ids(tile_ref[0] * PT, short * PT)


def narrow_product(w_ref, both):
    n = both.shape[1] // 2
    rows = dot(w_ref[0:W, :], both)
    return rows[:, 0:n] + rows[:, n:] + dot(w_ref[W : 2 * W, :], both[:, 0:n])


def product(w_ref, hi, lo):
    rows = dot(w_ref[...], hi)
    return rows[0:W] + rows[W : 2 * W] + dot(w_ref[0:W, :], lo)


def scaled_by_type(tw_ref, blocks, metas):
    his, los = [], []
    for v, meta in zip(blocks, metas):
        hi, lo = split(v)
        kind = meta[SLOTS : SLOTS + 1, :]
        his.append([jnp.where(kind == float(k), hi, jnp.zeros_like(hi)) for k in range(KINDS)])
        los.append([jnp.where(kind == float(k), lo, jnp.zeros_like(lo)) for k in range(KINDS)])

    def by_part(pieces):
        whole = [jnp.concatenate([p[k] for p in pieces], axis=1) for k in range(KINDS)]
        return jnp.concatenate([w[0:HALF] for w in whole] + [w[HALF:W] for w in whole], axis=0)

    s_hi, s_lo = split(narrow_product(tw_ref, jnp.concatenate([by_part(his), by_part(los)], axis=1)))
    return jnp.concatenate([s_hi, s_lo], axis=0)


def one_hot(at, meta, s):
    return jnp.where(at == meta[s : s + 1, :], 1.0, 0.0).astype(BF16)


def place(spots, parts, s, lanes_from):
    for (ref, lanes_at), part in zip(spots, parts):
        for half in range(2):
            at = half * PART + s * HALF
            ref[at : at + HALF, lanes_at] = part[half * HALF : (half + 1) * HALF, lanes_from]


def beside(ref):
    return ((ref, slice(0, PT)), (ref, slice(PT, 2 * PT)))


def clear_fill(refs):
    for ref in refs:
        for at in (SLOTS * HALF, PART + SLOTS * HALF):
            rows = PART - SLOTS * HALF
            ref[at : at + rows, :] = jnp.zeros((rows, ref.shape[1]), BF16)


def scatter_pairs(ref, stack, ids, metas, start_ref=None):
    for s in range(0, SLOTS, 2):
        pick = jnp.concatenate(
            [
                jnp.concatenate([one_hot(at, meta, t) for at, meta in zip(ids, metas)], axis=1)
                for t in (s, s + 1)
            ],
            axis=0,
        )
        g = dot_nt(stack, pick)
        g = g[0:W] + g[W : 2 * W]
        if start_ref is not None:
            g = g + start_ref[s * HALF : s * HALF + W, :]
        parts = split(g)
        for t in (0, 1):
            place(beside(ref), parts, s + t, slice(t * PT, (t + 1) * PT))


def gather_pairs(ref, blocks, ids, meta):
    stack = jnp.concatenate(split(jnp.concatenate(blocks, axis=1)), axis=0)
    for s in range(0, SLOTS, 2):
        pick = jnp.concatenate([one_hot(ids, meta, s), one_hot(ids, meta, s + 1)], axis=1)
        g = dot(stack, pick).astype(BF16)
        for t in (0, 1):
            parts = (g[0:W], g[W : 2 * W])
            place(beside(ref), parts, s + t, slice(t * PT, (t + 1) * PT))


def first_kernel(ids_ref, b_ref, nb_ref, pt_ref, tw_ref, stack_ref, sum_ref):
    ids = ids_ref[0 : 2 * PT, :]
    own = meta_rows(nb_ref, pt_ref)
    stack = scaled_by_type(tw_ref, (b_ref[...],), (own,))
    stack_ref[...] = stack
    for s in range(SLOTS):
        g = dot_nt(stack, one_hot(ids, own, s))
        sum_ref[s * W : (s + 1) * W, :] = g[0:W] + g[W : 2 * W]


def early_kernel(
    short,
    tile_ref,
    ids_ref,
    own_ref,
    sum_ref,
    nb_ref,
    pt_ref,
    x1_ref,
    x2_ref,
    fc_ref,
    tw_ref,
    lw_ref,
    part_ref,
    edge_ref,
    f_ref,
    ghi_ref,
    glo_ref,
):
    wide = Tiles(even_row(short, tile_ref), x1_ref, x2_ref)
    v, m, half = slice(0, W), slice(W, ROWS), slice(ROWS, ROWS + HALF)
    refs = (ghi_ref, glo_ref)
    ids, lr_ids = ids_ref[0 : 2 * PT, :], ids_ref[2 * PT : 3 * PT, :]
    own = meta_rows(nb_ref, pt_ref)
    metas = (wide.below(m), wide.above(m))
    clear_fill(refs + (f_ref,))
    stack = scaled_by_type(tw_ref, (wide.below(v), wide.above(v)), metas)
    for s in range(SLOTS):
        pick = jnp.concatenate([one_hot(ids, meta, s) for meta in metas], axis=1)
        g = dot_nt(stack, pick)
        g = g[0:W] + g[W : 2 * W] + sum_ref[s * W : (s + 1) * W, :]
        place([(ref, slice(None)) for ref in refs], split(g), s, slice(None))
    part_ref[...] = product(lw_ref, ghi_ref[...], glo_ref[...])
    stack = jnp.concatenate([own_ref[...], stack], axis=1)
    for s in range(0, SLOTS, 2):
        pick = jnp.concatenate(
            [
                jnp.concatenate([one_hot(lr_ids, meta, t) for meta in (own,) + metas], axis=1)
                for t in (s, s + 1)
            ],
            axis=0,
        )
        g = dot_nt(stack, pick)
        edge_ref[s * HALF : s * HALF + W, :] = g[0:W] + g[W : 2 * W]
    fc_ud = unpack_fc(wide.below(half), wide.above(half))
    gather_pairs(f_ref, (fc_ref[...], fc_ud), ids, own)


def main_kernel(
    short,
    tile_ref,
    ids_ref,
    b_ref,
    nb_ref,
    pt_ref,
    inc_ref,
    x1_ref,
    x2_ref,
    y1_ref,
    y2_ref,
    part_ref,
    edge_ref,
    f_ref,
    tw_ref,
    lw_ref,
    fw_ref,
    vec_ref,
    g_ref,
    h_ref,
):
    rows = Tiles(even_row(short, tile_ref), x1_ref, x2_ref)
    cols = Tiles(even_col(tile_ref), y1_ref, y2_ref)
    v, m = slice(0, W), slice(W, ROWS)
    ids = ids_ref[...]
    col = lanes(META) % 32
    b = b_ref[...]
    m_own = meta_rows(nb_ref, pt_ref)
    m_up, m_dn = rows.below(m), rows.above(m)
    m_ud = jnp.where(lanes(META) < 64, m_dn, m_up)
    m_lr = jnp.where(col >= 16, cols.below(m), cols.above(m))
    spot = lanes(W) % 32
    x_lr = jnp.where(spot >= 16, cols.below(v), cols.above(v))
    b_zone = (col < 12) | (col >= 20)
    row_id = lax.broadcasted_iota(jnp.int32, (META, PT), 0)
    m_b = jnp.where(b_zone | (row_id >= SLOTS), m_lr, 0.0)
    m_f = jnp.where(b_zone & (row_id < SLOTS), 0.0, m_lr)
    clear_fill((g_ref, h_ref))
    first, second = slice(0, PT), slice(PT, 2 * PT)
    own_ids, lr_ids, edge_ids = ids[0:PT, :], ids[2 * PT : 3 * PT, :], ids[3 * PT :, :]

    stack = scaled_by_type(tw_ref, (x_lr,), (m_b,))
    scatter_pairs(g_ref, stack, (edge_ids,), (m_b,), edge_ref)
    edge = narrow_product(lw_ref, g_ref[...])
    left, right = spot < 2, spot >= 30
    u1 = part_ref[:, first] + jnp.where(left | right, edge, 0.0)
    u1_ud = part_ref[:, second] + jnp.where(
        left, pltpu.roll(edge, PT - 2, 1), jnp.where(right, pltpu.roll(edge, 2, 1), 0.0)
    )
    u1_lr = jnp.where((spot >= 12) & (spot < 20), edge, 0.0)

    gather_pairs(h_ref, (x_lr,), lr_ids, m_own)
    exc = inc_ref[...] + narrow_product(fw_ref, h_ref[...] + f_ref[...])
    vec_ref[0:W, :] = b
    vec_ref[W : 2 * W, :] = u1
    vec_ref[2 * W : 3 * W, :] = exc

    metas = (m_own, m_ud, m_f)
    stack = scaled_by_type(tw_ref, (u1, u1_ud, u1_lr), metas)
    scatter_pairs(g_ref, stack, (own_ids,) * 3, metas)
    u2 = narrow_product(lw_ref, g_ref[...])

    lane, row = lanes(8), lax.broadcasted_iota(jnp.int32, (8, PT), 0)
    gram = jnp.zeros((8, PT), F32)
    for i, (p, q) in enumerate(((b, b), (b, u1), (u1, u1), (b, u2), (u1, u2), (u2, u2))):
        gram = jnp.where(lane == i, jnp.sum(p * q), gram)
    vec_ref[3 * W :, :] = jnp.where(row == 0, gram, m_own[SLOTS : SLOTS + 1, :])


def outer_kernel(tile_ref, own_ref, other_ref, chunk_ref):
    def both(rows):
        return jnp.concatenate([own_ref[rows, :], other_ref[rows, :]], axis=1)

    exc = both(slice(2 * W, 3 * W))
    e_hi, e_lo = split(jnp.concatenate([exc, jnp.zeros((64, 2 * PT), F32)], axis=0))
    v_hi, v_lo = split(both(slice(0, 2 * W)))
    kind = both(slice(3 * W + 1, 3 * W + 2))
    for k in range(2):
        here = kind == (2 * lax.rem(tile_ref[0], 2) + k).astype(F32)
        k_hi = jnp.where(here, v_hi, jnp.zeros_like(v_hi))
        k_lo = jnp.where(here, v_lo, jnp.zeros_like(v_lo))
        out = dot_nt(k_hi, e_hi) + dot_nt(k_lo, e_hi) + dot_nt(k_hi, e_lo)
        for which in range(2):
            for h in range(2):
                block = out[which * W + h * HALF : which * W + (h + 1) * HALF, :]
                edge = block[0:48, PT:] + pltpu.roll(block[48:96, PT:], 64, 1)
                at = (2 * k + h) * 8 * CHUNK + which * 18
                for i in range(18):
                    rows = block[8 * i : 8 * i + 8, 0:PT] if i < 12 else edge[8 * i - 96 : 8 * i - 88]
                    chunk_ref[pl.ds(at + i, 8, CHUNK), :] = rows
    gram = own_ref[3 * W : 3 * W + 1, :] + other_ref[3 * W : 3 * W + 1, :]
    for i in range(36, CHUNK):
        row = gram if i == 36 else jnp.zeros((1, PT), F32)
        chunk_ref[pl.ds(i, 32, CHUNK), :] = jnp.broadcast_to(row, (32, PT))


def spread_kernel(in_ref, out_ref):
    total = jnp.sum(in_ref[...], axis=0)
    for i in range(8):
        out_ref[i] = total


def sum_kernel(in_ref, out_ref):
    out_ref[...] = jnp.sum(in_ref[...], axis=0)


def combine_kernel(in_ref, out_ref, coef_ref):
    total = jnp.sum(in_ref[...], axis=0)
    lane = lanes(1)

    def entry(i):
        return jnp.sum(jnp.where(lane == i, total[36:37, :], 0.0), axis=1, keepdims=True)

    g00, g01, g11, g02, g12, g22 = [entry(i) for i in range(6)]
    alpha = g01 / g00
    beta = jnp.sqrt(g00)
    p2 = g11 - alpha * g01
    pn = jnp.sqrt(p2)
    h00 = 1.0 - alpha
    h10 = pn / beta
    h01 = (g02 - alpha * g01) / (beta * pn)
    qv1 = (g12 - alpha * g11 - alpha * g02 + alpha * alpha * g01) / p2
    h11 = 1.0 - qv1
    n00 = h00 * h00 + h10 * h10
    n01 = h00 * h01 + h10 * h11
    n11 = 1.0 - 2.0 * qv1 + (g22 - 2.0 * alpha * g12 + alpha * alpha * g11) / p2
    r0 = beta * h00
    r1 = beta * h01
    f00 = jnp.sqrt(n00)
    f10 = n01 / f00
    f11 = jnp.sqrt(n11 - f10 * f10)
    y0 = r0 / f00
    y1 = (r1 - f10 * y0) / f11
    w1 = y1 / f11
    w0 = (y0 - f10 * w1) / f00
    c1 = -w1 / pn
    c0 = w0 / beta - c1 * alpha
    mixed = c0 * total[0:18, :] + c1 * total[18:36, :]
    mixed = jnp.concatenate([mixed, jnp.zeros((BACK - 18, PT), F32)] * 2, axis=0)
    for i in range(16):
        out_ref[2 * BACK * i : 2 * BACK * (i + 1), :] = mixed
    coef_ref[0:4, :] = jnp.broadcast_to(c0, (4, PT))
    coef_ref[4:8, :] = jnp.broadcast_to(c1, (4, PT))


def expand_kernel(tile_ref, own_ref, other_ref, vec_ref, coef_ref, out_ref, adj_ref):
    adj_ref[...] = coef_ref[0:1, :] * vec_ref[0:W, :] + coef_ref[4:5, :] * vec_ref[W : 2 * W, :]
    core = lax.rem(tile_ref[0], 2)
    for ref, first in ((own_ref, 2 * core), (other_ref, 2 - 2 * core)):
        for k in range(2):
            for h in range(2):
                base, at = (2 * k + h) * BACK, h * HALF
                block = jnp.concatenate(
                    [ref[pl.ds(base + i, 8, 4 * BACK), :] for i in range(18)], axis=0
                )
                edge = block[96:144, :]
                out_ref[first + k, at : at + HALF, 0:PT] = block[0:HALF, :]
                out_ref[first + k, at : at + 48, PT:W] = edge[:, 0:64]
                out_ref[first + k, at + 48 : at + HALF, PT:W] = pltpu.roll(edge, 64, 1)[:, 0:64]


def call(kernel, shapes, *args, smem=0, whole=0, mib=6, dtype=F32, us=1, **kw):
    return pl.pallas_call(
        kernel,
        out_shape=[
            s if isinstance(s, jax.ShapeDtypeStruct) else jax.ShapeDtypeStruct(s, dtype)
            for s in shapes
        ],
        in_specs=[pl.BlockSpec(memory_space=pltpu.SMEM)] * smem
        + [pl.BlockSpec(memory_space=pltpu.VMEM)] * (len(args) - smem - whole)
        + [pl.BlockSpec(memory_space=pl.ANY)] * whole,
        cost_estimate=pl.CostEstimate(
            flops=us * 10**9, bytes_accessed=us * 3 * 10**6, transcendentals=0
        ),
        compiler_params=pltpu.CompilerParams(vmem_limit_bytes=mib * MIB),
        **kw,
    )(*args)


def swapped(one, two, axis):
    n = math.prod(lax.axis_size(name) for name in axis)
    near = [(i, i ^ 1) for i in range(n)]
    far = [(i, i - 1 if i % 2 == 0 else i + 1) for i in range(1, n - 1)]
    return lax.ppermute(one, axis, near), lax.ppermute(two, axis, far)


def body(
    forward_coeff,
    incident,
    cost_grad,
    tmat_real,
    tmat_imag,
    translation_real,
    translation_imaginary,
    neighbours,
    particle_type,
):
    n_short = lax.axis_size("x") * lax.axis_size("c")
    tile = lax.axis_index(TALL) * n_short + lax.axis_index(FLAT)
    tile = tile.astype(jnp.int32).reshape(1)
    kinds = particle_type.reshape(1, PT)
    (ids,) = call(
        functools.partial(target_ids_kernel, n_short), [(4 * PT, PT)], tile, smem=1, us=4
    )
    one, two = call(
        functools.partial(pack_wide_kernel, n_short),
        [(ROWS + HALF, PT)] * 2,
        tile,
        forward_coeff,
        cost_grad,
        neighbours,
        kinds,
        ids,
        smem=1,
        whole=1,
    )
    x1, x2 = swapped(one, two, TALL)
    one, two = call(
        functools.partial(pack_short_kernel, n_short),
        [(ROWS, PT)] * 2,
        tile,
        forward_coeff,
        cost_grad,
        neighbours,
        kinds,
        x1,
        x2,
        smem=1,
    )
    y1, y2 = swapped(one, two, FLAT)

    tw, lw, fw = call(
        weight_kernel,
        [(2 * W, KINDS * W), (2 * W, 2 * PART), (2 * W, 2 * PART)],
        tmat_real,
        tmat_imag,
        translation_real,
        translation_imaginary,
        mib=16,
        dtype=BF16,
    )

    own = call(
        first_kernel,
        [jax.ShapeDtypeStruct((2 * W, PT), BF16), (SLOTS * W, 2 * PT)],
        ids,
        cost_grad,
        neighbours,
        kinds,
        tw,
        mib=16,
        us=2,
    )
    scratch = [pltpu.VMEM((2 * PART, 2 * PT), BF16)] * 2
    early = call(
        functools.partial(early_kernel, n_short),
        [(W, 2 * PT), (SLOTS * HALF, 2 * PT)]
        + [jax.ShapeDtypeStruct((2 * PART, 2 * PT), BF16)],
        tile,
        ids,
        *own,
        neighbours,
        kinds,
        x1,
        x2,
        forward_coeff,
        tw,
        lw,
        smem=1,
        mib=24,
        us=4,
        scratch_shapes=scratch,
    )
    (vectors,) = call(
        functools.partial(main_kernel, n_short),
        [(3 * W + 8, PT)],
        tile,
        ids,
        cost_grad,
        neighbours,
        kinds,
        incident,
        x1,
        x2,
        y1,
        y2,
        *early,
        tw,
        lw,
        fw,
        smem=1,
        mib=24,
        us=4,
        scratch_shapes=scratch,
    )
    pair = [(0, 1), (1, 0)]
    partner = lax.ppermute(vectors, "c", pair)
    (chunks,) = call(outer_kernel, [(32 * CHUNK, PT)], tile, vectors, partner, smem=1)
    got = lax.all_to_all(chunks.reshape(4, 8 * CHUNK, PT), "x", 0, 0)
    (part,) = call(sum_kernel, [(8 * CHUNK, PT)], got)
    got = lax.all_to_all(part.reshape(8, CHUNK, PT), "y", 0, 0)
    (pieces,) = call(spread_kernel, [(8, CHUNK, PT)], got)
    got = lax.all_to_all(pieces, "z", 0, 0)
    mixed, coefs = call(combine_kernel, [(32 * BACK, PT), (8, PT)], got)
    got = lax.all_to_all(mixed.reshape(32, BACK, PT), ("y", "x"), 0, 0)
    half = got.reshape(32 * BACK, PT)
    other = lax.ppermute(half, "c", pair)
    sensitivity, adjoint = call(
        expand_kernel,
        [(KINDS, W, W), (W, PT)],
        tile,
        half,
        other,
        vectors,
        coefs,
        smem=1,
    )
    return (adjoint, sensitivity)


def solution(mesh):
    fine = Mesh(mesh.devices.reshape(8, 8, 4, 2), TALL + FLAT)
    split_in = P(None, TALL + FLAT)
    placed = (split_in, split_in, split_in, P(), P(), P(), P(), split_in, P(TALL + FLAT))
    return jax.shard_map(
        body, mesh=fine, in_specs=placed, out_specs=(split_in, P()), check_vma=False
    )
```

```python
import functools
import math

import jax
import jax.numpy as jnp
from jax import lax
from jax.experimental import pallas as pl
from jax.experimental.pallas import tpu as pltpu
from jax.sharding import Mesh
from jax.sharding import PartitionSpec as P

F32 = jnp.float32
BF16 = jnp.bfloat16
W = 192
HALF = 96
PT = 128
SLOTS = 10
KINDS = 4
META = 16
ROWS = W + META
CHUNK = 40
BACK = 24
TALL = ("z", "y")
FLAT = ("x", "c")
PART = 1024
MIB = 1024 * 1024


def split(x):
    hi = x.astype(BF16)
    return hi, (x - hi.astype(F32)).astype(BF16)


def dot(a, b):
    return lax.dot_general(a, b, (((1,), (0,)), ((), ())), preferred_element_type=F32)


def dot_nt(a, b):
    return lax.dot_general(a, b, (((1,), (1,)), ((), ())), preferred_element_type=F32)


def lanes(rows):
    return lax.broadcasted_iota(jnp.int32, (rows, PT), 1)


def meta_rows(nb_ref, pt_ref):
    return jnp.concatenate(
        [
            (nb_ref[...] + 1).astype(F32),
            pt_ref[...].astype(F32),
            jnp.zeros((META - SLOTS - 1, PT), F32),
        ],
        axis=0,
    )


def even_row(short, tile_ref):
    return lax.rem(lax.div(tile_ref[0], short), 2) == 0


def even_col(tile_ref):
    return lax.rem(tile_ref[0], 2) == 0


def pack_wide_kernel(short, tile_ref, fc_ref, b_ref, nb_ref, pt_ref, _, one_ref, two_ref):
    even = even_row(short, tile_ref)
    meta = meta_rows(nb_ref, pt_ref)
    top, low = fc_ref[0:HALF, :], fc_ref[HALF:W, :]
    first = lanes(HALF) < 64
    for ref in (one_ref, two_ref):
        ref[0:W, :] = b_ref[...]
        ref[W:ROWS, :] = meta
    up = jnp.where(first, pltpu.roll(top, 64, 1), low)
    dn = jnp.where(first, top, pltpu.roll(low, 64, 1))
    one_ref[ROWS : ROWS + HALF, :] = jnp.where(even, up, dn)
    two_ref[ROWS : ROWS + HALF, :] = jnp.where(even, dn, up)


def unpack_fc(up, dn):
    first = lanes(HALF) < 64
    return jnp.concatenate(
        [
            jnp.where(first, dn, pltpu.roll(up, 64, 1)),
            jnp.where(first, pltpu.roll(dn, 64, 1), up),
        ],
        axis=0,
    )


class Tiles:
    def __init__(self, even, one_ref, two_ref):
        self.even, self.one, self.two = even, one_ref, two_ref

    def below(self, rows):
        return jnp.where(self.even, self.two[rows, :], self.one[rows, :])

    def above(self, rows):
        return jnp.where(self.even, self.one[rows, :], self.two[rows, :])


def pack_short_kernel(
    short, tile_ref, fc_ref, b_ref, nb_ref, pt_ref, x1_ref, x2_ref, one_ref, two_ref
):
    wide = Tiles(even_row(short, tile_ref), x1_ref, x2_ref)
    even = even_col(tile_ref)
    half = slice(ROWS, ROWS + HALF)
    first = lanes(META) < 64
    meta = meta_rows(nb_ref, pt_ref)
    fc_ud = unpack_fc(wide.below(half), wide.above(half))

    def part(rows, tiles):
        col = lanes(rows.stop - rows.start) % 32
        up, own, dn, edge, edge_ud = tiles

        def moved(x, shift):
            return pltpu.roll(x, shift, 1) if shift else x

        low = moved(up, 0)
        low = jnp.where(col < 4, low, moved(own, 4))
        low = jnp.where(col < 8, low, moved(dn, 8))
        low = jnp.where(col < 12, low, moved(edge, 12))
        low = jnp.where(col < 14, low, moved(edge_ud, 14))
        high = moved(edge, 114)
        high = jnp.where(col < 18, high, moved(edge_ud, 116))
        high = jnp.where(col < 20, high, moved(up, 120))
        high = jnp.where(col < 24, high, moved(own, 124))
        high = jnp.where(col < 28, high, dn)
        one_ref[rows, :] = jnp.where(even, high, low)
        two_ref[rows, :] = jnp.where(even, low, high)

    v, m = slice(0, W), slice(W, ROWS)
    part(v, (wide.below(v), b_ref[...], wide.above(v), fc_ref[...], fc_ud))
    meta_up, meta_dn = wide.below(m), wide.above(m)
    part(m, (meta_up, meta, meta_dn, meta, jnp.where(first, meta_dn, meta_up)))


def weight_kernel(tr_ref, ti_ref, lr_ref, li_ref, tw_ref, lw_ref, fw_ref):
    def turned(ref):
        n = ref.shape[0]
        fill = -n * HALF % PT
        side = jnp.concatenate([ref[...].reshape(n * HALF, HALF), jnp.zeros((n * HALF, 32), F32)], axis=1)
        if fill:
            side = jnp.concatenate([side, jnp.zeros((fill, PT), F32)], axis=0)
        return split(jnp.transpose(side)[0:HALF, :])

    def beside(ref):
        n = ref.shape[0]
        return split(
            jnp.concatenate([ref[s] for s in range(n)] + [jnp.zeros((HALF, -n * HALF % PT), F32)], axis=1)
        )

    def store(ref, real, imag, sign):
        width = real[0].shape[1]
        for at, re, im in zip((0, W), real, imag):
            ref[at : at + HALF, 0:width] = re
            ref[at : at + HALF, width:] = im if sign > 0 else -im
            ref[at + HALF : at + W, 0:width] = -im if sign > 0 else im
            ref[at + HALF : at + W, width:] = re

    store(tw_ref, turned(tr_ref), turned(ti_ref), 1)
    store(lw_ref, turned(lr_ref), turned(li_ref), 1)
    store(fw_ref, beside(lr_ref), beside(li_ref), -1)


def target_ids(base, row_stride):
    spot = lax.broadcasted_iota(jnp.int32, (4 * PT, PT), 0)
    lane = spot % PT
    row, col = lane // 32, lane % 32
    shift = jnp.where(row < 2, row_stride, -row_stride)
    own = base + lane
    beside = base + row * 32
    lr = jnp.where(
        col < 14,
        beside + PT + col - 12,
        jnp.where(
            col < 16,
            beside + PT + shift + col - 14,
            jnp.where(col < 18, beside - PT + col + 14, beside - PT + shift + col + 12),
        ),
    )
    lr = jnp.where((col >= 12) & (col < 20), lr, -10)
    edge = jnp.where(
        (col < 2) | (col >= 30),
        own,
        jnp.where(col < 4, own - 2 + shift, jnp.where(col >= 28, own + 2 + shift, lr)),
    )
    ids = jnp.where(
        spot < PT,
        own,
        jnp.where(spot < 2 * PT, own + shift, jnp.where(spot < 3 * PT, lr, edge)),
    )
    return jnp.where(ids >= 0, ids + 1, -10).astype(F32)


def target_ids_kernel(short, tile_ref, ids_ref):
    ids_ref[...] = target_ids(tile_ref[0] * PT, short * PT)


def narrow_product(w_ref, both):
    n = both.shape[1] // 2
    rows = dot(w_ref[0:W, :], both)
    return rows[:, 0:n] + rows[:, n:] + dot(w_ref[W : 2 * W, :], both[:, 0:n])


def product(w_ref, hi, lo):
    rows = dot(w_ref[...], hi)
    return rows[0:W] + rows[W : 2 * W] + dot(w_ref[0:W, :], lo)


def scaled_by_type(tw_ref, blocks, metas):
    his, los = [], []
    for v, meta in zip(blocks, metas):
        hi, lo = split(v)
        kind = meta[SLOTS : SLOTS + 1, :]
        his.append([jnp.where(kind == float(k), hi, jnp.zeros_like(hi)) for k in range(KINDS)])
        los.append([jnp.where(kind == float(k), lo, jnp.zeros_like(lo)) for k in range(KINDS)])

    def by_part(pieces):
        whole = [jnp.concatenate([p[k] for p in pieces], axis=1) for k in range(KINDS)]
        return jnp.concatenate([w[0:HALF] for w in whole] + [w[HALF:W] for w in whole], axis=0)

    s_hi, s_lo = split(narrow_product(tw_ref, jnp.concatenate([by_part(his), by_part(los)], axis=1)))
    return jnp.concatenate([s_hi, s_lo], axis=0)


def one_hot(at, meta, s):
    return jnp.where(at == meta[s : s + 1, :], 1.0, 0.0).astype(BF16)


def place(spots, parts, s, lanes_from):
    for (ref, lanes_at), part in zip(spots, parts):
        for half in range(2):
            at = half * PART + s * HALF
            ref[at : at + HALF, lanes_at] = part[half * HALF : (half + 1) * HALF, lanes_from]


def beside(ref):
    return ((ref, slice(0, PT)), (ref, slice(PT, 2 * PT)))


def clear_fill(refs):
    for ref in refs:
        for at in (SLOTS * HALF, PART + SLOTS * HALF):
            rows = PART - SLOTS * HALF
            ref[at : at + rows, :] = jnp.zeros((rows, ref.shape[1]), BF16)


def scatter_pairs(ref, stack, ids, metas, start_ref=None):
    for s in range(0, SLOTS, 2):
        pick = jnp.concatenate(
            [
                jnp.concatenate([one_hot(at, meta, t) for at, meta in zip(ids, metas)], axis=1)
                for t in (s, s + 1)
            ],
            axis=0,
        )
        g = dot_nt(stack, pick)
        g = g[0:W] + g[W : 2 * W]
        if start_ref is not None:
            g = g + start_ref[s * HALF : s * HALF + W, :]
        parts = split(g)
        for t in (0, 1):
            place(beside(ref), parts, s + t, slice(t * PT, (t + 1) * PT))


def gather_pairs(ref, blocks, ids, meta):
    stack = jnp.concatenate(split(jnp.concatenate(blocks, axis=1)), axis=0)
    for s in range(0, SLOTS, 2):
        pick = jnp.concatenate([one_hot(ids, meta, s), one_hot(ids, meta, s + 1)], axis=1)
        g = dot(stack, pick).astype(BF16)
        for t in (0, 1):
            parts = (g[0:W], g[W : 2 * W])
            place(beside(ref), parts, s + t, slice(t * PT, (t + 1) * PT))


def first_kernel(ids_ref, b_ref, nb_ref, pt_ref, tw_ref, stack_ref, sum_ref):
    ids = ids_ref[0 : 2 * PT, :]
    own = meta_rows(nb_ref, pt_ref)
    stack = scaled_by_type(tw_ref, (b_ref[...],), (own,))
    stack_ref[...] = stack
    for s in range(SLOTS):
        g = dot_nt(stack, one_hot(ids, own, s))
        sum_ref[s * W : (s + 1) * W, :] = g[0:W] + g[W : 2 * W]


def early_kernel(
    short,
    tile_ref,
    ids_ref,
    own_ref,
    sum_ref,
    nb_ref,
    pt_ref,
    x1_ref,
    x2_ref,
    fc_ref,
    tw_ref,
    lw_ref,
    part_ref,
    edge_ref,
    f_ref,
    ghi_ref,
    glo_ref,
):
    wide = Tiles(even_row(short, tile_ref), x1_ref, x2_ref)
    v, m, half = slice(0, W), slice(W, ROWS), slice(ROWS, ROWS + HALF)
    refs = (ghi_ref, glo_ref)
    ids, lr_ids = ids_ref[0 : 2 * PT, :], ids_ref[2 * PT : 3 * PT, :]
    own = meta_rows(nb_ref, pt_ref)
    metas = (wide.below(m), wide.above(m))
    clear_fill(refs + (f_ref,))
    stack = scaled_by_type(tw_ref, (wide.below(v), wide.above(v)), metas)
    for s in range(SLOTS):
        pick = jnp.concatenate([one_hot(ids, meta, s) for meta in metas], axis=1)
        g = dot_nt(stack, pick)
        g = g[0:W] + g[W : 2 * W] + sum_ref[s * W : (s + 1) * W, :]
        place([(ref, slice(None)) for ref in refs], split(g), s, slice(None))
    part_ref[...] = product(lw_ref, ghi_ref[...], glo_ref[...])
    stack = jnp.concatenate([own_ref[...], stack], axis=1)
    for s in range(0, SLOTS, 2):
        pick = jnp.concatenate(
            [
                jnp.concatenate([one_hot(lr_ids, meta, t) for meta in (own,) + metas], axis=1)
                for t in (s, s + 1)
            ],
            axis=0,
        )
        g = dot_nt(stack, pick)
        edge_ref[s * HALF : s * HALF + W, :] = g[0:W] + g[W : 2 * W]
    fc_ud = unpack_fc(wide.below(half), wide.above(half))
    gather_pairs(f_ref, (fc_ref[...], fc_ud), ids, own)


def main_kernel(
    short,
    tile_ref,
    ids_ref,
    b_ref,
    nb_ref,
    pt_ref,
    inc_ref,
    x1_ref,
    x2_ref,
    y1_ref,
    y2_ref,
    part_ref,
    edge_ref,
    f_ref,
    tw_ref,
    lw_ref,
    fw_ref,
    vec_ref,
    g_ref,
    h_ref,
):
    rows = Tiles(even_row(short, tile_ref), x1_ref, x2_ref)
    cols = Tiles(even_col(tile_ref), y1_ref, y2_ref)
    v, m = slice(0, W), slice(W, ROWS)
    ids = ids_ref[...]
    col = lanes(META) % 32
    b = b_ref[...]
    m_own = meta_rows(nb_ref, pt_ref)
    m_up, m_dn = rows.below(m), rows.above(m)
    m_ud = jnp.where(lanes(META) < 64, m_dn, m_up)
    m_lr = jnp.where(col >= 16, cols.below(m), cols.above(m))
    spot = lanes(W) % 32
    x_lr = jnp.where(spot >= 16, cols.below(v), cols.above(v))
    b_zone = (col < 12) | (col >= 20)
    row_id = lax.broadcasted_iota(jnp.int32, (META, PT), 0)
    m_b = jnp.where(b_zone | (row_id >= SLOTS), m_lr, 0.0)
    m_f = jnp.where(b_zone & (row_id < SLOTS), 0.0, m_lr)
    clear_fill((g_ref, h_ref))
    first, second = slice(0, PT), slice(PT, 2 * PT)
    own_ids, lr_ids, edge_ids = ids[0:PT, :], ids[2 * PT : 3 * PT, :], ids[3 * PT :, :]

    stack = scaled_by_type(tw_ref, (x_lr,), (m_b,))
    scatter_pairs(g_ref, stack, (edge_ids,), (m_b,), edge_ref)
    edge = narrow_product(lw_ref, g_ref[...])
    left, right = spot < 2, spot >= 30
    u1 = part_ref[:, first] + jnp.where(left | right, edge, 0.0)
    u1_ud = part_ref[:, second] + jnp.where(
        left, pltpu.roll(edge, PT - 2, 1), jnp.where(right, pltpu.roll(edge, 2, 1), 0.0)
    )
    u1_lr = jnp.where((spot >= 12) & (spot < 20), edge, 0.0)

    gather_pairs(h_ref, (x_lr,), lr_ids, m_own)
    exc = inc_ref[...] + narrow_product(fw_ref, h_ref[...] + f_ref[...])
    vec_ref[0:W, :] = b
    vec_ref[W : 2 * W, :] = u1
    vec_ref[2 * W : 3 * W, :] = exc

    metas = (m_own, m_ud, m_f)
    stack = scaled_by_type(tw_ref, (u1, u1_ud, u1_lr), metas)
    scatter_pairs(g_ref, stack, (own_ids,) * 3, metas)
    u2 = narrow_product(lw_ref, g_ref[...])

    lane, row = lanes(8), lax.broadcasted_iota(jnp.int32, (8, PT), 0)
    gram = jnp.zeros((8, PT), F32)
    for i, (p, q) in enumerate(((b, b), (b, u1), (u1, u1), (b, u2), (u1, u2), (u2, u2))):
        gram = jnp.where(lane == i, jnp.sum(p * q), gram)
    vec_ref[3 * W :, :] = jnp.where(row == 0, gram, m_own[SLOTS : SLOTS + 1, :])


def outer_kernel(tile_ref, own_ref, other_ref, chunk_ref):
    def both(rows):
        return jnp.concatenate([own_ref[rows, :], other_ref[rows, :]], axis=1)

    exc = both(slice(2 * W, 3 * W))
    e_hi, e_lo = split(jnp.concatenate([exc, jnp.zeros((64, 2 * PT), F32)], axis=0))
    v_hi, v_lo = split(both(slice(0, 2 * W)))
    kind = both(slice(3 * W + 1, 3 * W + 2))
    for k in range(2):
        here = kind == (2 * lax.rem(tile_ref[0], 2) + k).astype(F32)
        k_hi = jnp.where(here, v_hi, jnp.zeros_like(v_hi))
        k_lo = jnp.where(here, v_lo, jnp.zeros_like(v_lo))
        out = dot_nt(k_hi, e_hi) + dot_nt(k_lo, e_hi) + dot_nt(k_hi, e_lo)
        for which in range(2):
            for h in range(2):
                block = out[which * W + h * HALF : which * W + (h + 1) * HALF, :]
                edge = block[0:48, PT:] + pltpu.roll(block[48:96, PT:], 64, 1)
                at = (2 * k + h) * 8 * CHUNK + which * 18
                for i in range(18):
                    rows = block[8 * i : 8 * i + 8, 0:PT] if i < 12 else edge[8 * i - 96 : 8 * i - 88]
                    chunk_ref[pl.ds(at + i, 8, CHUNK), :] = rows
    gram = own_ref[3 * W : 3 * W + 1, :] + other_ref[3 * W : 3 * W + 1, :]
    for i in range(36, CHUNK):
        row = gram if i == 36 else jnp.zeros((1, PT), F32)
        chunk_ref[pl.ds(i, 32, CHUNK), :] = jnp.broadcast_to(row, (32, PT))


def spread_kernel(in_ref, out_ref):
    total = jnp.sum(in_ref[...], axis=0)
    for i in range(8):
        out_ref[i] = total


def sum_kernel(in_ref, out_ref):
    out_ref[...] = jnp.sum(in_ref[...], axis=0)


def combine_kernel(in_ref, out_ref, coef_ref):
    total = jnp.sum(in_ref[...], axis=0)
    lane = lanes(1)

    def entry(i):
        return jnp.sum(jnp.where(lane == i, total[36:37, :], 0.0), axis=1, keepdims=True)

    g00, g01, g11, g02, g12, g22 = [entry(i) for i in range(6)]
    alpha = g01 / g00
    beta = jnp.sqrt(g00)
    p2 = g11 - alpha * g01
    pn = jnp.sqrt(p2)
    h00 = 1.0 - alpha
    h10 = pn / beta
    h01 = (g02 - alpha * g01) / (beta * pn)
    qv1 = (g12 - alpha * g11 - alpha * g02 + alpha * alpha * g01) / p2
    h11 = 1.0 - qv1
    n00 = h00 * h00 + h10 * h10
    n01 = h00 * h01 + h10 * h11
    n11 = 1.0 - 2.0 * qv1 + (g22 - 2.0 * alpha * g12 + alpha * alpha * g11) / p2
    r0 = beta * h00
    r1 = beta * h01
    f00 = jnp.sqrt(n00)
    f10 = n01 / f00
    f11 = jnp.sqrt(n11 - f10 * f10)
    y0 = r0 / f00
    y1 = (r1 - f10 * y0) / f11
    w1 = y1 / f11
    w0 = (y0 - f10 * w1) / f00
    c1 = -w1 / pn
    c0 = w0 / beta - c1 * alpha
    mixed = c0 * total[0:18, :] + c1 * total[18:36, :]
    mixed = jnp.concatenate([mixed, jnp.zeros((BACK - 18, PT), F32)] * 2, axis=0)
    for i in range(16):
        out_ref[2 * BACK * i : 2 * BACK * (i + 1), :] = mixed
    coef_ref[0:4, :] = jnp.broadcast_to(c0, (4, PT))
    coef_ref[4:8, :] = jnp.broadcast_to(c1, (4, PT))


def spread_types(ref, out_ref, first):
    for k in range(2):
        for h in range(2):
            base, at = (2 * k + h) * BACK, h * HALF
            block = jnp.concatenate(
                [ref[pl.ds(base + i, 8, 4 * BACK), :] for i in range(18)], axis=0
            )
            edge = block[96:144, :]
            out_ref[first + k, at : at + HALF, 0:PT] = block[0:HALF, :]
            out_ref[first + k, at : at + 48, PT:W] = edge[:, 0:64]
            out_ref[first + k, at + 48 : at + HALF, PT:W] = pltpu.roll(edge, 64, 1)[:, 0:64]


def own_types_kernel(own_ref, vec_ref, coef_ref, half_ref, adj_ref):
    adj_ref[...] = coef_ref[0:1, :] * vec_ref[0:W, :] + coef_ref[4:5, :] * vec_ref[W : 2 * W, :]
    spread_types(own_ref, half_ref, 0)


def expand_kernel(tile_ref, half_ref, other_ref, out_ref):
    core = lax.rem(tile_ref[0], 2)
    for k in range(2):
        out_ref[2 * core + k] = half_ref[k]
    spread_types(other_ref, out_ref, 2 - 2 * core)


def call(kernel, shapes, *args, smem=0, whole=0, mib=6, dtype=F32, us=1, **kw):
    return pl.pallas_call(
        kernel,
        out_shape=[
            s if isinstance(s, jax.ShapeDtypeStruct) else jax.ShapeDtypeStruct(s, dtype)
            for s in shapes
        ],
        in_specs=[pl.BlockSpec(memory_space=pltpu.SMEM)] * smem
        + [pl.BlockSpec(memory_space=pltpu.VMEM)] * (len(args) - smem - whole)
        + [pl.BlockSpec(memory_space=pl.ANY)] * whole,
        cost_estimate=pl.CostEstimate(
            flops=us * 10**9, bytes_accessed=us * 3 * 10**6, transcendentals=0
        ),
        compiler_params=pltpu.CompilerParams(vmem_limit_bytes=mib * MIB),
        **kw,
    )(*args)


def swapped(one, two, axis):
    n = math.prod(lax.axis_size(name) for name in axis)
    near = [(i, i ^ 1) for i in range(n)]
    far = [(i, i - 1 if i % 2 == 0 else i + 1) for i in range(1, n - 1)]
    return lax.ppermute(one, axis, near), lax.ppermute(two, axis, far)


def body(
    forward_coeff,
    incident,
    cost_grad,
    tmat_real,
    tmat_imag,
    translation_real,
    translation_imaginary,
    neighbours,
    particle_type,
):
    n_short = lax.axis_size("x") * lax.axis_size("c")
    tile = lax.axis_index(TALL) * n_short + lax.axis_index(FLAT)
    tile = tile.astype(jnp.int32).reshape(1)
    kinds = particle_type.reshape(1, PT)
    (ids,) = call(
        functools.partial(target_ids_kernel, n_short), [(4 * PT, PT)], tile, smem=1, us=4
    )
    one, two = call(
        functools.partial(pack_wide_kernel, n_short),
        [(ROWS + HALF, PT)] * 2,
        tile,
        forward_coeff,
        cost_grad,
        neighbours,
        kinds,
        ids,
        smem=1,
        whole=1,
    )
    x1, x2 = swapped(one, two, TALL)
    one, two = call(
        functools.partial(pack_short_kernel, n_short),
        [(ROWS, PT)] * 2,
        tile,
        forward_coeff,
        cost_grad,
        neighbours,
        kinds,
        x1,
        x2,
        smem=1,
    )
    y1, y2 = swapped(one, two, FLAT)

    tw, lw, fw = call(
        weight_kernel,
        [(2 * W, KINDS * W), (2 * W, 2 * PART), (2 * W, 2 * PART)],
        tmat_real,
        tmat_imag,
        translation_real,
        translation_imaginary,
        mib=16,
        dtype=BF16,
    )

    own = call(
        first_kernel,
        [jax.ShapeDtypeStruct((2 * W, PT), BF16), (SLOTS * W, 2 * PT)],
        ids,
        cost_grad,
        neighbours,
        kinds,
        tw,
        mib=16,
        us=2,
    )
    scratch = [pltpu.VMEM((2 * PART, 2 * PT), BF16)] * 2
    early = call(
        functools.partial(early_kernel, n_short),
        [(W, 2 * PT), (SLOTS * HALF, 2 * PT)]
        + [jax.ShapeDtypeStruct((2 * PART, 2 * PT), BF16)],
        tile,
        ids,
        *own,
        neighbours,
        kinds,
        x1,
        x2,
        forward_coeff,
        tw,
        lw,
        smem=1,
        mib=24,
        us=4,
        scratch_shapes=scratch,
    )
    (vectors,) = call(
        functools.partial(main_kernel, n_short),
        [(3 * W + 8, PT)],
        tile,
        ids,
        cost_grad,
        neighbours,
        kinds,
        incident,
        x1,
        x2,
        y1,
        y2,
        *early,
        tw,
        lw,
        fw,
        smem=1,
        mib=24,
        us=4,
        scratch_shapes=scratch,
    )
    pair = [(0, 1), (1, 0)]
    partner = lax.ppermute(vectors, "c", pair)
    (chunks,) = call(outer_kernel, [(32 * CHUNK, PT)], tile, vectors, partner, smem=1)
    got = lax.all_to_all(chunks.reshape(4, 8 * CHUNK, PT), "x", 0, 0)
    (part,) = call(sum_kernel, [(8 * CHUNK, PT)], got)
    got = lax.all_to_all(part.reshape(8, CHUNK, PT), "y", 0, 0)
    (pieces,) = call(spread_kernel, [(8, CHUNK, PT)], got)
    got = lax.all_to_all(pieces, "z", 0, 0)
    mixed, coefs = call(combine_kernel, [(32 * BACK, PT), (8, PT)], got)
    got = lax.all_to_all(mixed.reshape(32, BACK, PT), ("y", "x"), 0, 0)
    half = got.reshape(32 * BACK, PT)
    other = lax.ppermute(half, "c", pair)
    own_half, adjoint = call(own_types_kernel, [(2, W, W), (W, PT)], half, vectors, coefs)
    (sensitivity,) = call(expand_kernel, [(KINDS, W, W)], tile, own_half, other, smem=1)
    return (adjoint, sensitivity)


def solution(mesh):
    fine = Mesh(mesh.devices.reshape(8, 8, 4, 2), TALL + FLAT)
    split_in = P(None, TALL + FLAT)
    placed = (split_in, split_in, split_in, P(), P(), P(), P(), split_in, P(TALL + FLAT))
    return jax.shard_map(
        body, mesh=fine, in_specs=placed, out_specs=(split_in, P()), check_vma=False
    )
```

```python
import functools
import math

import jax
import jax.numpy as jnp
from jax import lax
from jax.experimental import pallas as pl
from jax.experimental.pallas import tpu as pltpu
from jax.sharding import Mesh
from jax.sharding import PartitionSpec as P

F32 = jnp.float32
BF16 = jnp.bfloat16
W = 192
HALF = 96
PT = 128
SLOTS = 10
KINDS = 4
META = 16
ROWS = W + META
CHUNK = 40
BACK = 24
TALL = ("z", "y")
FLAT = ("x", "c")
PART = 1024
MIB = 1024 * 1024


def split(x):
    hi = x.astype(BF16)
    return hi, (x - hi.astype(F32)).astype(BF16)


def dot(a, b):
    return lax.dot_general(a, b, (((1,), (0,)), ((), ())), preferred_element_type=F32)


def dot_nt(a, b):
    return lax.dot_general(a, b, (((1,), (1,)), ((), ())), preferred_element_type=F32)


def lanes(rows):
    return lax.broadcasted_iota(jnp.int32, (rows, PT), 1)


def meta_rows(nb_ref, pt_ref):
    return jnp.concatenate(
        [
            (nb_ref[...] + 1).astype(F32),
            pt_ref[...].astype(F32),
            jnp.zeros((META - SLOTS - 1, PT), F32),
        ],
        axis=0,
    )


def even_row(short, tile_ref):
    return lax.rem(lax.div(tile_ref[0], short), 2) == 0


def even_col(tile_ref):
    return lax.rem(tile_ref[0], 2) == 0


def pack_wide_kernel(short, tile_ref, fc_ref, b_ref, nb_ref, pt_ref, _, one_ref, two_ref):
    even = even_row(short, tile_ref)
    meta = meta_rows(nb_ref, pt_ref)
    top, low = fc_ref[0:HALF, :], fc_ref[HALF:W, :]
    first = lanes(HALF) < 64
    for ref in (one_ref, two_ref):
        ref[0:W, :] = b_ref[...]
        ref[W:ROWS, :] = meta
    up = jnp.where(first, pltpu.roll(top, 64, 1), low)
    dn = jnp.where(first, top, pltpu.roll(low, 64, 1))
    one_ref[ROWS : ROWS + HALF, :] = jnp.where(even, up, dn)
    two_ref[ROWS : ROWS + HALF, :] = jnp.where(even, dn, up)


def unpack_fc(up, dn):
    first = lanes(HALF) < 64
    return jnp.concatenate(
        [
            jnp.where(first, dn, pltpu.roll(up, 64, 1)),
            jnp.where(first, pltpu.roll(dn, 64, 1), up),
        ],
        axis=0,
    )


class Tiles:
    def __init__(self, even, one_ref, two_ref):
        self.even, self.one, self.two = even, one_ref, two_ref

    def below(self, rows):
        return jnp.where(self.even, self.two[rows, :], self.one[rows, :])

    def above(self, rows):
        return jnp.where(self.even, self.one[rows, :], self.two[rows, :])


def pack_short_kernel(
    short, tile_ref, fc_ref, b_ref, nb_ref, pt_ref, x1_ref, x2_ref, one_ref, two_ref
):
    wide = Tiles(even_row(short, tile_ref), x1_ref, x2_ref)
    even = even_col(tile_ref)
    half = slice(ROWS, ROWS + HALF)
    first = lanes(META) < 64
    meta = meta_rows(nb_ref, pt_ref)
    fc_ud = unpack_fc(wide.below(half), wide.above(half))

    def part(rows, tiles):
        col = lanes(rows.stop - rows.start) % 32
        up, own, dn, edge, edge_ud = tiles

        def moved(x, shift):
            return pltpu.roll(x, shift, 1) if shift else x

        low = moved(up, 0)
        low = jnp.where(col < 4, low, moved(own, 4))
        low = jnp.where(col < 8, low, moved(dn, 8))
        low = jnp.where(col < 12, low, moved(edge, 12))
        low = jnp.where(col < 14, low, moved(edge_ud, 14))
        high = moved(edge, 114)
        high = jnp.where(col < 18, high, moved(edge_ud, 116))
        high = jnp.where(col < 20, high, moved(up, 120))
        high = jnp.where(col < 24, high, moved(own, 124))
        high = jnp.where(col < 28, high, dn)
        one_ref[rows, :] = jnp.where(even, high, low)
        two_ref[rows, :] = jnp.where(even, low, high)

    v, m = slice(0, W), slice(W, ROWS)
    part(v, (wide.below(v), b_ref[...], wide.above(v), fc_ref[...], fc_ud))
    meta_up, meta_dn = wide.below(m), wide.above(m)
    part(m, (meta_up, meta, meta_dn, meta, jnp.where(first, meta_dn, meta_up)))


def weight_kernel(tr_ref, ti_ref, lr_ref, li_ref, tw_ref, lw_ref, fw_ref):
    def turned(ref):
        n = ref.shape[0]
        fill = -n * HALF % PT
        side = jnp.concatenate([ref[...].reshape(n * HALF, HALF), jnp.zeros((n * HALF, 32), F32)], axis=1)
        if fill:
            side = jnp.concatenate([side, jnp.zeros((fill, PT), F32)], axis=0)
        return split(jnp.transpose(side)[0:HALF, :])

    def beside(ref):
        n = ref.shape[0]
        return split(
            jnp.concatenate([ref[s] for s in range(n)] + [jnp.zeros((HALF, -n * HALF % PT), F32)], axis=1)
        )

    def store(ref, real, imag, sign):
        width = real[0].shape[1]
        for at, re, im in zip((0, W), real, imag):
            ref[at : at + HALF, 0:width] = re
            ref[at : at + HALF, width:] = im if sign > 0 else -im
            ref[at + HALF : at + W, 0:width] = -im if sign > 0 else im
            ref[at + HALF : at + W, width:] = re

    store(tw_ref, turned(tr_ref), turned(ti_ref), 1)
    store(lw_ref, turned(lr_ref), turned(li_ref), 1)
    store(fw_ref, beside(lr_ref), beside(li_ref), -1)


def target_ids(base, row_stride):
    spot = lax.broadcasted_iota(jnp.int32, (4 * PT, PT), 0)
    lane = spot % PT
    row, col = lane // 32, lane % 32
    shift = jnp.where(row < 2, row_stride, -row_stride)
    own = base + lane
    beside = base + row * 32
    lr = jnp.where(
        col < 14,
        beside + PT + col - 12,
        jnp.where(
            col < 16,
            beside + PT + shift + col - 14,
            jnp.where(col < 18, beside - PT + col + 14, beside - PT + shift + col + 12),
        ),
    )
    lr = jnp.where((col >= 12) & (col < 20), lr, -10)
    edge = jnp.where(
        (col < 2) | (col >= 30),
        own,
        jnp.where(col < 4, own - 2 + shift, jnp.where(col >= 28, own + 2 + shift, lr)),
    )
    ids = jnp.where(
        spot < PT,
        own,
        jnp.where(spot < 2 * PT, own + shift, jnp.where(spot < 3 * PT, lr, edge)),
    )
    return jnp.where(ids >= 0, ids + 1, -10).astype(F32)


def target_ids_kernel(short, tile_ref, ids_ref):
    ids_ref[...] = target_ids(tile_ref[0] * PT, short * PT)


def narrow_product(w_ref, both):
    n = both.shape[1] // 2
    rows = dot(w_ref[0:W, :], both)
    return rows[:, 0:n] + rows[:, n:] + dot(w_ref[W : 2 * W, :], both[:, 0:n])


def product(w_ref, hi, lo):
    rows = dot(w_ref[...], hi)
    return rows[0:W] + rows[W : 2 * W] + dot(w_ref[0:W, :], lo)


def scaled_by_type(tw_ref, blocks, metas):
    his, los = [], []
    for v, meta in zip(blocks, metas):
        hi, lo = split(v)
        kind = meta[SLOTS : SLOTS + 1, :]
        his.append([jnp.where(kind == float(k), hi, jnp.zeros_like(hi)) for k in range(KINDS)])
        los.append([jnp.where(kind == float(k), lo, jnp.zeros_like(lo)) for k in range(KINDS)])

    def by_part(pieces):
        whole = [jnp.concatenate([p[k] for p in pieces], axis=1) for k in range(KINDS)]
        return jnp.concatenate([w[0:HALF] for w in whole] + [w[HALF:W] for w in whole], axis=0)

    s_hi, s_lo = split(narrow_product(tw_ref, jnp.concatenate([by_part(his), by_part(los)], axis=1)))
    return jnp.concatenate([s_hi, s_lo], axis=0)


def one_hot(at, meta, s):
    return jnp.where(at == meta[s : s + 1, :], 1.0, 0.0).astype(BF16)


def place(spots, parts, s, lanes_from):
    for (ref, lanes_at), part in zip(spots, parts):
        for half in range(2):
            at = half * PART + s * HALF
            ref[at : at + HALF, lanes_at] = part[half * HALF : (half + 1) * HALF, lanes_from]


def beside(ref):
    return ((ref, slice(0, PT)), (ref, slice(PT, 2 * PT)))


def clear_fill(refs):
    for ref in refs:
        for at in (SLOTS * HALF, PART + SLOTS * HALF):
            rows = PART - SLOTS * HALF
            ref[at : at + rows, :] = jnp.zeros((rows, ref.shape[1]), BF16)


def scatter_pairs(ref, stack, ids, metas, start_ref=None):
    for s in range(0, SLOTS, 2):
        pick = jnp.concatenate(
            [
                jnp.concatenate([one_hot(at, meta, t) for at, meta in zip(ids, metas)], axis=1)
                for t in (s, s + 1)
            ],
            axis=0,
        )
        g = dot_nt(stack, pick)
        g = g[0:W] + g[W : 2 * W]
        if start_ref is not None:
            g = g + start_ref[s * HALF : s * HALF + W, :]
        parts = split(g)
        for t in (0, 1):
            place(beside(ref), parts, s + t, slice(t * PT, (t + 1) * PT))


def gather_pairs(ref, blocks, ids, meta):
    stack = jnp.concatenate(split(jnp.concatenate(blocks, axis=1)), axis=0)
    for s in range(0, SLOTS, 2):
        pick = jnp.concatenate([one_hot(ids, meta, s), one_hot(ids, meta, s + 1)], axis=1)
        g = dot(stack, pick).astype(BF16)
        for t in (0, 1):
            parts = (g[0:W], g[W : 2 * W])
            place(beside(ref), parts, s + t, slice(t * PT, (t + 1) * PT))


def first_kernel(ids_ref, b_ref, nb_ref, pt_ref, tw_ref, stack_ref, sum_ref):
    ids = ids_ref[0 : 2 * PT, :]
    own = meta_rows(nb_ref, pt_ref)
    stack = scaled_by_type(tw_ref, (b_ref[...],), (own,))
    stack_ref[...] = stack
    for s in range(SLOTS):
        g = dot_nt(stack, one_hot(ids, own, s))
        sum_ref[s * W : (s + 1) * W, :] = g[0:W] + g[W : 2 * W]


def early_kernel(
    short,
    tile_ref,
    ids_ref,
    own_ref,
    sum_ref,
    nb_ref,
    pt_ref,
    x1_ref,
    x2_ref,
    fc_ref,
    tw_ref,
    lw_ref,
    part_ref,
    edge_ref,
    f_ref,
    ghi_ref,
    glo_ref,
):
    wide = Tiles(even_row(short, tile_ref), x1_ref, x2_ref)
    v, m, half = slice(0, W), slice(W, ROWS), slice(ROWS, ROWS + HALF)
    refs = (ghi_ref, glo_ref)
    ids, lr_ids = ids_ref[0 : 2 * PT, :], ids_ref[2 * PT : 3 * PT, :]
    own = meta_rows(nb_ref, pt_ref)
    metas = (wide.below(m), wide.above(m))
    clear_fill(refs + (f_ref,))
    stack = scaled_by_type(tw_ref, (wide.below(v), wide.above(v)), metas)
    for s in range(SLOTS):
        pick = jnp.concatenate([one_hot(ids, meta, s) for meta in metas], axis=1)
        g = dot_nt(stack, pick)
        g = g[0:W] + g[W : 2 * W] + sum_ref[s * W : (s + 1) * W, :]
        place([(ref, slice(None)) for ref in refs], split(g), s, slice(None))
    part_ref[...] = product(lw_ref, ghi_ref[...], glo_ref[...])
    stack = jnp.concatenate([own_ref[...], stack], axis=1)
    for s in range(0, SLOTS, 2):
        pick = jnp.concatenate(
            [
                jnp.concatenate([one_hot(lr_ids, meta, t) for meta in (own,) + metas], axis=1)
                for t in (s, s + 1)
            ],
            axis=0,
        )
        g = dot_nt(stack, pick)
        edge_ref[s * HALF : s * HALF + W, :] = g[0:W] + g[W : 2 * W]
    fc_ud = unpack_fc(wide.below(half), wide.above(half))
    gather_pairs(f_ref, (fc_ref[...], fc_ud), ids, own)


def main_kernel(
    short,
    tile_ref,
    ids_ref,
    b_ref,
    nb_ref,
    pt_ref,
    inc_ref,
    x1_ref,
    x2_ref,
    y1_ref,
    y2_ref,
    part_ref,
    edge_ref,
    f_ref,
    tw_ref,
    lw_ref,
    fw_ref,
    vec_ref,
    g_ref,
    h_ref,
):
    rows = Tiles(even_row(short, tile_ref), x1_ref, x2_ref)
    cols = Tiles(even_col(tile_ref), y1_ref, y2_ref)
    v, m = slice(0, W), slice(W, ROWS)
    ids = ids_ref[...]
    col = lanes(META) % 32
    b = b_ref[...]
    m_own = meta_rows(nb_ref, pt_ref)
    m_up, m_dn = rows.below(m), rows.above(m)
    m_ud = jnp.where(lanes(META) < 64, m_dn, m_up)
    m_lr = jnp.where(col >= 16, cols.below(m), cols.above(m))
    spot = lanes(W) % 32
    x_lr = jnp.where(spot >= 16, cols.below(v), cols.above(v))
    b_zone = (col < 12) | (col >= 20)
    row_id = lax.broadcasted_iota(jnp.int32, (META, PT), 0)
    m_b = jnp.where(b_zone | (row_id >= SLOTS), m_lr, 0.0)
    m_f = jnp.where(b_zone & (row_id < SLOTS), 0.0, m_lr)
    clear_fill((g_ref, h_ref))
    first, second = slice(0, PT), slice(PT, 2 * PT)
    own_ids, lr_ids, edge_ids = ids[0:PT, :], ids[2 * PT : 3 * PT, :], ids[3 * PT :, :]

    stack = scaled_by_type(tw_ref, (x_lr,), (m_b,))
    scatter_pairs(g_ref, stack, (edge_ids,), (m_b,), edge_ref)
    edge = narrow_product(lw_ref, g_ref[...])
    left, right = spot < 2, spot >= 30
    u1 = part_ref[:, first] + jnp.where(left | right, edge, 0.0)
    u1_ud = part_ref[:, second] + jnp.where(
        left, pltpu.roll(edge, PT - 2, 1), jnp.where(right, pltpu.roll(edge, 2, 1), 0.0)
    )
    u1_lr = jnp.where((spot >= 12) & (spot < 20), edge, 0.0)

    gather_pairs(h_ref, (x_lr,), lr_ids, m_own)
    exc = inc_ref[...] + narrow_product(fw_ref, h_ref[...] + f_ref[...])
    vec_ref[0:W, :] = b
    vec_ref[W : 2 * W, :] = u1
    vec_ref[2 * W : 3 * W, :] = exc

    metas = (m_own, m_ud, m_f)
    stack = scaled_by_type(tw_ref, (u1, u1_ud, u1_lr), metas)
    scatter_pairs(g_ref, stack, (own_ids,) * 3, metas)
    u2 = narrow_product(lw_ref, g_ref[...])

    lane, row = lanes(8), lax.broadcasted_iota(jnp.int32, (8, PT), 0)
    gram = jnp.zeros((8, PT), F32)
    for i, (p, q) in enumerate(((b, b), (b, u1), (u1, u1), (b, u2), (u1, u2), (u2, u2))):
        gram = jnp.where(lane == i, jnp.sum(p * q), gram)
    vec_ref[3 * W :, :] = jnp.where(row == 0, gram, m_own[SLOTS : SLOTS + 1, :])


def outer_kernel(tile_ref, own_ref, other_ref, chunk_ref):
    def both(rows):
        return jnp.concatenate([own_ref[rows, :], other_ref[rows, :]], axis=1)

    exc = both(slice(2 * W, 3 * W))
    e_hi, e_lo = split(jnp.concatenate([exc, jnp.zeros((64, 2 * PT), F32)], axis=0))
    v_hi, v_lo = split(both(slice(0, 2 * W)))
    kind = both(slice(3 * W + 1, 3 * W + 2))
    for k in range(2):
        here = kind == (2 * lax.rem(tile_ref[0], 2) + k).astype(F32)
        k_hi = jnp.where(here, v_hi, jnp.zeros_like(v_hi))
        k_lo = jnp.where(here, v_lo, jnp.zeros_like(v_lo))
        out = dot_nt(k_hi, e_hi) + dot_nt(k_lo, e_hi) + dot_nt(k_hi, e_lo)
        for which in range(2):
            for h in range(2):
                block = out[which * W + h * HALF : which * W + (h + 1) * HALF, :]
                edge = block[0:48, PT:] + pltpu.roll(block[48:96, PT:], 64, 1)
                at = (2 * k + h) * 8 * CHUNK + which * 18
                for i in range(18):
                    rows = block[8 * i : 8 * i + 8, 0:PT] if i < 12 else edge[8 * i - 96 : 8 * i - 88]
                    chunk_ref[pl.ds(at + i, 8, CHUNK), :] = rows
    gram = own_ref[3 * W : 3 * W + 1, :] + other_ref[3 * W : 3 * W + 1, :]
    for i in range(36, CHUNK):
        row = gram if i == 36 else jnp.zeros((1, PT), F32)
        chunk_ref[pl.ds(i, 32, CHUNK), :] = jnp.broadcast_to(row, (32, PT))


def spread_kernel(in_ref, out_ref):
    total = jnp.sum(in_ref[...], axis=0)
    for i in range(8):
        out_ref[i] = total


def sum_kernel(in_ref, out_ref):
    out_ref[...] = jnp.sum(in_ref[...], axis=0)


def combine_kernel(in_ref, out_ref, coef_ref):
    total = jnp.sum(in_ref[...], axis=0)
    lane = lanes(1)

    def entry(i):
        return jnp.sum(jnp.where(lane == i, total[36:37, :], 0.0), axis=1, keepdims=True)

    g00, g01, g11, g02, g12, g22 = [entry(i) for i in range(6)]
    alpha = g01 / g00
    beta = jnp.sqrt(g00)
    p2 = g11 - alpha * g01
    pn = jnp.sqrt(p2)
    h00 = 1.0 - alpha
    h10 = pn / beta
    h01 = (g02 - alpha * g01) / (beta * pn)
    qv1 = (g12 - alpha * g11 - alpha * g02 + alpha * alpha * g01) / p2
    h11 = 1.0 - qv1
    n00 = h00 * h00 + h10 * h10
    n01 = h00 * h01 + h10 * h11
    n11 = 1.0 - 2.0 * qv1 + (g22 - 2.0 * alpha * g12 + alpha * alpha * g11) / p2
    r0 = beta * h00
    r1 = beta * h01
    f00 = jnp.sqrt(n00)
    f10 = n01 / f00
    f11 = jnp.sqrt(n11 - f10 * f10)
    y0 = r0 / f00
    y1 = (r1 - f10 * y0) / f11
    w1 = y1 / f11
    w0 = (y0 - f10 * w1) / f00
    c1 = -w1 / pn
    c0 = w0 / beta - c1 * alpha
    mixed = c0 * total[0:18, :] + c1 * total[18:36, :]
    mixed = jnp.concatenate([mixed, jnp.zeros((BACK - 18, PT), F32)] * 2, axis=0)
    for i in range(16):
        out_ref[2 * BACK * i : 2 * BACK * (i + 1), :] = mixed
    coef_ref[0:4, :] = jnp.broadcast_to(c0, (4, PT))
    coef_ref[4:8, :] = jnp.broadcast_to(c1, (4, PT))


def spread_types(ref, out_ref, first):
    for k in range(2):
        for h in range(2):
            base, at = (2 * k + h) * BACK, h * HALF
            block = jnp.concatenate(
                [ref[pl.ds(base + i, 8, 4 * BACK), :] for i in range(18)], axis=0
            )
            edge = block[96:144, :]
            out_ref[first + k, at : at + HALF, 0:PT] = block[0:HALF, :]
            out_ref[first + k, at : at + 48, PT:W] = edge[:, 0:64]
            out_ref[first + k, at + 48 : at + HALF, PT:W] = pltpu.roll(edge, 64, 1)[:, 0:64]


def own_types_kernel(own_ref, vec_ref, coef_ref, half_ref, adj_ref):
    adj_ref[...] = coef_ref[0:1, :] * vec_ref[0:W, :] + coef_ref[4:5, :] * vec_ref[W : 2 * W, :]
    spread_types(own_ref, half_ref, 0)


def expand_kernel(tile_ref, half_ref, other_ref, out_ref):
    core = lax.rem(tile_ref[0], 2)
    for k in range(2):
        out_ref[2 * core + k] = half_ref[k]
    spread_types(other_ref, out_ref, 2 - 2 * core)


def call(kernel, shapes, *args, smem=0, whole=0, mib=6, dtype=F32, us=1, **kw):
    return pl.pallas_call(
        kernel,
        out_shape=[
            s if isinstance(s, jax.ShapeDtypeStruct) else jax.ShapeDtypeStruct(s, dtype)
            for s in shapes
        ],
        in_specs=[pl.BlockSpec(memory_space=pltpu.SMEM)] * smem
        + [pl.BlockSpec(memory_space=pltpu.VMEM)] * (len(args) - smem - whole)
        + [pl.BlockSpec(memory_space=pl.ANY)] * whole,
        cost_estimate=pl.CostEstimate(
            flops=us * 10**9, bytes_accessed=us * 3 * 10**6, transcendentals=0
        ),
        compiler_params=pltpu.CompilerParams(vmem_limit_bytes=mib * MIB),
        **kw,
    )(*args)


def swapped(one, two, axis):
    n = math.prod(lax.axis_size(name) for name in axis)
    near = [(i, i ^ 1) for i in range(n)]
    far = [(i, i - 1 if i % 2 == 0 else i + 1) for i in range(1, n - 1)]
    return lax.ppermute(one, axis, near), lax.ppermute(two, axis, far)


def body(
    forward_coeff,
    incident,
    cost_grad,
    tmat_real,
    tmat_imag,
    translation_real,
    translation_imaginary,
    neighbours,
    particle_type,
):
    n_short = lax.axis_size("x") * lax.axis_size("c")
    tile = lax.axis_index(TALL) * n_short + lax.axis_index(FLAT)
    tile = tile.astype(jnp.int32).reshape(1)
    kinds = particle_type.reshape(1, PT)
    (ids,) = call(
        functools.partial(target_ids_kernel, n_short), [(4 * PT, PT)], tile, smem=1, us=4
    )
    one, two = call(
        functools.partial(pack_wide_kernel, n_short),
        [(ROWS + HALF, PT)] * 2,
        tile,
        forward_coeff,
        cost_grad,
        neighbours,
        kinds,
        ids,
        smem=1,
        whole=1,
    )
    x1, x2 = swapped(one, two, TALL)
    one, two = call(
        functools.partial(pack_short_kernel, n_short),
        [(ROWS, PT)] * 2,
        tile,
        forward_coeff,
        cost_grad,
        neighbours,
        kinds,
        x1,
        x2,
        smem=1,
    )
    y1, y2 = swapped(one, two, FLAT)

    tw, lw, fw = call(
        weight_kernel,
        [(2 * W, KINDS * W), (2 * W, 2 * PART), (2 * W, 2 * PART)],
        tmat_real,
        tmat_imag,
        translation_real,
        translation_imaginary,
        mib=16,
        dtype=BF16,
    )

    own = call(
        first_kernel,
        [jax.ShapeDtypeStruct((2 * W, PT), BF16), (SLOTS * W, 2 * PT)],
        ids,
        cost_grad,
        neighbours,
        kinds,
        tw,
        mib=16,
        us=2,
    )
    scratch = [pltpu.VMEM((2 * PART, 2 * PT), BF16)] * 2
    early = call(
        functools.partial(early_kernel, n_short),
        [(W, 2 * PT), (SLOTS * HALF, 2 * PT)]
        + [jax.ShapeDtypeStruct((2 * PART, 2 * PT), BF16)],
        tile,
        ids,
        *own,
        neighbours,
        kinds,
        x1,
        x2,
        forward_coeff,
        tw,
        lw,
        smem=1,
        mib=24,
        us=4,
        scratch_shapes=scratch,
    )
    (vectors,) = call(
        functools.partial(main_kernel, n_short),
        [(3 * W + 8, PT)],
        tile,
        ids,
        cost_grad,
        neighbours,
        kinds,
        incident,
        x1,
        x2,
        y1,
        y2,
        *early,
        tw,
        lw,
        fw,
        smem=1,
        mib=24,
        us=4,
        scratch_shapes=scratch,
    )
    pair = [(0, 1), (1, 0)]
    partner = lax.ppermute(vectors, "c", pair)
    (chunks,) = call(outer_kernel, [(32 * CHUNK, PT)], tile, vectors, partner, smem=1)
    got = lax.all_to_all(chunks.reshape(4, 8 * CHUNK, PT), "x", 0, 0)
    (part,) = call(sum_kernel, [(8 * CHUNK, PT)], got)
    got = lax.all_to_all(part.reshape(8, CHUNK, PT), "z", 0, 0)
    (pieces,) = call(spread_kernel, [(8, CHUNK, PT)], got)
    got = lax.all_to_all(pieces, "y", 0, 0)
    mixed, coefs = call(combine_kernel, [(32 * BACK, PT), (8, PT)], got)
    got = lax.all_to_all(mixed.reshape(32, BACK, PT), ("z", "x"), 0, 0)
    half = got.reshape(32 * BACK, PT)
    other = lax.ppermute(half, "c", pair)
    own_half, adjoint = call(own_types_kernel, [(2, W, W), (W, PT)], half, vectors, coefs)
    (sensitivity,) = call(expand_kernel, [(KINDS, W, W)], tile, own_half, other, smem=1)
    return (adjoint, sensitivity)


def solution(mesh):
    fine = Mesh(mesh.devices.reshape(8, 8, 4, 2), TALL + FLAT)
    split_in = P(None, TALL + FLAT)
    placed = (split_in, split_in, split_in, P(), P(), P(), P(), split_in, P(TALL + FLAT))
    return jax.shard_map(
        body, mesh=fine, in_specs=placed, out_specs=(split_in, P()), check_vma=False
    )
```
